32 devices in a mesh: dp: 4 (over z), wide: 8 (over y, x, core).
Axes of the slice: x: 2, y: 2, z: 4, core: 2. Of those that a mesh axis runs over, the one named last changes fastest.
Arguments:
- big_act: bfloat16 [256, 96, 729], P('dp', 'wide'), may hold values from -6 to 6
- big_cls: bfloat16 [256, 96], P('dp', 'wide'), may hold values from -6 to 6
- small_act: bfloat16 [192, 96, 121], P('dp', 'wide'), may hold values from -6 to 6
- small_cls: bfloat16 [192, 96], P('dp', 'wide'), may hold values from -6 to 6
- big_order: int32 [4, 64], P('dp'), may hold values from 0 to 63, each once within a row
- small_order: int32 [4, 48], P('dp'), may hold values from 0 to 47, each once within a row
- big_cot: bfloat16 [256, 197, 192], P(('dp', 'wide')), may hold values from -6 to 6
- small_cot: bfloat16 [192, 37, 192], P(('dp', 'wide')), may hold values from -6 to 6
- vec_params: float32 [23, 192], replicated, may hold values from -1 to 1.3
- vec_moments: float32 [2, 23, 192], replicated, as said below
- head_weight: float32 [96, 192], P('wide', 'dp'), may hold values from -0.625 to 0.625
- qkv_weight: float32 [192, 576], P('wide', 'dp'), may hold values from -0.4375 to 0.4375
- proj_weight: float32 [192, 192], P('wide', 'dp'), may hold values from -1.75 to 1.75
- up_weight: float32 [192, 768], P('wide', 'dp'), may hold values from -0.4375 to 0.4375
- down_weight: float32 [768, 192], P('wide', 'dp'), may hold values from -0.21875 to 0.21875
- head_moments: float32 [2, 96, 192], P(None, 'wide', 'dp'), as said below
- qkv_moments: float32 [2, 192, 576], P(None, 'wide', 'dp'), as said below
- proj_moments: float32 [2, 192, 192], P(None, 'wide', 'dp'), as said below
- up_moments: float32 [2, 192, 768], P(None, 'wide', 'dp'), as said below
- down_moments: float32 [2, 768, 192], P(None, 'wide', 'dp'), as said below
- basis_input: float32 [96, 96], replicated, may hold values from -1 to 1, as said below
- basis_model: float32 [6, 192, 192], replicated, may hold values from -1 to 1, as said below
- basis_qkv: float32 [576, 576], replicated, may hold values from -1 to 1, as said below
- basis_hidden: float32 [2, 768, 768], replicated, may hold values from -1 to 1, as said below
- step: int32 [1], replicated, may hold values from 2 to 20
Outputs:
- big_out: float32 [256, 197, 192], P(('dp', 'wide'))
- small_out: float32 [192, 37, 192], P(('dp', 'wide'))
- big_act_grad: float32 [256, 96, 729], P('dp', 'wide')
- big_cls_grad: float32 [256, 96], P('dp', 'wide')
- small_act_grad: float32 [192, 96, 121], P('dp', 'wide')
- small_cls_grad: float32 [192, 96], P('dp', 'wide')
- grad_norm: float32 [1], replicated
- new_vec_params: float32 [23, 192], replicated
- new_vec_moments: float32 [2, 23, 192], replicated
- new_head_weight: float32 [96, 192], P('wide', 'dp')
- new_qkv_weight: float32 [192, 576], P('wide', 'dp')
- new_proj_weight: float32 [192, 192], P('wide', 'dp')
- new_up_weight: float32 [192, 768], P('wide', 'dp')
- new_down_weight: float32 [768, 192], P('wide', 'dp')
- new_head_moments: float32 [2, 96, 192], P(None, 'wide', 'dp')
- new_qkv_moments: float32 [2, 192, 576], P(None, 'wide', 'dp')
- new_proj_moments: float32 [2, 192, 192], P(None, 'wide', 'dp')
- new_up_moments: float32 [2, 192, 768], P(None, 'wide', 'dp')
- new_down_moments: float32 [2, 768, 192], P(None, 'wide', 'dp')
- head_copy: bfloat16 [96, 192], P('wide', 'dp')
- qkv_copy: bfloat16 [192, 576], P('wide', 'dp')
- proj_copy: bfloat16 [192, 192], P('wide', 'dp')
- up_copy: bfloat16 [192, 768], P('wide', 'dp')
- down_copy: bfloat16 [768, 192], P('wide', 'dp')
The draws below stay inside these ranges and needn't reach their ends.
Inputs may be any that keep to these rules, and one draw needn't show every extreme that they name: `big_order`: each row lists every slot index once. `small_order`: each row lists every slot index once. `vec_moments`: the roots of the second moments (index 1) are positive. `head_moments`: the roots of the second moments (index 1) are positive. `qkv_moments`: the roots of the second moments (index 1) are positive. `proj_moments`: the roots of the second moments (index 1) are positive. `up_moments`: the roots of the second moments (index 1) are positive. `down_moments`: the roots of the second moments (index 1) are positive. `basis_input`: orthogonal. `basis_model`: each member is orthogonal. `basis_qkv`: orthogonal. `basis_hidden`: each member is orthogonal.
All inputs are finite; a program needn't handle non-finite values.
Results may differ from the reference program's by a relative error of at most 0.01.
The reference program's roundings to bfloat16 on the way count: a program that leaves them out, or rounds other values in their place, can miss the bound.
Values may be sent and summed in bfloat16 or wider, within the bound.
A program may use at most 192 MiB of HBM per device.

```python
import jax
import jax.numpy as jnp
from jax import lax

D = 192
C1 = 96
FF = 768
HEADS = 4
HD = 48
GB = 27
GS = 11
PB = 14
PS = 6
TB = 197
TS = 37
BIG_DEV = 8
SMALL_DEV = 6
BIG_ROW = 64
SMALL_ROW = 48
BIG = 256
SMALL = 192
VROWS = 23
N_DP = 4
N_WIDE = 8


def grad_scale():
    return (C1 * D + 4 * D * D + 2 * D * FF + VROWS * D) ** (-0.5)


def state_pair(key, rows_n, cols_n):
    first_key, second_key = jax.random.split(key, 2)
    spread = grad_scale()
    first_moment = jnp.clip(jax.random.normal(first_key, (rows_n, cols_n), jnp.float32), -4.0, 4.0) * (0.111 * spread)
    ratios = jnp.exp(jax.random.uniform(second_key, (rows_n, cols_n), jnp.float32, jnp.log(0.5), jnp.log(8.0)))
    second_root = jnp.sqrt(ratios * 0.001) * spread
    return jnp.stack([first_moment, second_root])


def orthogonal(key, matrix_n):
    row_key, col_key, sign_key, flip_key = jax.random.split(key, 4)
    row_perm = jax.random.permutation(row_key, matrix_n)
    col_perm = jax.random.permutation(col_key, matrix_n)
    row_sign = (2 * jax.random.randint(sign_key, (matrix_n,), 0, 2) - 1).astype(jnp.float32)
    col_sign = (2 * jax.random.randint(flip_key, (matrix_n,), 0, 2) - 1).astype(jnp.float32)
    phases = (2 * col_perm[None, :] + 1) * row_perm[:, None] % (4 * matrix_n)
    cosines = jnp.cos(jnp.pi * phases.astype(jnp.float32) / (2.0 * matrix_n))
    row_weight = jnp.where(row_perm == 0, (1.0 / matrix_n) ** 0.5, (2.0 / matrix_n) ** 0.5)
    return cosines * row_weight[:, None] * row_sign[:, None] * col_sign[None, :]


def draw_vec_params(key, part):
    row_ids = jnp.arange(VROWS)[:, None]
    noises = jnp.clip(jax.random.normal(key, (VROWS, D), jnp.float32), -3.0, 3.0)
    gain_rows = (row_ids == 11) | (row_ids == 16)
    spread = jnp.where(row_ids < 9, 1.0 / 3.0, jnp.where(gain_rows, 0.1, 0.3))
    return noises * spread + jnp.where(gain_rows, 1.0, 0.0)


def draw_vec_moments(key, part):
    return state_pair(key, VROWS, D)


def draw_head_moments(key, part):
    return state_pair(key, C1, D)


def draw_qkv_moments(key, part):
    return state_pair(key, D, 3 * D)


def draw_proj_moments(key, part):
    return state_pair(key, D, D)


def draw_up_moments(key, part):
    return state_pair(key, D, FF)


def draw_down_moments(key, part):
    return state_pair(key, FF, D)


def draw_basis_input(key, part):
    return orthogonal(key, C1)


def draw_basis_model(key, part):
    return jnp.stack([orthogonal(jax.random.fold_in(key, member), D) for member in range(6)])


def draw_basis_qkv(key, part):
    return orthogonal(key, 3 * D)


def draw_basis_hidden(key, part):
    return jnp.stack([orthogonal(jax.random.fold_in(key, member), FF) for member in range(2)])


def shard_levels(own_key, dims, cuts, least, largest):
    def one(axis_at, blocks):
        draws = jax.random.uniform(jax.random.fold_in(jax.random.fold_in(own_key, 6), axis_at), (blocks,), jnp.float32, least / len(cuts), largest / len(cuts))
        return jnp.repeat(jnp.exp(draws), dims[axis_at] // blocks).reshape((-1,) + (1,) * (len(dims) - axis_at - 1))

    level = one(*cuts[0])
    for cut in cuts[1:]:
        level = level * one(*cut)
    return level


def scatter_about(rng, dims, width, most, shards=(), kind=jnp.bfloat16):
    values = width * jax.random.normal(rng, dims, jnp.float32)
    if shards:
        values = values * shard_levels(rng, dims, shards, -0.22, 0.18)
    return jnp.clip(values, -most, most).astype(kind)


def setup_inputs(seed: int = 0) -> dict:
    arg_keys = jax.random.split(jax.random.key(seed), 26)
    big_act = scatter_about(arg_keys[0], (BIG, C1, GB * GB), 1.0, 6.0, ((0, 4), (1, 8)))
    big_cls = scatter_about(arg_keys[1], (BIG, C1), 1.0, 6.0, ((0, 4), (1, 8)))
    small_act = scatter_about(arg_keys[2], (SMALL, C1, GS * GS), 1.0, 6.0, ((0, 4), (1, 8)))
    small_cls = scatter_about(arg_keys[3], (SMALL, C1), 1.0, 6.0, ((0, 4), (1, 8)))
    big_order = jax.vmap(lambda own: jax.random.permutation(own, BIG_ROW))(jax.random.split(arg_keys[4], N_DP)).reshape((N_DP, BIG_ROW)).astype(jnp.int32)
    small_order = jax.vmap(lambda own: jax.random.permutation(own, SMALL_ROW))(jax.random.split(arg_keys[5], N_DP)).reshape((N_DP, SMALL_ROW)).astype(jnp.int32)
    big_cot = scatter_about(arg_keys[6], (BIG, TB, D), 1.0, 6.0, ((0, 32),))
    small_cot = scatter_about(arg_keys[7], (SMALL, TS, D), 1.0, 6.0, ((0, 32),))
    vec_params = draw_vec_params(jax.random.fold_in(arg_keys[25], 71), 0)
    vec_moments = draw_vec_moments(jax.random.fold_in(arg_keys[25], 71), 0)
    head_weight = scatter_about(arg_keys[10], (C1, D), C1 ** -0.5, 0.625, ((0, 8), (1, 4)), jnp.float32)
    qkv_weight = scatter_about(arg_keys[11], (D, 3 * D), D ** -0.5, 0.4375, ((0, 8), (1, 4)), jnp.float32)
    proj_weight = scatter_about(arg_keys[12], (D, D), (D // 16) ** -0.5, 1.75, ((0, 8), (1, 4)), jnp.float32)
    up_weight = scatter_about(arg_keys[13], (D, FF), D ** -0.5, 0.4375, ((0, 8), (1, 4)), jnp.float32)
    down_weight = scatter_about(arg_keys[14], (FF, D), FF ** -0.5, 0.21875, ((0, 8), (1, 4)), jnp.float32)
    head_moments = draw_head_moments(jax.random.fold_in(arg_keys[25], 71), 0)
    qkv_moments = draw_qkv_moments(jax.random.fold_in(arg_keys[25], 71), 0)
    proj_moments = draw_proj_moments(jax.random.fold_in(arg_keys[25], 71), 0)
    up_moments = draw_up_moments(jax.random.fold_in(arg_keys[25], 71), 0)
    down_moments = draw_down_moments(jax.random.fold_in(arg_keys[25], 71), 0)
    basis_input = draw_basis_input(jax.random.fold_in(arg_keys[25], 71), 0)
    basis_model = draw_basis_model(jax.random.fold_in(arg_keys[25], 71), 0)
    basis_qkv = draw_basis_qkv(jax.random.fold_in(arg_keys[25], 71), 0)
    basis_hidden = draw_basis_hidden(jax.random.fold_in(arg_keys[25], 71), 0)
    step = jax.random.randint(arg_keys[24], (1,), 2, 21).astype(jnp.int32)
    return {"big_act": big_act, "big_cls": big_cls, "small_act": small_act, "small_cls": small_cls, "big_order": big_order, "small_order": small_order, "big_cot": big_cot, "small_cot": small_cot, "vec_params": vec_params, "vec_moments": vec_moments, "head_weight": head_weight, "qkv_weight": qkv_weight, "proj_weight": proj_weight, "up_weight": up_weight, "down_weight": down_weight, "head_moments": head_moments, "qkv_moments": qkv_moments, "proj_moments": proj_moments, "up_moments": up_moments, "down_moments": down_moments, "basis_input": basis_input, "basis_model": basis_model, "basis_qkv": basis_qkv, "basis_hidden": basis_hidden, "step": step}


beta_one = 0.9
beta_two = 0.999
adam_eps = 1e-08
norm_eps = 1e-06
rate_matrix = 0.08
rate_vector = 0.25
decay_rate = 0.05
clip_limit = 1.0

@jax.custom_vjp
def low(v):
    return lax.optimization_barrier(v.astype(jnp.bfloat16)).astype(jnp.float32)

@jax.custom_vjp
def low_back(v):
    return v

def low_keep(v):
    return (low(v), None)

def low_pass(kept, grad):
    return (grad,)

def back_keep(v):
    return (v, None)

def back_low(kept, grad):
    return (low(grad),)
low.defvjp(low_keep, low_pass)
low_back.defvjp(back_keep, back_low)

def exact_dot(left_side, right_side):
    return jnp.dot(left_side, right_side, precision=lax.Precision.HIGHEST, preferred_element_type=jnp.float32)

def layer_norm(values, scaling, offset):
    average = lax.optimization_barrier(jnp.mean(values, -1, keepdims=True))
    centered = values - average
    variance = lax.optimization_barrier(jnp.mean(centered * centered, -1, keepdims=True))
    return centered * lax.rsqrt(variance + norm_eps) * scaling + offset

def pool_grid(images, conv_taps, shifts, grid_size, pool_size):
    img_count, channels = (images.shape[0], images.shape[1])
    spatial = jnp.repeat(images.reshape(img_count, channels, grid_size, grid_size), 2, axis=1)
    padded = jnp.pad(spatial, ((0, 0), (0, 0), (1, 1), (1, 1)))
    totals = jnp.zeros((img_count, 2 * channels, pool_size, pool_size), jnp.float32) + shifts[None, :, None, None]
    for tap_row in range(3):
        for tap_col in range(3):
            window = padded[:, :, tap_row:tap_row + 2 * pool_size - 1:2, tap_col:tap_col + 2 * pool_size - 1:2]
            totals = totals + conv_taps[tap_row * 3 + tap_col][None, :, None, None] * window
    return jnp.transpose(totals.reshape(img_count, 2 * channels, pool_size * pool_size), (0, 2, 1))

def attention(packed, length):
    img_count = packed.shape[0] // length
    pieces = packed.reshape(img_count, length, 3, HEADS, HD)
    queries, keys_in, values = (pieces[:, :, 0], pieces[:, :, 1], pieces[:, :, 2])
    scores = low_back(jnp.einsum('nqhd,nkhd->nhqk', queries, keys_in, precision=lax.Precision.HIGHEST) * HD ** (-0.5))
    probas = low(jax.nn.softmax(scores, axis=-1))
    mixture = jnp.einsum('nhqk,nkhd->nqhd', probas, values, precision=lax.Precision.HIGHEST)
    return mixture.reshape(img_count * length, D)

def layer_step(weights, vecs, big_tokens, small_tokens):
    qkv_full, proj_full, up_full, down_full = weights
    split_at = big_tokens.shape[0] * TB
    rows_in = jnp.concatenate([big_tokens.reshape(-1, D), small_tokens.reshape(-1, D)], 0)
    normed = low(layer_norm(rows_in, vecs[11], vecs[12]))
    bias_qkv = jnp.concatenate([vecs[13], jnp.zeros((D,), jnp.float32), vecs[14]])
    packed = low(low_back(exact_dot(normed, qkv_full) + bias_qkv))
    mixture = jnp.concatenate([attention(packed[:split_at], TB), attention(packed[split_at:], TS)], 0)
    mixture = low(low_back(mixture))
    middle = rows_in + low_back(exact_dot(mixture, proj_full) + vecs[15])
    normed_two = low(layer_norm(middle, vecs[16], vecs[17]))
    hidden = low_back(exact_dot(normed_two, up_full) + vecs[19:].reshape(FF))
    active = low(jax.nn.gelu(hidden, approximate=False))
    result = middle + low_back(exact_dot(active, down_full) + vecs[18])
    return (result[:split_at].reshape(big_tokens.shape), result[split_at:].reshape(small_tokens.shape))

def forward(big_act, big_cls, small_act, small_cls, vecs, head_weight, qkv_weight, proj_weight, up_weight, down_weight, big_slots, small_slots):
    weights = (low(qkv_weight), low(proj_weight), low(up_weight), low(down_weight))
    head_full = low(head_weight)
    groups = N_DP * N_WIDE
    big_a = big_act[big_slots].reshape(groups, BIG_DEV, C1, GB * GB)
    big_c = big_cls[big_slots].reshape(groups, BIG_DEV, C1)
    small_a = small_act[small_slots].reshape(groups, SMALL_DEV, C1, GS * GS)
    small_c = small_cls[small_slots].reshape(groups, SMALL_DEV, C1)

    def crop_tokens(images, classes, grid_size, pool_size):
        pooled = low(low_back(pool_grid(images, vecs[0:9], vecs[9], grid_size, pool_size)))
        head = low_back(exact_dot(low_back(classes), head_full) + vecs[10])
        return jnp.concatenate([head[:, None, :], pooled], 1)

    def group_step(pieces):
        act_big, cls_big, act_small, cls_small = pieces
        return layer_step(weights, vecs, crop_tokens(act_big, cls_big, GB, PB), crop_tokens(act_small, cls_small, GS, PS))
    big_out, small_out = lax.map(jax.checkpoint(group_step), (big_a, big_c, small_a, small_c))
    return (big_out.reshape(BIG, TB, D), small_out.reshape(SMALL, TS, D))

def soap_step(master, moments, gradient, left_basis, right_basis, step_count):
    turned = exact_dot(exact_dot(left_basis.T, gradient), right_basis)
    first_moment = beta_one * moments[0] + (1.0 - beta_one) * turned
    second_moment = beta_two * moments[1] * moments[1] + (1.0 - beta_two) * turned * turned
    direction = first_moment / (1.0 - beta_one ** step_count) / (jnp.sqrt(second_moment / (1.0 - beta_two ** step_count)) + adam_eps)
    update = exact_dot(exact_dot(left_basis, direction), right_basis.T)
    return (master - rate_matrix * update, jnp.stack([first_moment, jnp.sqrt(second_moment)]))

def reference(big_act, big_cls, small_act, small_cls, big_order, small_order, big_cot, small_cot, vec_params, vec_moments, head_weight, qkv_weight, proj_weight, up_weight, down_weight, head_moments, qkv_moments, proj_moments, up_moments, down_moments, basis_input, basis_model, basis_qkv, basis_hidden, step):
    big_slots = (big_order + jnp.arange(N_DP, dtype=jnp.int32)[:, None] * BIG_ROW).reshape(-1).astype(jnp.int32)
    small_slots = (small_order + jnp.arange(N_DP, dtype=jnp.int32)[:, None] * SMALL_ROW).reshape(-1).astype(jnp.int32)

    def bound(act_big, cls_big, act_small, cls_small, vecs, head_w, qkv_w, proj_w, up_w, down_w):
        return forward(act_big, cls_big, act_small, cls_small, vecs, head_w, qkv_w, proj_w, up_w, down_w, big_slots, small_slots)
    outputs, pullback = jax.vjp(bound, big_act.astype(jnp.float32), big_cls.astype(jnp.float32), small_act.astype(jnp.float32), small_cls.astype(jnp.float32), vec_params, head_weight, qkv_weight, proj_weight, up_weight, down_weight)
    grads = pullback((big_cot.astype(jnp.float32), small_cot.astype(jnp.float32)))
    mat_grads = grads[5:10]
    vec_grad = grads[4]
    square = jnp.sum(vec_grad * vec_grad)
    for gradient in mat_grads:
        square = square + jnp.sum(gradient * gradient)
    grad_norm = jnp.sqrt(square)
    factor = jnp.minimum(1.0, clip_limit / (grad_norm + 1e-06))
    step_count = step[0].astype(jnp.float32)
    masters = (head_weight, qkv_weight, proj_weight, up_weight, down_weight)
    states = (head_moments, qkv_moments, proj_moments, up_moments, down_moments)
    basis_pairs = ((basis_input, basis_model[0]), (basis_model[1], basis_qkv), (basis_model[2], basis_model[3]), (basis_model[4], basis_hidden[0]), (basis_hidden[1], basis_model[5]))
    new_masters = []
    new_states = []
    for member in range(5):
        fresh, moments = soap_step(masters[member], states[member], mat_grads[member] * factor, basis_pairs[member][0], basis_pairs[member][1], step_count)
        new_masters.append(fresh)
        new_states.append(moments)
    vec_scaled = vec_grad * factor
    first_moment = beta_one * vec_moments[0] + (1.0 - beta_one) * vec_scaled
    second_moment = beta_two * vec_moments[1] * vec_moments[1] + (1.0 - beta_two) * vec_scaled * vec_scaled
    direction = first_moment / (1.0 - beta_one ** step_count) / (jnp.sqrt(second_moment / (1.0 - beta_two ** step_count)) + adam_eps)
    new_vec = vec_params * (1.0 - rate_vector * decay_rate) - rate_vector * direction
    return (outputs[0], outputs[1], grads[0], grads[1], grads[2], grads[3], grad_norm.reshape(1), new_vec, jnp.stack([first_moment, jnp.sqrt(second_moment)]), new_masters[0], new_masters[1], new_masters[2], new_masters[3], new_masters[4], new_states[0], new_states[1], new_states[2], new_states[3], new_states[4], new_masters[0].astype(jnp.bfloat16), new_masters[1].astype(jnp.bfloat16), new_masters[2].astype(jnp.bfloat16), new_masters[3].astype(jnp.bfloat16), new_masters[4].astype(jnp.bfloat16))
```

```python
from functools import partial

import jax
import jax.numpy as jnp
import numpy as np
from jax import lax
from jax.experimental import pallas as pl
from jax.experimental.pallas import tpu as pltpu
from jax.sharding import PartitionSpec as P

HEADS = 4
HD = 48
beta_one = 0.9
beta_two = 0.999
adam_eps = 1e-08
norm_eps = 1e-06
rate_matrix = 0.08
rate_vector = 0.25
decay_rate = 0.05
clip_limit = 1.0
LANES = 256
SPLIT = 208


def nt(a, b):
    return lax.dot_general(a, b, (((1,), (1,)), ((), ())), preferred_element_type=jnp.float32)


def tn(a, b):
    return lax.dot_general(a, b, (((0,), (0,)), ((), ())), preferred_element_type=jnp.float32)


def nn(a, b):
    return jnp.dot(a, b, preferred_element_type=jnp.float32)


def colsum(v):
    return jnp.sum(v, 0, keepdims=True)


def norm_forward(rows, gain, shift):
    centered = rows - jnp.mean(rows, -1, keepdims=True)
    scale = lax.rsqrt(jnp.mean(centered * centered, -1, keepdims=True) + norm_eps)
    hat = centered * scale
    return hat, scale, (hat * gain + shift).astype(jnp.bfloat16)


def norm_backward(grad, hat, scale, gain):
    inner = grad * gain
    mean_a = jnp.mean(inner, -1, keepdims=True)
    mean_b = jnp.mean(inner * hat, -1, keepdims=True)
    return scale * (inner - mean_a - hat * mean_b)


def block_kernel(
    counts,
    tok,
    bcot,
    scot,
    vec,
    ubias,
    wh,
    wqkv,
    wp,
    wu,
    wd,
    bout,
    sout,
    gtok,
    gh,
    gqkv,
    gp,
    gu,
    gdt,
    gvec,
    gub,
    probs,
    bias,
    cot,
):
    big_n, small_n, big_len, small_len = counts
    step = pl.program_id(0)
    width = vec.shape[1]
    row_id = lax.broadcasted_iota(jnp.int32, (LANES, 1), 0)
    lane_id = lax.broadcasted_iota(jnp.int32, (1, width), 1)

    @pl.when(step == 0)
    def _():
        for ref in (gh, gqkv, gp, gu, gdt, gvec, gub):
            ref[...] = jnp.zeros_like(ref)
        cot[...] = jnp.zeros_like(cot)
        key_id = lax.broadcasted_iota(jnp.int32, (LANES, LANES), 1)
        query_id = lax.broadcasted_iota(jnp.int32, (LANES, LANES), 0)
        keep_big = (query_id < SPLIT) & (key_id < big_len)
        keep_small = (query_id >= SPLIT) & (key_id >= SPLIT) & (key_id < SPLIT + small_len)
        bias[...] = jnp.where(keep_big | keep_small, 0.0, -1e30)

    raw = jnp.transpose(tok[0].astype(jnp.float32))
    raw_low = raw.astype(jnp.bfloat16)
    is_head = (row_id == 0) | (row_id == SPLIT)
    rows = jnp.where(is_head, nn(raw_low, wh[...]) + vec[10:11], raw)
    hat_one, scale_one, normed_one = norm_forward(rows, vec[11:12], vec[12:13])
    queries = (nn(normed_one, wqkv[0]) + vec[13:14]).astype(jnp.bfloat16)
    keys_in = nn(normed_one, wqkv[1]).astype(jnp.bfloat16)
    values = (nn(normed_one, wqkv[2]) + vec[14:15]).astype(jnp.bfloat16)
    zero = jnp.zeros((), jnp.bfloat16)
    in_head = [(lane_id >= h * HD) & (lane_id < (h + 1) * HD) for h in range(HEADS)]
    mixture = jnp.zeros((LANES, width), jnp.float32)
    for h in range(HEADS):
        scores = nt(jnp.where(in_head[h], queries, zero), keys_in) * HD ** (-0.5) + bias[...]
        weights = jnp.exp(scores - jnp.max(scores, -1, keepdims=True))
        probas = weights * (1.0 / jnp.sum(weights, -1, keepdims=True))
        probs[h] = probas
        mixture += nn(probas.astype(jnp.bfloat16), jnp.where(in_head[h], values, zero))
    mixture = mixture.astype(jnp.bfloat16)
    middle = rows + nn(mixture, wp[...]) + vec[15:16]
    hat_two, scale_two, normed_two = norm_forward(middle, vec[16:17], vec[17:18])
    pre = nn(normed_two, wu[...]) + ubias[...]
    cdf = 0.5 + 0.5 * lax.erf(pre * 0.7071067811865476)
    slope = cdf + pre * jnp.exp(pre * pre * -0.5) * 0.3989422804014327
    active = (pre * cdf).astype(jnp.bfloat16)
    result = middle + nn(active, wd[...]) + vec[18:19]
    bout[0] = result[:big_len]
    cot[:big_len] = bcot[0]

    @pl.when(step < small_n)
    def _():
        sout[0] = result[SPLIT : SPLIT + small_len]
        cot[SPLIT : SPLIT + small_len] = scot[0]

    @pl.when(step == small_n)
    def _():
        cot[SPLIT:] = jnp.zeros((LANES - SPLIT, width), jnp.bfloat16)

    cot_low = cot[...]
    cot_rows = cot_low.astype(jnp.float32)
    gdt[...] += tn(cot_low, active)
    gvec[8:9] += colsum(cot_rows)
    grad_pre = (nt(cot_low, wd[...]) * slope).astype(jnp.bfloat16)
    gu[...] += tn(normed_two, grad_pre)
    gub[...] += colsum(grad_pre.astype(jnp.float32))
    grad_two = nt(grad_pre, wu[...])
    gvec[6:7] += colsum(grad_two * hat_two)
    gvec[7:8] += colsum(grad_two)
    grad_mid = norm_backward(grad_two, hat_two, scale_two, vec[16:17]) + cot_rows
    branch = grad_mid.astype(jnp.bfloat16)
    gp[...] += tn(mixture, branch)
    gvec[5:6] += colsum(branch.astype(jnp.float32))
    grad_mix = nt(branch, wp[...]).astype(jnp.bfloat16)
    grad_q = jnp.zeros((LANES, width), jnp.float32)
    grad_k = jnp.zeros((LANES, width), jnp.float32)
    grad_v = jnp.zeros((LANES, width), jnp.float32)
    for h in range(HEADS):
        probas = probs[h]
        own = jnp.where(in_head[h], grad_mix, zero)
        grad_probs = nt(own, values)
        inner = jnp.sum(probas * grad_probs, -1, keepdims=True)
        grad_scores = (probas * (grad_probs - inner)).astype(jnp.bfloat16)
        grad_q += nn(grad_scores, jnp.where(in_head[h], keys_in, zero))
        grad_k += tn(grad_scores, jnp.where(in_head[h], queries, zero))
        grad_v += tn(probas.astype(jnp.bfloat16), own)
    grad_q = (grad_q * HD ** (-0.5)).astype(jnp.bfloat16)
    grad_k = (grad_k * HD ** (-0.5)).astype(jnp.bfloat16)
    grad_v = grad_v.astype(jnp.bfloat16)
    gqkv[0] += tn(normed_one, grad_q)
    gqkv[1] += tn(normed_one, grad_k)
    gqkv[2] += tn(normed_one, grad_v)
    gvec[3:4] += colsum(grad_q.astype(jnp.float32))
    gvec[4:5] += colsum(grad_v.astype(jnp.float32))
    grad_one = nt(grad_q, wqkv[0]) + nt(grad_k, wqkv[1]) + nt(grad_v, wqkv[2])
    gvec[1:2] += colsum(grad_one * hat_one)
    gvec[2:3] += colsum(grad_one)
    grad_tok = norm_backward(grad_one, hat_one, scale_one, vec[11:12]) + grad_mid
    grad_head = jnp.where(is_head, grad_tok, 0.0).astype(jnp.bfloat16)
    gh[...] += tn(raw_low, grad_head)
    gvec[0:1] += colsum(grad_head.astype(jnp.float32))
    gtok[0] = jnp.transpose(jnp.where(is_head, nt(grad_head, wh[...]), grad_tok)).astype(jnp.bfloat16)


def whole(shape):
    return pl.BlockSpec(shape, lambda i: (0,) * len(shape))


def run_block(tok, big_cot, small_cot, vec, ubias, wh, wqkv, wp, wu, wd):
    big_n, big_len, width = big_cot.shape
    small_n, small_len = small_cot.shape[:2]
    f32 = jnp.float32
    hidden = wu.shape[1]
    outs = [
        ((big_n, big_len, width), f32),
        ((small_n, small_len, width), f32),
        (tok.shape, jnp.bfloat16),
        ((width, width), f32),
        ((3, width, width), f32),
        ((width, width), f32),
        ((width, hidden), f32),
        ((width, hidden), f32),
        ((16, width), f32),
        ((1, hidden), f32),
    ]
    one_big = pl.BlockSpec((1, big_len, width), lambda i: (i, 0, 0))
    one_small = pl.BlockSpec((1, small_len, width), lambda i: (jnp.minimum(i, small_n - 1), 0, 0))
    one_tok = pl.BlockSpec((1, width, LANES), lambda i: (i, 0, 0))
    return pl.pallas_call(
        partial(block_kernel, (big_n, small_n, big_len, small_len)),
        grid=(big_n,),
        in_specs=[one_tok, one_big, one_small]
        + [whole(a.shape) for a in (vec, ubias, wh, wqkv, wp, wu, wd)],
        out_specs=[one_big, one_small, one_tok] + [whole(s) for s, _ in outs[3:]],
        out_shape=[jax.ShapeDtypeStruct(s, d) for s, d in outs],
        scratch_shapes=[
            pltpu.VMEM((HEADS, LANES, LANES), f32),
            pltpu.VMEM((LANES, LANES), f32),
            pltpu.VMEM((LANES, width), jnp.bfloat16),
        ],
        compiler_params=pltpu.CompilerParams(vmem_limit_bytes=56 * 1024 * 1024),
        name="block",
    )(tok, big_cot, small_cot, vec, ubias, wh, wqkv, wp, wu, wd)


def row_permutation(channels, images):
    width = 192
    group = width // (2 * channels * images)
    table = np.zeros((width, width), np.float32)
    for s in range(group):
        for e in range(2):
            for c in range(channels):
                for i in range(images):
                    row = ((s * 2 + e) * channels + c) * images + i
                    table[row, i * (width // images) + s * 2 * channels + 2 * c + e] = 1.0
    return jnp.asarray(table, jnp.bfloat16)
MESH = pl.DeviceIdType.MESH
CELLS_PAD = 896
WIDTH = 192


def up_to(value, unit):
    return -(-value // unit) * unit


def spread(axis, count, me, src_of, dst, send, recv):
    copies = []
    for k in range(1, count):
        peer = lax.rem(me + k, count)
        copy = pltpu.make_async_remote_copy(
            src_ref=src_of(peer),
            dst_ref=dst,
            send_sem=send.at[k - 1],
            recv_sem=recv.at[k - 1],
            device_id={axis: peer},
            device_id_type=MESH,
        )
        copy.start()
        copies.append(copy)
    return copies


def arrived(copies):
    for copy in copies:
        copy.wait_recv()


def sent(copies):
    for copy in copies:
        copy.wait_send()


def greet(axes):
    barrier = pltpu.get_barrier_semaphore()
    total = 0
    for axis, count, me in axes:
        for k in range(1, count):
            pl.semaphore_signal(
                barrier,
                inc=1,
                device_id={axis: lax.rem(me + k, count)},
                device_id_type=MESH,
            )
        total += count - 1
    pl.semaphore_wait(barrier, total)


class Sizes:
    def __init__(self, wide, dp, channels, images, small_images):
        self.wide, self.dp = wide, dp
        self.channels, self.images, self.small_images = channels, images, small_images
        self.slots = wide * images
        self.rows = channels * self.slots
        self.piece_rows = 2 * channels * images
        self.br = WIDTH // wide
        self.bh = self.br // 2
        self.bc = WIDTH // dp
        self.pair_rows = up_to(2 * self.br, 16)
        self.block_lanes = up_to(7 * self.bc, 128)
        self.head_rows = up_to(self.bh, 16)

    def block_places(self):
        br, bh, bc = self.br, self.bh, self.bc
        return (
            [(0, 6 * bc, bh, bc)],
            [(br, 0, br, 3 * bc)],
            [(br, 3 * bc, br, bc)],
            [(0, 0, br, 4 * bc)],
            [(0, 4 * bc, br, bc), (0, 5 * bc, br, bc), (br, 4 * bc, br, bc), (br, 5 * bc, br, bc)],
        )

    def pack_blocks(self, ref, blocks):
        for block, places in zip(blocks, self.block_places()):
            at = 0
            for row, lane, rows, lanes in places:
                ref[row : row + rows, lane : lane + lanes] = block[at : at + rows]
                at += rows

    def unpack_blocks(self, packed):
        result = []
        for places in self.block_places():
            parts = [packed[r : r + n, q : q + m] for r, q, n, m in places]
            result.append(parts[0] if len(parts) == 1 else jnp.concatenate(parts, 0))
        return result


def local_columns(vec, me, sizes, member):
    channel = lax.broadcasted_iota(jnp.int32, (sizes.rows, WIDTH), 0) // sizes.slots
    lane = lax.broadcasted_iota(jnp.int32, (sizes.rows, WIDTH), 1)
    pick = (lane == 2 * (me * sizes.channels + channel) + member).astype(jnp.float32)
    return lax.dot_general(
        pick,
        vec[0:16],
        (((1,), (1,)), ((), ())),
        precision=lax.Precision.HIGHEST,
        preferred_element_type=jnp.float32,
    )


def front_kernel(
    sizes,
    lens,
    cells,
    heads,
    vec,
    table,
    perm,
    mh,
    mqkv,
    mp,
    mu,
    md,
    tok,
    wins,
    wh,
    wqkv,
    wp,
    wu,
    wd,
    stage_one,
    stage_two,
    stage_head,
    got_one,
    got_two,
    got_head,
    pooled,
    received,
    totals,
    one_send,
    one_recv,
    two_send,
    two_recv,
    head_send,
    head_recv,
    act_send,
    act_recv,
):
    bf16 = jnp.bfloat16
    me_w, me_d = lax.axis_index("wide"), lax.axis_index("dp")
    n_w, n_d = sizes.wide, sizes.dp
    br, bh, bc = sizes.br, sizes.bh, sizes.bc
    greet((("wide", n_w, me_w), ("dp", n_d, me_d)))
    stage_one[...] = jnp.zeros_like(stage_one)
    sizes.pack_blocks(stage_one, (mh[...], mqkv[...], mp[...], mu[...], md[...]))
    got_one[me_d] = stage_one[...].astype(bf16)
    one = spread("dp", n_d, me_d, lambda peer: got_one.at[me_d], got_one.at[me_d], one_send, one_recv)

    taps = [local_columns(vec, me_w, sizes, e) for e in range(2)]

    def pool(tap):
        win = nt(cells[...], table[tap * LANES : (tap + 1) * LANES, :])
        wins[tap] = win.astype(bf16)
        for e in range(2):
            part = taps[e][:, tap : tap + 1] * win
            if tap == 0:
                totals[e] = part
            else:
                totals[e] += part

    for tap in range(4):
        pool(tap)
    arrived(one)
    stage_two[...] = jnp.zeros_like(stage_two)
    stage_head[...] = jnp.zeros_like(stage_head)
    for d in range(n_d):
        head, qkv, proj, up, down = sizes.unpack_blocks(got_one[d].astype(jnp.float32))
        stage_head[0:bh, d * bc : (d + 1) * bc] = head
        stage_two[0:br, d * 4 * bc : (d + 1) * 4 * bc] = up
        for part in range(3):
            low, high = d * 3 * bc, (d + 1) * 3 * bc
            a, b = max(low, part * WIDTH), min(high, (part + 1) * WIDTH)
            if a < b:
                row = 0 if part < 2 else br
                base = (4 + part) * WIDTH if part < 2 else 0
                stage_two[row : row + br, base + a - part * WIDTH : base + b - part * WIDTH] = qkv[
                    :, a - low : b - low
                ]
        stage_two[br : 2 * br, WIDTH + d * bc : WIDTH + (d + 1) * bc] = proj
        for j in range(4):
            at = (2 + j) * WIDTH + d * bc
            stage_two[br : 2 * br, at : at + bc] = down[j * br : (j + 1) * br]
    got_two[me_w] = stage_two[...].astype(bf16)
    got_head[me_w] = stage_head[...].astype(bf16)
    two = spread("wide", n_w, me_w, lambda peer: got_two.at[me_w], got_two.at[me_w], two_send, two_recv)
    two += spread(
        "wide", n_w, me_w, lambda peer: got_head.at[me_w], got_head.at[me_w], head_send, head_recv
    )
    for tap in range(4, 9):
        pool(tap)

    big_len, small_len = lens
    lane = lax.broadcasted_iota(jnp.int32, (1, LANES), 1)
    token = ((lane >= 1) & (lane < big_len)) | ((lane > SPLIT) & (lane < SPLIT + small_len))
    for e in range(2):
        rest = jnp.zeros((), jnp.float32)
        if e == 0:
            rest = jnp.where(
                lane == 0, heads[:, 0:1], jnp.where(lane == SPLIT, heads[:, 1:2], 0.0)
            )
        full = jnp.where(token, totals[e] + taps[e][:, 9:10], rest)
        for c in range(sizes.channels):
            for w in range(n_w):
                at = (c * n_w + w) * sizes.images
                to = (e * sizes.channels + c) * sizes.images
                pooled[w, to : to + sizes.images] = full[at : at + sizes.images].astype(bf16)
    act = spread(
        "wide", n_w, me_w, lambda peer: pooled.at[peer], received.at[me_w], act_send, act_recv
    )
    received[me_w] = pooled[me_w]

    arrived(two)
    wh[...] = jnp.zeros_like(wh)
    rows_in = lax.broadcasted_iota(jnp.int32, (WIDTH, sizes.head_rows), 0)
    cols_in = lax.broadcasted_iota(jnp.int32, (WIDTH, sizes.head_rows), 1)
    heads_full = jnp.zeros((WIDTH, WIDTH), jnp.float32)
    for w in range(n_w):
        block = got_two[w]
        at = w * br
        wu[at : at + br] = block[0:br, 0 : 4 * WIDTH]
        for part in range(2):
            wqkv[part, at : at + br] = block[0:br, (4 + part) * WIDTH : (5 + part) * WIDTH]
        wqkv[2, at : at + br] = block[br : 2 * br, 0:WIDTH]
        wp[at : at + br] = block[br : 2 * br, WIDTH : 2 * WIDTH]
        for j in range(4):
            wd[4 * at + j * br : 4 * at + (j + 1) * br] = block[
                br : 2 * br, (2 + j) * WIDTH : (3 + j) * WIDTH
            ]
        place = (rows_in == 2 * (w * bh + cols_in)) & (cols_in < bh)
        heads_full += nn(place.astype(bf16), got_head[w])
    wh[...] = heads_full.astype(bf16)

    arrived(act)
    groups = n_w * sizes.piece_rows // WIDTH
    per_group = n_w // groups
    piece = WIDTH // sizes.images
    for group in range(groups):
        block = received[group * per_group : (group + 1) * per_group].reshape(WIDTH, LANES)
        moved = tn(perm[...], block)
        for image in range(sizes.images):
            tok[image, group * piece : (group + 1) * piece, :] = moved[
                image * piece : (image + 1) * piece
            ].astype(bf16)
    sent(one)
    sent(two)
    sent(act)
def tail_kernel(
    sizes,
    lens,
    gtok,
    gh,
    gqkv,
    gp,
    gu,
    gdt,
    gvec,
    gub,
    vec,
    perm,
    step,
    sh,
    sqkv,
    sp,
    su,
    sd,
    table_hbm,
    wins_hbm,
    binput_hbm,
    bmodel_hbm,
    bqkv_hbm,
    bhidden_hbm,
    dact,
    cols,
    update,
    states,
    vtotal,
    scalars,
    table,
    wins,
    binput,
    bmodel,
    bqkv,
    bhidden,
    load_sem,
    outgoing,
    returned,
    grads,
    weighted,
    tapsum,
    stage_two,
    stage_head,
    rs_send,
    rs_got,
    rsh_send,
    rsh_got,
    stage_one,
    t_send,
    t_got,
    vpart,
    v_wide,
    v_dp,
    s_wide,
    mpack,
    dirs_got,
    row_head,
    row_qkv,
    row_proj,
    row_up,
    row_down,
    y_got,
    *sems,
):
    bf16, f32 = jnp.bfloat16, jnp.float32
    me_w, me_d = lax.axis_index("wide"), lax.axis_index("dp")
    n_w, n_d = sizes.wide, sizes.dp
    br, bh, bc = sizes.br, sizes.bh, sizes.bc
    sems = iter(sems)

    def scatter(axis, src_of, dst):
        count, me = (n_w, me_w) if axis == "wide" else (n_d, me_d)
        return spread(axis, count, me, src_of, dst, next(sems), next(sems))

    loads = []
    for at, (src, dst) in enumerate(
        (
            (bmodel_hbm, bmodel),
            (bhidden_hbm, bhidden),
            (binput_hbm, binput),
            (table_hbm, table),
            (wins_hbm, wins),
            (bqkv_hbm, bqkv),
        )
    ):
        copy = pltpu.make_async_copy(src, dst, load_sem.at[at])
        copy.start()
        loads.append(copy)
    greet((("wide", n_w, me_w), ("dp", n_d, me_d)))

    groups = n_w * sizes.piece_rows // WIDTH
    per_group = n_w // groups
    piece = WIDTH // sizes.images
    for group in range(groups):
        block = jnp.concatenate(
            [
                gtok[image, group * piece : (group + 1) * piece, :].astype(f32)
                for image in range(sizes.images)
            ],
            0,
        )
        moved = nn(perm[...], block.astype(bf16)).astype(bf16)
        outgoing[group * per_group : (group + 1) * per_group] = moved.reshape(
            per_group, sizes.piece_rows, LANES
        )
    back = scatter("wide", lambda peer: outgoing.at[peer], returned.at[me_w])
    returned[me_w] = outgoing[me_w]

    for load in loads[0:3]:
        load.wait()
    even = (
        lax.broadcasted_iota(jnp.int32, (WIDTH // 2, WIDTH), 1)
        == 2 * lax.broadcasted_iota(jnp.int32, (WIDTH // 2, WIDTH), 0)
    ).astype(bf16)
    u_head = tn(binput[...].astype(bf16), nn(even, gh[...].astype(bf16)).astype(bf16))
    left = bmodel[1].astype(bf16)
    u_qkv = [tn(left, gqkv[part].astype(bf16)) for part in range(3)]
    u_proj = tn(bmodel[2].astype(bf16), gp[...].astype(bf16))
    u_up = tn(bmodel[4].astype(bf16), gu[...].astype(bf16))
    u_down = jnp.transpose(nn(gdt[...].astype(bf16), bhidden[1].astype(bf16)))
    stage_two[...] = jnp.zeros_like(stage_two)
    stage_head[...] = jnp.zeros_like(stage_head)
    for w in range(n_w):
        at = w * br
        stage_two[0:br, 0 : 4 * WIDTH] = u_up[at : at + br]
        for part in range(2):
            stage_two[0:br, (4 + part) * WIDTH : (5 + part) * WIDTH] = u_qkv[part][at : at + br]
        stage_two[br : 2 * br, 0:WIDTH] = u_qkv[2][at : at + br]
        stage_two[br : 2 * br, WIDTH : 2 * WIDTH] = u_proj[at : at + br]
        for j in range(4):
            stage_two[br : 2 * br, (2 + j) * WIDTH : (3 + j) * WIDTH] = u_down[
                4 * at + j * br : 4 * at + (j + 1) * br
            ]
        stage_head[0:bh] = u_head[w * bh : (w + 1) * bh]
        rs_send[w] = stage_two[...].astype(bf16)
        rsh_send[w] = stage_head[...].astype(bf16)
    first = scatter("wide", lambda peer: rs_send.at[peer], rs_got.at[me_w])
    first += scatter("wide", lambda peer: rsh_send.at[peer], rsh_got.at[me_w])
    rs_got[me_w] = rs_send[me_w]
    rsh_got[me_w] = rsh_send[me_w]

    mpack[...] = jnp.zeros_like(mpack)
    for half in range(2):
        sizes.pack_blocks(
            mpack.at[half], (sh[half], sqkv[half], sp[half], su[half], sd[half])
        )

    taps = [local_columns(vec, me_w, sizes, e) for e in range(2)]
    for load in loads[3:5]:
        load.wait()
    arrived(back)
    for w in range(n_w):
        block = returned[w].astype(f32)
        for e in range(2):
            for c in range(sizes.channels):
                at = (e * sizes.channels + c) * sizes.images
                to = (c * n_w + w) * sizes.images
                grads[e, to : to + sizes.images] = block[at : at + sizes.images]
    big_len, small_len = lens
    lane = lax.broadcasted_iota(jnp.int32, (1, LANES), 1)
    token = ((lane >= 1) & (lane < big_len)) | ((lane > SPLIT) & (lane < SPLIT + small_len))
    lane_low = lax.broadcasted_iota(jnp.int32, (1, 128), 1)
    half_rows = sizes.channels * 8

    def collect(product):
        part = jnp.sum(product.reshape(sizes.channels, sizes.slots // 8, 8, LANES), 1)
        return jnp.sum(part.reshape(half_rows, LANES), -1, keepdims=True)

    for e in range(2):
        tapsum[e] = jnp.where(lane_low == 9, collect(jnp.where(token, grads[e], 0.0)), 0.0)
    for tap in range(9):
        win = wins[tap].astype(f32)
        mixed = jnp.zeros((), f32)
        for e in range(2):
            tapsum[e] = jnp.where(lane_low == tap, collect(grads[e] * win), tapsum[e])
            mixed += taps[e][:, tap : tap + 1] * grads[e]
        weighted[:, tap * LANES : (tap + 1) * LANES] = mixed.astype(bf16)
    cols[...] = jnp.where(lane_low == 0, grads[0, :, 0:128], grads[0, :, 128:256])

    @pl.loop(0, sizes.rows // 256)
    def _(chunk):
        at = pl.ds(pl.multiple_of(chunk * 256, 256), 256)
        dact[at, :] = nn(weighted[at, :], table[...])

    vpart[...] = jnp.zeros_like(vpart)
    own_channel = lax.broadcasted_iota(jnp.int32, (half_rows, WIDTH), 0) // 8
    own_lane = lax.broadcasted_iota(jnp.int32, (half_rows, WIDTH), 1)
    conv = jnp.zeros((128, WIDTH), f32)
    for e in range(2):
        place = (own_lane == 2 * (me_w * sizes.channels + own_channel) + e).astype(f32)
        conv += lax.dot_general(
            tapsum[e],
            place,
            (((0,), (0,)), ((), ())),
            precision=lax.Precision.HIGHEST,
            preferred_element_type=f32,
        )
    vpart[0:10] = conv[0:10]
    vpart[10:19] = gvec[0:9]
    for j in range(4):
        vpart[19 + j : 20 + j] = gub[:, j * WIDTH : (j + 1) * WIDTH]
    v_wide[me_w] = vpart[...]
    vec_one = scatter("wide", lambda peer: v_wide.at[me_w], v_wide.at[me_w])

    loads[5].wait()
    arrived(first)
    rows_two = rs_got[0].astype(f32)
    rows_head = rsh_got[0].astype(f32)
    for w in range(1, n_w):
        rows_two += rs_got[w].astype(f32)
        rows_head += rsh_got[w].astype(f32)
    rows_two = rows_two.astype(bf16)
    right = bqkv[...].astype(bf16)
    t_up = nn(rows_two[0:br, 0 : 4 * WIDTH], bhidden[0].astype(bf16))
    t_qkv = nn(rows_two[0:br, 4 * WIDTH : 6 * WIDTH], right[0 : 2 * WIDTH]) + nn(
        rows_two[br : 2 * br, 0:WIDTH], right[2 * WIDTH :]
    )
    t_proj = nn(rows_two[br : 2 * br, WIDTH : 2 * WIDTH], bmodel[3].astype(bf16))
    right = bmodel[5].astype(bf16)
    t_down = [
        nn(rows_two[br : 2 * br, (2 + j) * WIDTH : (3 + j) * WIDTH], right) for j in range(4)
    ]
    t_head = nn(rows_head.astype(bf16), bmodel[0].astype(bf16))
    stage_one[...] = jnp.zeros_like(stage_one)
    for d in range(n_d):
        own = slice(d * bc, (d + 1) * bc)
        sizes.pack_blocks(
            stage_one,
            (
                t_head[0:bh, own],
                t_qkv[:, 3 * d * bc : 3 * (d + 1) * bc],
                t_proj[:, own],
                t_up[:, 4 * d * bc : 4 * (d + 1) * bc],
                jnp.concatenate([t[:, own] for t in t_down], 0),
            ),
        )
        t_send[d] = stage_one[...].astype(bf16)
    second = scatter("dp", lambda peer: t_send.at[peer], t_got.at[me_d])
    t_got[me_d] = t_send[me_d]

    arrived(vec_one)
    vsum = v_wide[0]
    for w in range(1, n_w):
        vsum += v_wide[w]
    arrived(second)
    turned = t_got[0].astype(f32)
    for d in range(1, n_d):
        turned += t_got[d].astype(f32)
    own_square = jnp.sum(jnp.sum(turned * turned, -1, keepdims=True), 0, keepdims=True)
    last_row = lax.broadcasted_iota(jnp.int32, vsum.shape, 0) == vsum.shape[0] - 1
    v_dp[me_d] = jnp.where(last_row, own_square, vsum)
    vec_two = scatter("dp", lambda peer: v_dp.at[me_d], v_dp.at[me_d])
    arrived(vec_two)
    vsum = v_dp[0]
    for d in range(1, n_d):
        vsum += v_dp[d]
    s_wide[me_w] = jnp.broadcast_to(vsum[23:24, 0:128], (8, 128))
    third = scatter("wide", lambda peer: s_wide.at[me_w], s_wide.at[me_w])
    vsum = jnp.where(last_row, 0.0, vsum)
    vtotal[...] = vsum
    vec_square = jnp.sum(jnp.sum(vsum * vsum, -1, keepdims=True), 0, keepdims=True)
    count = jnp.full((8, 128), step[0], jnp.int32).astype(f32)[0:1, 0:1]
    fix_one = 1.0 - jnp.exp(count * float(np.log(beta_one)))
    fix_two = 1.0 - jnp.exp(count * float(np.log(beta_two)))
    arrived(third)
    square = s_wide[0][0:1, 0:1]
    for w in range(1, n_w):
        square += s_wide[w][0:1, 0:1]
    norm = jnp.sqrt(square + vec_square)
    factor = jnp.minimum(1.0, clip_limit / (norm + 1e-06))
    which = lax.broadcasted_iota(jnp.int32, (8, 128), 1)
    scalars[...] = jnp.where(
        which == 0,
        norm,
        jnp.where(which == 1, factor, jnp.where(which == 2, fix_one, fix_two)),
    )

    turned = turned * factor
    moment = beta_one * mpack[0] + (1.0 - beta_one) * turned
    second_moment = beta_two * mpack[1] * mpack[1] + (1.0 - beta_two) * turned * turned
    states[0] = moment
    states[1] = jnp.sqrt(second_moment)
    direction = moment / fix_one / (jnp.sqrt(second_moment / fix_two) + adam_eps)
    dirs_got[me_d] = direction.astype(bf16)
    fourth = scatter("dp", lambda peer: dirs_got.at[me_d], dirs_got.at[me_d])
    arrived(fourth)
    for d in range(n_d):
        head, qkv, proj, up, down = sizes.unpack_blocks(dirs_got[d].astype(f32))
        row_head[0:bh, d * bc : (d + 1) * bc] = head
        row_qkv[:, 3 * d * bc : 3 * (d + 1) * bc] = qkv
        row_proj[:, d * bc : (d + 1) * bc] = proj
        row_up[:, 4 * d * bc : 4 * (d + 1) * bc] = up
        row_down[:, d * bc : (d + 1) * bc] = down

    def right_rows(ref, size):
        return ref[pl.ds(pl.multiple_of(me_d * size, 8), size), :].astype(bf16)

    stage_one[...] = jnp.zeros_like(stage_one)
    sizes.pack_blocks(
        stage_one,
        (
            nt(row_head[...].astype(bf16), right_rows(bmodel.at[0], bc))[0:bh],
            nt(row_qkv[...].astype(bf16), right_rows(bqkv, 3 * bc)),
            nt(row_proj[...].astype(bf16), right_rows(bmodel.at[3], bc)),
            nt(row_up[...].astype(bf16), right_rows(bhidden.at[0], 4 * bc)),
            nt(row_down[...].astype(bf16), right_rows(bmodel.at[5], bc)),
        ),
    )
    y_got[me_w] = stage_one[...].astype(bf16)
    fifth = scatter("wide", lambda peer: y_got.at[me_w], y_got.at[me_w])
    def left_rows(ref, size):
        if size % 8 == 0:
            return ref[pl.ds(pl.multiple_of(me_w * size, 8), size), :].astype(bf16)
        own = lax.broadcasted_iota(jnp.int32, (size, ref.shape[0]), 0) + me_w * size
        pick = own == lax.broadcasted_iota(jnp.int32, (size, ref.shape[0]), 1)
        return nn(pick.astype(bf16), ref[...].astype(bf16)).astype(bf16)

    lefts = (
        left_rows(binput, bh),
        left_rows(bmodel.at[1], br),
        left_rows(bmodel.at[2], br),
        left_rows(bmodel.at[4], br),
        left_rows(bhidden.at[1], 4 * br),
    )
    arrived(fifth)
    parts = [sizes.unpack_blocks(y_got[w].astype(f32)) for w in range(n_w)]
    update[...] = jnp.zeros_like(update)
    sizes.pack_blocks(
        update,
        [
            nn(
                lefts[member],
                jnp.concatenate([part[member] for part in parts], 0).astype(bf16),
            )
            for member in range(5)
        ],
    )
    for copies in (back, first, vec_one, second, vec_two, third, fourth, fifth):
        sent(copies)


def finish_kernel(
    sizes, mh, mqkv, mp, mu, md, vec, vmom, update, states, vtotal, scalars, nvec, nvmom, *outs
):
    factor, fix_one, fix_two = (scalars[0:1, j : j + 1] for j in (1, 2, 3))
    updates = sizes.unpack_blocks(update[...])
    firsts = sizes.unpack_blocks(states[0])
    seconds = sizes.unpack_blocks(states[1])
    for member, master in enumerate((mh, mqkv, mp, mu, md)):
        fresh = master[...] - rate_matrix * updates[member]
        outs[member][...] = fresh
        outs[5 + member][0] = firsts[member]
        outs[5 + member][1] = seconds[member]
        outs[10 + member][...] = fresh.astype(jnp.bfloat16)
    scaled = vtotal[0:23] * factor
    first = beta_one * vmom[0] + (1.0 - beta_one) * scaled
    second = beta_two * vmom[1] * vmom[1] + (1.0 - beta_two) * scaled * scaled
    direction = first / fix_one / (jnp.sqrt(second / fix_two) + adam_eps)
    nvec[...] = vec[...] * (1.0 - rate_vector * decay_rate) - rate_vector * direction
    nvmom[0] = first
    nvmom[1] = jnp.sqrt(second)


VM = pl.BlockSpec(memory_space=pltpu.VMEM)
SM = pl.BlockSpec(memory_space=pltpu.SMEM)
HB = pl.BlockSpec(memory_space=pl.ANY)
LIMIT = 60 * 1024 * 1024


def dma_sems(*counts):
    return [pltpu.SemaphoreType.DMA((n,)) for n in counts]


def run_front(sizes, lens, cells, heads, vec, table, perm, masters):
    bf16, f32 = jnp.bfloat16, jnp.float32
    w, d = sizes.wide, sizes.dp
    outs = [
        ((sizes.images, WIDTH, LANES), bf16),
        ((9, sizes.rows, LANES), bf16),
        ((WIDTH, WIDTH), bf16),
        ((3, WIDTH, WIDTH), bf16),
        ((WIDTH, WIDTH), bf16),
        ((WIDTH, 4 * WIDTH), bf16),
        ((4 * WIDTH, WIDTH), bf16),
    ]
    return pl.pallas_call(
        partial(front_kernel, sizes, lens),
        in_specs=[VM] * 10,
        out_specs=[VM] * len(outs),
        out_shape=[jax.ShapeDtypeStruct(s, t) for s, t in outs],
        scratch_shapes=[
            pltpu.VMEM((sizes.pair_rows, sizes.block_lanes), f32),
            pltpu.VMEM((sizes.pair_rows, 6 * WIDTH), f32),
            pltpu.VMEM((sizes.head_rows, WIDTH), f32),
            pltpu.VMEM((d, sizes.pair_rows, sizes.block_lanes), bf16),
            pltpu.VMEM((w, sizes.pair_rows, 6 * WIDTH), bf16),
            pltpu.VMEM((w, sizes.head_rows, WIDTH), bf16),
            pltpu.VMEM((w, sizes.piece_rows, LANES), bf16),
            pltpu.VMEM((w, sizes.piece_rows, LANES), bf16),
            pltpu.VMEM((2, sizes.rows, LANES), f32),
        ]
        + dma_sems(d - 1, d - 1, w - 1, w - 1, w - 1, w - 1, w - 1, w - 1),
        compiler_params=pltpu.CompilerParams(
            collective_id=0, has_side_effects=True, vmem_limit_bytes=LIMIT
        ),
        name="front",
    )(cells, heads, vec, table, perm, *masters)


def run_tail(sizes, lens, grads, vec, perm, step, moments, table, wins, bases):
    bf16, f32 = jnp.bfloat16, jnp.float32
    w, d = sizes.wide, sizes.dp
    pack = (sizes.pair_rows, sizes.block_lanes)
    outs = [
        ((sizes.rows, CELLS_PAD), f32),
        ((sizes.rows, 128), f32),
        (pack, f32),
        ((2,) + pack, f32),
        ((24, WIDTH), f32),
        ((8, 128), f32),
    ]
    two = (sizes.pair_rows, 6 * WIDTH)
    head = (sizes.head_rows, WIDTH)
    piece = (w, sizes.piece_rows, LANES)
    return pl.pallas_call(
        partial(tail_kernel, sizes, lens),
        in_specs=[VM] * 10 + [SM] + [VM] * 5 + [HB] * 6,
        out_specs=[VM] * len(outs),
        out_shape=[jax.ShapeDtypeStruct(s, t) for s, t in outs],
        scratch_shapes=[pltpu.VMEM(a.shape, a.dtype) for a in (table, wins, *bases)]
        + dma_sems(6)
        + [
            pltpu.VMEM(piece, bf16),
            pltpu.VMEM(piece, bf16),
            pltpu.VMEM((2, sizes.rows, LANES), f32),
            pltpu.VMEM((sizes.rows, 9 * LANES), bf16),
            pltpu.VMEM((2, sizes.channels * 8, 128), f32),
            pltpu.VMEM(two, f32),
            pltpu.VMEM(head, f32),
            pltpu.VMEM((w,) + two, bf16),
            pltpu.VMEM((w,) + two, bf16),
            pltpu.VMEM((w,) + head, bf16),
            pltpu.VMEM((w,) + head, bf16),
            pltpu.VMEM(pack, f32),
            pltpu.VMEM((d,) + pack, bf16),
            pltpu.VMEM((d,) + pack, bf16),
            pltpu.VMEM((24, WIDTH), f32),
            pltpu.VMEM((w, 24, WIDTH), f32),
            pltpu.VMEM((d, 24, WIDTH), f32),
            pltpu.VMEM((w, 8, 128), f32),
            pltpu.VMEM((2,) + pack, f32),
            pltpu.VMEM((d,) + pack, bf16),
            pltpu.VMEM((sizes.bh, WIDTH), f32),
            pltpu.VMEM((sizes.br, 3 * WIDTH), f32),
            pltpu.VMEM((sizes.br, WIDTH), f32),
            pltpu.VMEM((sizes.br, 4 * WIDTH), f32),
            pltpu.VMEM((4 * sizes.br, WIDTH), f32),
            pltpu.VMEM((w,) + pack, bf16),
        ]
        + dma_sems(
            *(n - 1 for n in (w, w, w, w, w, w, w, w, d, d, d, d, w, w, d, d, w, w))
        ),
        compiler_params=pltpu.CompilerParams(
            collective_id=1, has_side_effects=True, vmem_limit_bytes=LIMIT
        ),
        name="tail",
    )(*grads, vec, perm, step, *moments, table, wins, *bases)


def run_finish(sizes, masters, vec, vmom, packs):
    f32, bf16 = jnp.float32, jnp.bfloat16
    shapes = [m.shape for m in masters]
    outs = [(vec.shape, f32), (vmom.shape, f32)]
    outs += [(s, f32) for s in shapes] + [((2,) + s, f32) for s in shapes]
    outs += [(s, bf16) for s in shapes]
    return pl.pallas_call(
        partial(finish_kernel, sizes),
        in_specs=[VM] * 11,
        out_specs=[VM] * len(outs),
        out_shape=[jax.ShapeDtypeStruct(s, t) for s, t in outs],
        name="finish",
    )(*masters, vec, vmom, *packs)


def pool_table(grids):
    table = np.zeros((9, LANES, CELLS_PAD), np.float32)
    base = 0
    for grid, side, lane in grids:
        for tap in range(9):
            for y in range(side):
                for x in range(side):
                    sy, sx = 2 * y + tap // 3 - 1, 2 * x + tap % 3 - 1
                    if 0 <= sy < grid and 0 <= sx < grid:
                        table[tap, lane + y * side + x, base + sy * grid + sx] = 1.0
        base += grid * grid
    return jnp.asarray(table.reshape(9 * LANES, CELLS_PAD), jnp.bfloat16)


def per_device(
    wide_n,
    dp_n,
    big_act,
    big_cls,
    small_act,
    small_cls,
    big_order,
    small_order,
    big_cot,
    small_cot,
    vec_params,
    vec_moments,
    *rest,
):
    masters, moments, bases, step = rest[0:5], rest[5:10], rest[10:14], rest[14]
    channels = big_act.shape[1]
    images, small_images = big_cot.shape[0], small_cot.shape[0]
    lens = (big_cot.shape[1], small_cot.shape[1])
    sizes = Sizes(wide_n, dp_n, channels, images, small_images)
    big_cells, small_cells = big_act.shape[2], small_act.shape[2]
    grids = tuple(
        (int(cells**0.5), int((length - 1) ** 0.5), lane)
        for cells, length, lane in ((big_cells, lens[0], 1), (small_cells, lens[1], SPLIT + 1))
    )
    table = pool_table(grids)
    perm = row_permutation(channels, images)
    take = lambda a, i, axis: jnp.take(a, i, axis=axis, mode="clip")

    big_slots = big_order[0]
    small_slots = jnp.pad(
        small_order[0].reshape(wide_n, small_images), ((0, 0), (0, images - small_images))
    ).reshape(-1)
    cells = jnp.concatenate(
        [
            take(big_act, big_slots, 0),
            take(small_act, small_slots, 0),
            jnp.zeros(
                (big_slots.shape[0], channels, CELLS_PAD - big_cells - small_cells), jnp.bfloat16
            ),
        ],
        2,
    )
    cells = jnp.swapaxes(cells, 0, 1).reshape(sizes.rows, CELLS_PAD)
    heads = jnp.stack([take(big_cls, big_slots, 0), take(small_cls, small_slots, 0)], 2)
    heads = jnp.swapaxes(heads, 0, 1).reshape(sizes.rows, 2).astype(jnp.float32)

    tok, wins, wh, wqkv, wp, wu, wd = run_front(
        sizes, lens, cells, heads, vec_params, table, perm, masters
    )
    hidden = wu.shape[1]
    block = run_block(
        tok, big_cot, small_cot, vec_params, vec_params[19:].reshape(1, hidden), wh, wqkv, wp, wu, wd
    )
    dact, cols, update, states, vtotal, scalars = run_tail(
        sizes, lens, block[2:], vec_params, perm, step, moments, table, wins, bases
    )
    results = run_finish(
        sizes, masters, vec_params, vec_moments, (update, states, vtotal, scalars)
    )

    ids = lambda n: jnp.arange(n, dtype=jnp.int32)
    big_count, small_count = big_act.shape[0], small_act.shape[0]
    big_inverse = jnp.sum(
        jnp.where(big_slots[:, None] == ids(big_count)[None], ids(big_count)[:, None], 0), 0
    )
    small_at = ids(small_count) // small_images * images + ids(small_count) % small_images
    small_inverse = jnp.sum(
        jnp.where(small_order[0][:, None] == ids(small_count)[None], small_at[:, None], 0), 0
    )
    dact = dact.reshape(channels, sizes.slots, CELLS_PAD)
    cols = cols.reshape(channels, sizes.slots, 128)
    low = SPLIT - 128
    big_act_grad = jnp.swapaxes(take(dact[:, :, :big_cells], big_inverse, 1), 0, 1)
    small_act_grad = jnp.swapaxes(
        take(dact[:, :, big_cells : big_cells + small_cells], small_inverse, 1), 0, 1
    )
    big_cls_grad = jnp.swapaxes(take(cols[:, :, 0], big_inverse, 1), 0, 1)
    small_cls_grad = jnp.swapaxes(take(cols[:, :, low], small_inverse, 1), 0, 1)
    return (
        block[0],
        block[1],
        big_act_grad,
        big_cls_grad,
        small_act_grad,
        small_cls_grad,
        scalars[0, 0:1],
        *results,
    )


def solution(mesh):
    split, wide_first, free = P("dp", "wide", None), P("wide", "dp"), P()
    moment = P(None, "wide", "dp")
    both = P(("dp", "wide"), None, None)
    acts = (split, P("dp", "wide"), split, P("dp", "wide"))
    in_specs = (
        acts
        + (P("dp", None), P("dp", None), both, both, free, free)
        + (wide_first,) * 5
        + (moment,) * 5
        + (free,) * 5
    )
    out_specs = (
        (both, both) + acts + (free,) * 3 + (wide_first,) * 5 + (moment,) * 5 + (wide_first,) * 5
    )
    return jax.shard_map(
        partial(per_device, mesh.shape["wide"], mesh.shape["dp"]),
        mesh=mesh,
        in_specs=in_specs,
        out_specs=out_specs,
        check_vma=False,
    )
```

```python
from functools import partial

import jax
import jax.numpy as jnp
import numpy as np
from jax import lax
from jax.experimental import pallas as pl
from jax.experimental.pallas import tpu as pltpu
from jax.sharding import PartitionSpec as P

HEADS = 4
HD = 48
beta_one = 0.9
beta_two = 0.999
adam_eps = 1e-08
norm_eps = 1e-06
rate_matrix = 0.08
rate_vector = 0.25
decay_rate = 0.05
clip_limit = 1.0
LANES = 256
SPLIT = 208


def nt(a, b):
    return lax.dot_general(a, b, (((1,), (1,)), ((), ())), preferred_element_type=jnp.float32)


def tn(a, b):
    return lax.dot_general(a, b, (((0,), (0,)), ((), ())), preferred_element_type=jnp.float32)


def nn(a, b):
    return jnp.dot(a, b, preferred_element_type=jnp.float32)


def colsum(v):
    return jnp.sum(v, 0, keepdims=True)


def norm_forward(rows, gain, shift):
    centered = rows - jnp.mean(rows, -1, keepdims=True)
    scale = lax.rsqrt(jnp.mean(centered * centered, -1, keepdims=True) + norm_eps)
    hat = centered * scale
    return hat, scale, (hat * gain + shift).astype(jnp.bfloat16)


def norm_backward(grad, hat, scale, gain):
    inner = grad * gain
    mean_a = jnp.mean(inner, -1, keepdims=True)
    mean_b = jnp.mean(inner * hat, -1, keepdims=True)
    return scale * (inner - mean_a - hat * mean_b)


def block_kernel(
    counts,
    tok,
    bcot,
    scot,
    vec,
    wh,
    wqkv,
    wp,
    wu,
    wd,
    bout,
    sout,
    gtok,
    gh,
    gqkv,
    gp,
    gu,
    gdt,
    gvec,
    gub,
    probs,
    bias,
    cot,
    ubias,
):
    big_n, small_n, big_len, small_len = counts
    step = pl.program_id(0)
    width = vec.shape[1]
    row_id = lax.broadcasted_iota(jnp.int32, (LANES, 1), 0)
    lane_id = lax.broadcasted_iota(jnp.int32, (1, width), 1)

    @pl.when(step == 0)
    def _():
        for ref in (gh, gqkv, gp, gu, gdt, gvec, gub):
            ref[...] = jnp.zeros_like(ref)
        cot[...] = jnp.zeros_like(cot)
        for j in range(4):
            ubias[:, j * width : (j + 1) * width] = vec[19 + j : 20 + j]
        key_id = lax.broadcasted_iota(jnp.int32, (LANES, LANES), 1)
        query_id = lax.broadcasted_iota(jnp.int32, (LANES, LANES), 0)
        keep_big = (query_id < SPLIT) & (key_id < big_len)
        keep_small = (query_id >= SPLIT) & (key_id >= SPLIT) & (key_id < SPLIT + small_len)
        bias[...] = jnp.where(keep_big | keep_small, 0.0, -1e30)

    raw = jnp.transpose(tok[0].astype(jnp.float32))
    raw_low = raw.astype(jnp.bfloat16)
    is_head = (row_id == 0) | (row_id == SPLIT)
    rows = jnp.where(is_head, nn(raw_low, wh[...]) + vec[10:11], raw)
    hat_one, scale_one, normed_one = norm_forward(rows, vec[11:12], vec[12:13])
    queries = (nn(normed_one, wqkv[0]) + vec[13:14]).astype(jnp.bfloat16)
    keys_in = nn(normed_one, wqkv[1]).astype(jnp.bfloat16)
    values = (nn(normed_one, wqkv[2]) + vec[14:15]).astype(jnp.bfloat16)
    zero = jnp.zeros((), jnp.bfloat16)
    in_head = [(lane_id >= h * HD) & (lane_id < (h + 1) * HD) for h in range(HEADS)]
    mixture = jnp.zeros((LANES, width), jnp.float32)
    for h in range(HEADS):
        scores = nt(jnp.where(in_head[h], queries, zero), keys_in) * HD ** (-0.5) + bias[...]
        weights = jnp.exp(scores - jnp.max(scores, -1, keepdims=True))
        probas = weights * (1.0 / jnp.sum(weights, -1, keepdims=True))
        probs[h] = probas
        mixture += nn(probas.astype(jnp.bfloat16), jnp.where(in_head[h], values, zero))
    mixture = mixture.astype(jnp.bfloat16)
    middle = rows + nn(mixture, wp[...]) + vec[15:16]
    hat_two, scale_two, normed_two = norm_forward(middle, vec[16:17], vec[17:18])
    pre = nn(normed_two, wu[...]) + ubias[...]
    cdf = 0.5 + 0.5 * lax.erf(pre * 0.7071067811865476)
    slope = cdf + pre * jnp.exp(pre * pre * -0.5) * 0.3989422804014327
    active = (pre * cdf).astype(jnp.bfloat16)
    result = middle + nn(active, wd[...]) + vec[18:19]
    bout[0] = jnp.transpose(result)[:, :big_len]
    cot[:big_len] = jnp.transpose(bcot[0].astype(jnp.float32)).astype(jnp.bfloat16)

    @pl.when(step < small_n)
    def _():
        sout[0] = result[SPLIT : SPLIT + small_len]
        cot[SPLIT : SPLIT + small_len] = scot[0]

    @pl.when(step == small_n)
    def _():
        cot[SPLIT:] = jnp.zeros((LANES - SPLIT, width), jnp.bfloat16)

    cot_low = cot[...]
    cot_rows = cot_low.astype(jnp.float32)
    gdt[...] += tn(cot_low, active)
    gvec[8:9] += colsum(cot_rows)
    grad_pre = (nt(cot_low, wd[...]) * slope).astype(jnp.bfloat16)
    gu[...] += tn(normed_two, grad_pre)
    gub[...] += colsum(grad_pre.astype(jnp.float32))
    grad_two = nt(grad_pre, wu[...])
    gvec[6:7] += colsum(grad_two * hat_two)
    gvec[7:8] += colsum(grad_two)
    grad_mid = norm_backward(grad_two, hat_two, scale_two, vec[16:17]) + cot_rows
    branch = grad_mid.astype(jnp.bfloat16)
    gp[...] += tn(mixture, branch)
    gvec[5:6] += colsum(branch.astype(jnp.float32))
    grad_mix = nt(branch, wp[...]).astype(jnp.bfloat16)
    grad_q = jnp.zeros((LANES, width), jnp.float32)
    grad_k = jnp.zeros((LANES, width), jnp.float32)
    grad_v = jnp.zeros((LANES, width), jnp.float32)
    for h in range(HEADS):
        probas = probs[h]
        own = jnp.where(in_head[h], grad_mix, zero)
        grad_probs = nt(own, values)
        inner = jnp.sum(probas * grad_probs, -1, keepdims=True)
        grad_scores = (probas * (grad_probs - inner)).astype(jnp.bfloat16)
        grad_q += nn(grad_scores, jnp.where(in_head[h], keys_in, zero))
        grad_k += tn(grad_scores, jnp.where(in_head[h], queries, zero))
        grad_v += tn(probas.astype(jnp.bfloat16), own)
    grad_q = (grad_q * HD ** (-0.5)).astype(jnp.bfloat16)
    grad_k = (grad_k * HD ** (-0.5)).astype(jnp.bfloat16)
    grad_v = grad_v.astype(jnp.bfloat16)
    gqkv[0] += tn(normed_one, grad_q)
    gqkv[1] += tn(normed_one, grad_k)
    gqkv[2] += tn(normed_one, grad_v)
    gvec[3:4] += colsum(grad_q.astype(jnp.float32))
    gvec[4:5] += colsum(grad_v.astype(jnp.float32))
    grad_one = nt(grad_q, wqkv[0]) + nt(grad_k, wqkv[1]) + nt(grad_v, wqkv[2])
    gvec[1:2] += colsum(grad_one * hat_one)
    gvec[2:3] += colsum(grad_one)
    grad_tok = norm_backward(grad_one, hat_one, scale_one, vec[11:12]) + grad_mid
    grad_head = jnp.where(is_head, grad_tok, 0.0).astype(jnp.bfloat16)
    gh[...] += tn(raw_low, grad_head)
    gvec[0:1] += colsum(grad_head.astype(jnp.float32))
    gtok[0] = jnp.transpose(jnp.where(is_head, nt(grad_head, wh[...]), grad_tok)).astype(jnp.bfloat16)


def whole(shape):
    return pl.BlockSpec(shape, lambda i: (0,) * len(shape))


def run_block(tok, big_cot, small_cot, vec, wh, wqkv, wp, wu, wd):
    big_n, width, big_len = big_cot.shape
    small_n, small_len = small_cot.shape[:2]
    f32 = jnp.float32
    hidden = wu.shape[1]
    outs = [
        ((big_n, width, big_len), f32),
        ((small_n, small_len, width), f32),
        (tok.shape, jnp.bfloat16),
        ((width, width), f32),
        ((3, width, width), f32),
        ((width, width), f32),
        ((width, hidden), f32),
        ((width, hidden), f32),
        ((16, width), f32),
        ((1, hidden), f32),
    ]
    one_big = pl.BlockSpec((1, width, big_len), lambda i: (i, 0, 0))
    one_small = pl.BlockSpec((1, small_len, width), lambda i: (jnp.minimum(i, small_n - 1), 0, 0))
    one_tok = pl.BlockSpec((1, width, LANES), lambda i: (i, 0, 0))
    return pl.pallas_call(
        partial(block_kernel, (big_n, small_n, big_len, small_len)),
        grid=(big_n,),
        in_specs=[one_tok, one_big, one_small]
        + [whole(a.shape) for a in (vec, wh, wqkv, wp, wu, wd)],
        out_specs=[one_big, one_small, one_tok] + [whole(s) for s, _ in outs[3:]],
        out_shape=[jax.ShapeDtypeStruct(s, d) for s, d in outs],
        scratch_shapes=[
            pltpu.VMEM((HEADS, LANES, LANES), f32),
            pltpu.VMEM((LANES, LANES), f32),
            pltpu.VMEM((LANES, width), jnp.bfloat16),
            pltpu.VMEM((1, hidden), f32),
        ],
        compiler_params=pltpu.CompilerParams(vmem_limit_bytes=56 * 1024 * 1024),
        name="block",
    )(tok, big_cot, small_cot, vec, wh, wqkv, wp, wu, wd)


def row_permutation(channels, images):
    width = 192
    group = width // (2 * channels * images)
    table = np.zeros((width, width), np.float32)
    for s in range(group):
        for e in range(2):
            for c in range(channels):
                for i in range(images):
                    row = ((s * 2 + e) * channels + c) * images + i
                    table[row, i * (width // images) + s * 2 * channels + 2 * c + e] = 1.0
    return jnp.asarray(table, jnp.bfloat16)
MESH = pl.DeviceIdType.MESH
WIDTH = 192


def up_to(value, unit):
    return -(-value // unit) * unit


def spread(axis, count, me, src_of, dst, send, recv):
    copies = []
    for k in range(1, count):
        peer = lax.rem(me + k, count)
        copy = pltpu.make_async_remote_copy(
            src_ref=src_of(peer),
            dst_ref=dst,
            send_sem=send.at[k - 1],
            recv_sem=recv.at[k - 1],
            device_id={axis: peer},
            device_id_type=MESH,
        )
        copy.start()
        copies.append(copy)
    return copies


def arrived(copies):
    for copy in copies:
        copy.wait_recv()


def sent(copies):
    for copy in copies:
        copy.wait_send()


def greet(axes):
    barrier = pltpu.get_barrier_semaphore()
    total = 0
    for axis, count, me in axes:
        for k in range(1, count):
            pl.semaphore_signal(
                barrier,
                inc=1,
                device_id={axis: lax.rem(me + k, count)},
                device_id_type=MESH,
            )
        total += count - 1
    pl.semaphore_wait(barrier, total)


class Sizes:
    def __init__(self, wide, dp, channels, images, small_images):
        self.wide, self.dp = wide, dp
        self.channels, self.images, self.small_images = channels, images, small_images
        self.slots = wide * images
        self.rows = channels * self.slots
        self.small_slots = wide * small_images
        self.small_rows = channels * self.small_slots
        self.piece_rows = 2 * channels * images
        self.br = WIDTH // wide
        self.bh = self.br // 2
        self.bc = WIDTH // dp
        self.pair_rows = up_to(2 * self.br, 16)
        self.block_lanes = up_to(7 * self.bc, 128)
        self.head_rows = up_to(self.bh, 16)

    def block_places(self):
        br, bh, bc = self.br, self.bh, self.bc
        return (
            [(0, 6 * bc, bh, bc)],
            [(br, 0, br, 3 * bc)],
            [(br, 3 * bc, br, bc)],
            [(0, 0, br, 4 * bc)],
            [(0, 4 * bc, br, bc), (0, 5 * bc, br, bc), (br, 4 * bc, br, bc), (br, 5 * bc, br, bc)],
        )

    def pack_blocks(self, ref, blocks):
        for block, places in zip(blocks, self.block_places()):
            at = 0
            for row, lane, rows, lanes in places:
                ref[row : row + rows, lane : lane + lanes] = block[at : at + rows]
                at += rows

    def unpack_blocks(self, packed):
        result = []
        for places in self.block_places():
            parts = [packed[r : r + n, q : q + m] for r, q, n, m in places]
            result.append(parts[0] if len(parts) == 1 else jnp.concatenate(parts, 0))
        return result


def placements(order_big, order_small, sizes):
    n, m = sizes.slots, sizes.small_slots
    big = order_big[...] == lax.broadcasted_iota(jnp.int32, (n, n), 0)
    small = order_small[...] == lax.broadcasted_iota(jnp.int32, (m, m), 0)
    slot = lax.broadcasted_iota(jnp.int32, (m, n), 0)
    padded = lax.broadcasted_iota(jnp.int32, (m, n), 1)
    inside = padded % sizes.images
    spread_out = (slot == padded // sizes.images * sizes.small_images + inside) & (
        inside < sizes.small_images
    )
    one = lambda v: v.astype(jnp.float32).astype(jnp.bfloat16)
    return one(big), nn(one(small), one(spread_out)).astype(jnp.bfloat16)


def token_lanes(lens):
    low = lax.broadcasted_iota(jnp.int32, (1, LANES), 1)
    high = lax.broadcasted_iota(jnp.int32, (1, 128), 1) + 128
    return (low >= 1) & (low < lens[0]), (high > SPLIT) & (high < SPLIT + lens[1])


def front_kernel(
    sizes,
    lens,
    act_big,
    act_small,
    cls_big,
    cls_small,
    order_big,
    order_small,
    vec,
    table_big,
    table_small,
    perm,
    mh,
    mqkv,
    mp,
    mu,
    md,
    tok,
    wins_big,
    wins_small,
    wh,
    wqkv,
    wp,
    wu,
    wd,
    stage_one,
    stage_two,
    stage_head,
    got_one,
    got_two,
    got_head,
    pooled,
    received,
    sum_big,
    sum_small,
    one_send,
    one_recv,
    two_send,
    two_recv,
    head_send,
    head_recv,
    act_send,
    act_recv,
):
    bf16 = jnp.bfloat16
    me_w, me_d = lax.axis_index("wide"), lax.axis_index("dp")
    n_w, n_d = sizes.wide, sizes.dp
    br, bh, bc = sizes.br, sizes.bh, sizes.bc
    greet((("wide", n_w, me_w), ("dp", n_d, me_d)))
    stage_one[...] = jnp.zeros_like(stage_one)
    sizes.pack_blocks(stage_one, (mh[...], mqkv[...], mp[...], mu[...], jnp.transpose(md[...])))
    got_one[me_d] = stage_one[...].astype(bf16)
    one = spread("dp", n_d, me_d, lambda peer: got_one.at[me_d], got_one.at[me_d], one_send, one_recv)

    n_big, n_small = sizes.slots, sizes.small_slots
    rows_big = act_big[...].reshape(sizes.rows, act_big.shape[2])
    rows_small = act_small[...].reshape(sizes.small_rows, act_small.shape[2])

    def pool(tap):
        for rows, table, wins, sums, count in (
            (rows_big, table_big, wins_big, sum_big, n_big),
            (rows_small, table_small, wins_small, sum_small, n_small),
        ):
            win = nt(rows, table[tap])
            wins[tap] = win.astype(bf16)
            for c in range(sizes.channels):
                own = slice(c * count, (c + 1) * count)
                for e in range(2):
                    part = vec[tap, 2 * (me_w * sizes.channels + c) + e] * win[own]
                    if tap == 0:
                        sums[e, own] = part
                    else:
                        sums[e, own] += part

    for tap in range(4):
        pool(tap)
    arrived(one)
    stage_two[...] = jnp.zeros_like(stage_two)
    stage_head[...] = jnp.zeros_like(stage_head)
    for d in range(n_d):
        head, qkv, proj, up, down = sizes.unpack_blocks(got_one[d].astype(jnp.float32))
        stage_head[0:bh, d * bc : (d + 1) * bc] = head
        stage_two[0:br, d * 4 * bc : (d + 1) * 4 * bc] = up
        for part in range(3):
            low, high = d * 3 * bc, (d + 1) * 3 * bc
            a, b = max(low, part * WIDTH), min(high, (part + 1) * WIDTH)
            if a < b:
                row = 0 if part < 2 else br
                base = (4 + part) * WIDTH if part < 2 else 0
                stage_two[row : row + br, base + a - part * WIDTH : base + b - part * WIDTH] = qkv[
                    :, a - low : b - low
                ]
        stage_two[br : 2 * br, WIDTH + d * bc : WIDTH + (d + 1) * bc] = proj
        for j in range(4):
            at = (2 + j) * WIDTH + d * bc
            stage_two[br : 2 * br, at : at + bc] = down[j * br : (j + 1) * br]
    got_two[me_w] = stage_two[...].astype(bf16)
    got_head[me_w] = stage_head[...].astype(bf16)
    two = spread("wide", n_w, me_w, lambda peer: got_two.at[me_w], got_two.at[me_w], two_send, two_recv)
    two += spread(
        "wide", n_w, me_w, lambda peer: got_head.at[me_w], got_head.at[me_w], head_send, head_recv
    )
    for tap in range(4, 9):
        pool(tap)

    put_big, put_small = placements(order_big, order_small, sizes)
    slot_big = jnp.transpose(put_big.astype(jnp.float32)).astype(bf16)
    slot_small = jnp.transpose(put_small.astype(jnp.float32)).astype(bf16)
    head_big, head_small = nt(slot_big, cls_big[...]), nt(slot_small, cls_small[...])
    token_big, token_small = token_lanes(lens)
    lane = lax.broadcasted_iota(jnp.int32, (1, 128), 1)
    for e in range(2):
        for c in range(sizes.channels):
            shift = vec[9, 2 * (me_w * sizes.channels + c) + e]
            big = jnp.where(token_big, sum_big[e, c * n_big : (c + 1) * n_big] + shift, 0.0)
            small = jnp.where(
                token_small, sum_small[e, c * n_small : (c + 1) * n_small] + shift, 0.0
            )
            big = nn(slot_big, big.astype(bf16))
            low, high = big[:, 0:128], big[:, 128:256] + nn(slot_small, small.astype(bf16))
            if e == 0:
                low = jnp.where(lane == 0, head_big[:, c : c + 1], low)
                high = jnp.where(lane == SPLIT - 128, head_small[:, c : c + 1], high)
            at = (e * sizes.channels + c) * sizes.images
            for half, value in enumerate((low, high)):
                value = value.reshape(n_w, sizes.images, 128).astype(bf16)
                pooled[:, at : at + sizes.images, half * 128 : half * 128 + 128] = value
    act = spread(
        "wide", n_w, me_w, lambda peer: pooled.at[peer], received.at[me_w], act_send, act_recv
    )
    received[me_w] = pooled[me_w]

    arrived(two)
    wh[...] = jnp.zeros_like(wh)
    rows_in = lax.broadcasted_iota(jnp.int32, (WIDTH, sizes.head_rows), 0)
    cols_in = lax.broadcasted_iota(jnp.int32, (WIDTH, sizes.head_rows), 1)
    heads_full = jnp.zeros((WIDTH, WIDTH), jnp.float32)
    for w in range(n_w):
        block = got_two[w]
        at = w * br
        wu[at : at + br] = block[0:br, 0 : 4 * WIDTH]
        for part in range(2):
            wqkv[part, at : at + br] = block[0:br, (4 + part) * WIDTH : (5 + part) * WIDTH]
        wqkv[2, at : at + br] = block[br : 2 * br, 0:WIDTH]
        wp[at : at + br] = block[br : 2 * br, WIDTH : 2 * WIDTH]
        for j in range(4):
            wd[4 * at + j * br : 4 * at + (j + 1) * br] = block[
                br : 2 * br, (2 + j) * WIDTH : (3 + j) * WIDTH
            ]
        place = (rows_in == 2 * (w * bh + cols_in)) & (cols_in < bh)
        heads_full += nn(place.astype(bf16), got_head[w])
    wh[...] = heads_full.astype(bf16)

    arrived(act)
    groups = n_w * sizes.piece_rows // WIDTH
    per_group = n_w // groups
    piece = WIDTH // sizes.images
    for group in range(groups):
        block = received[group * per_group : (group + 1) * per_group].reshape(WIDTH, LANES)
        moved = tn(perm[...], block)
        for image in range(sizes.images):
            tok[image, group * piece : (group + 1) * piece, :] = moved[
                image * piece : (image + 1) * piece
            ].astype(bf16)
    sent(one)
    sent(two)
    sent(act)
def tail_kernel(
    sizes,
    lens,
    gtok,
    gh,
    gqkv,
    gp,
    gu,
    gdt,
    gvec,
    gub,
    vec,
    order_big,
    order_small,
    perm,
    step,
    sh,
    sqkv,
    sp,
    su,
    sd,
    tbig_hbm,
    tsmall_hbm,
    wbig_hbm,
    wsmall_hbm,
    binput_hbm,
    bmodel_hbm,
    bqkv_hbm,
    bhidden_hbm,
    dact_big,
    dact_small,
    dcls_big,
    dcls_small,
    update,
    states,
    vtotal,
    scalars,
    table_big,
    table_small,
    wins_big,
    wins_small,
    binput,
    bmodel,
    bqkv,
    bhidden,
    load_sem,
    outgoing,
    returned,
    grads,
    mixed_big,
    mixed_small,
    taps,
    stage_two,
    stage_head,
    rs_send,
    rs_got,
    rsh_send,
    rsh_got,
    stage_one,
    t_send,
    t_got,
    vpart,
    v_wide,
    v_dp,
    s_wide,
    mpack,
    dirs_got,
    row_head,
    row_qkv,
    row_proj,
    row_up,
    row_down,
    y_got,
    *sems,
):
    bf16, f32 = jnp.bfloat16, jnp.float32
    me_w, me_d = lax.axis_index("wide"), lax.axis_index("dp")
    n_w, n_d = sizes.wide, sizes.dp
    br, bh, bc = sizes.br, sizes.bh, sizes.bc
    sems = iter(sems)

    def scatter(axis, src_of, dst):
        count, me = (n_w, me_w) if axis == "wide" else (n_d, me_d)
        return spread(axis, count, me, src_of, dst, next(sems), next(sems))

    loads = []
    for at, (src, dst) in enumerate(
        (
            (bmodel_hbm, bmodel),
            (bhidden_hbm, bhidden),
            (binput_hbm, binput),
            (wbig_hbm, wins_big),
            (wsmall_hbm, wins_small),
            (tbig_hbm, table_big),
            (tsmall_hbm, table_small),
            (bqkv_hbm, bqkv),
        )
    ):
        copy = pltpu.make_async_copy(src, dst, load_sem.at[at])
        copy.start()
        loads.append(copy)
    greet((("wide", n_w, me_w), ("dp", n_d, me_d)))

    groups = n_w * sizes.piece_rows // WIDTH
    per_group = n_w // groups
    piece = WIDTH // sizes.images
    for group in range(groups):
        block = jnp.concatenate(
            [
                gtok[image, group * piece : (group + 1) * piece, :].astype(f32)
                for image in range(sizes.images)
            ],
            0,
        )
        moved = nn(perm[...], block.astype(bf16)).astype(bf16)
        outgoing[group * per_group : (group + 1) * per_group] = moved.reshape(
            per_group, sizes.piece_rows, LANES
        )
    back = scatter("wide", lambda peer: outgoing.at[peer], returned.at[me_w])
    returned[me_w] = outgoing[me_w]

    for load in loads[0:3]:
        load.wait()
    even = (
        lax.broadcasted_iota(jnp.int32, (WIDTH // 2, WIDTH), 1)
        == 2 * lax.broadcasted_iota(jnp.int32, (WIDTH // 2, WIDTH), 0)
    ).astype(bf16)
    u_head = tn(binput[...].astype(bf16), nn(even, gh[...].astype(bf16)).astype(bf16))
    left = bmodel[1].astype(bf16)
    u_qkv = [tn(left, gqkv[part].astype(bf16)) for part in range(3)]
    u_proj = tn(bmodel[2].astype(bf16), gp[...].astype(bf16))
    u_up = tn(bmodel[4].astype(bf16), gu[...].astype(bf16))
    u_down = jnp.transpose(nn(gdt[...].astype(bf16), bhidden[1].astype(bf16)))
    stage_two[...] = jnp.zeros_like(stage_two)
    stage_head[...] = jnp.zeros_like(stage_head)
    for w in range(n_w):
        at = w * br
        stage_two[0:br, 0 : 4 * WIDTH] = u_up[at : at + br]
        for part in range(2):
            stage_two[0:br, (4 + part) * WIDTH : (5 + part) * WIDTH] = u_qkv[part][at : at + br]
        stage_two[br : 2 * br, 0:WIDTH] = u_qkv[2][at : at + br]
        stage_two[br : 2 * br, WIDTH : 2 * WIDTH] = u_proj[at : at + br]
        for j in range(4):
            stage_two[br : 2 * br, (2 + j) * WIDTH : (3 + j) * WIDTH] = u_down[
                4 * at + j * br : 4 * at + (j + 1) * br
            ]
        stage_head[0:bh] = u_head[w * bh : (w + 1) * bh]
        rs_send[w] = stage_two[...].astype(bf16)
        rsh_send[w] = stage_head[...].astype(bf16)
    first = scatter("wide", lambda peer: rs_send.at[peer], rs_got.at[me_w])
    first += scatter("wide", lambda peer: rsh_send.at[peer], rsh_got.at[me_w])
    rs_got[me_w] = rs_send[me_w]
    rsh_got[me_w] = rsh_send[me_w]

    mpack[...] = jnp.zeros_like(mpack)
    for half in range(2):
        sizes.pack_blocks(
            mpack.at[half],
            (sh[:, half, :], sqkv[half], sp[half], su[half], jnp.transpose(sd[half])),
        )

    put_big, put_small = placements(order_big, order_small, sizes)
    n_big, n_small = sizes.slots, sizes.small_slots
    token_big, token_small = token_lanes(lens)
    lane = lax.broadcasted_iota(jnp.int32, (1, 128), 1)
    for load in loads[3:5]:
        load.wait()
    arrived(back)
    for w in range(n_w):
        block = returned[w].astype(f32)
        for e in range(2):
            for c in range(sizes.channels):
                at = (e * sizes.channels + c) * sizes.images
                to = (c * n_w + w) * sizes.images
                grads[e, to : to + sizes.images] = block[at : at + sizes.images]

    def fold(big, small):
        value = jnp.sum(big.reshape(n_big // 8, 8, LANES), 0)
        return value[:, 0:128] + value[:, 128:256] + jnp.sum(small.reshape(n_small // 8, 8, 128), 0)

    heads_big = jnp.zeros((n_big, 128), f32)
    heads_small = jnp.zeros((n_small, 128), f32)
    for c in range(sizes.channels):
        own_big, own_small = slice(c * n_big, (c + 1) * n_big), slice(c * n_small, (c + 1) * n_small)
        group = slice(c * 8, (c + 1) * 8)
        pair = []
        for e in range(2):
            block = grads[e, own_big].astype(bf16)
            pair.append((nn(put_big, block), nn(put_small, block[:, 128:256])))
            taps[9, e, group] = fold(
                jnp.where(token_big, pair[e][0], 0.0), jnp.where(token_small, pair[e][1], 0.0)
            )
        heads_big = jnp.where(lane == c, pair[0][0][:, 0:1], heads_big)
        heads_small = jnp.where(
            lane == c, pair[0][1][:, SPLIT - 128 : SPLIT - 127], heads_small
        )
        for tap in range(9):
            big, small = wins_big[tap, own_big].astype(f32), wins_small[tap, own_small].astype(f32)
            for e in range(2):
                taps[tap, e, group] = fold(pair[e][0] * big, pair[e][1] * small)
            one, two = (vec[tap, 2 * (me_w * sizes.channels + c) + e] for e in range(2))
            mixed_big[own_big, tap * LANES : (tap + 1) * LANES] = (
                one * pair[0][0] + two * pair[1][0]
            ).astype(bf16)
            mixed_small[own_small, tap * 128 : (tap + 1) * 128] = (
                one * pair[0][1] + two * pair[1][1]
            ).astype(bf16)
    dcls_big[...] = heads_big
    dcls_small[...] = heads_small
    for load in loads[5:7]:
        load.wait()

    @pl.loop(0, sizes.rows // 256)
    def _(chunk):
        at = pl.ds(pl.multiple_of(chunk * 256, 256), 256)
        dact_big[at, :] = nn(mixed_big[at, :], table_big[...])

    dact_small[...] = nn(mixed_small[...], table_small[...])

    vpart[...] = jnp.zeros_like(vpart)
    half_rows = sizes.channels * 8
    own_channel = lax.broadcasted_iota(jnp.int32, (half_rows, WIDTH), 0) // 8
    own_lane = lax.broadcasted_iota(jnp.int32, (half_rows, WIDTH), 1)
    conv = jnp.zeros((128, WIDTH), f32)
    for e in range(2):
        place = (own_lane == 2 * (me_w * sizes.channels + own_channel) + e).astype(f32)
        part = jnp.zeros((half_rows, 128), f32)
        for tap in range(10):
            part = jnp.where(lane == tap, jnp.sum(taps[tap, e], -1, keepdims=True), part)
        conv += lax.dot_general(
            part,
            place,
            (((0,), (0,)), ((), ())),
            precision=lax.Precision.HIGHEST,
            preferred_element_type=f32,
        )
    vpart[0:10] = conv[0:10]
    vpart[10:19] = gvec[0:9]
    for j in range(4):
        vpart[19 + j : 20 + j] = gub[:, j * WIDTH : (j + 1) * WIDTH]
    v_wide[me_w] = vpart[...]
    vec_one = scatter("wide", lambda peer: v_wide.at[me_w], v_wide.at[me_w])

    loads[7].wait()
    arrived(first)
    rows_two = rs_got[0].astype(f32)
    rows_head = rsh_got[0].astype(f32)
    for w in range(1, n_w):
        rows_two += rs_got[w].astype(f32)
        rows_head += rsh_got[w].astype(f32)
    rows_two = rows_two.astype(bf16)
    right = bqkv[...].astype(bf16)
    t_up = nn(rows_two[0:br, 0 : 4 * WIDTH], bhidden[0].astype(bf16))
    t_qkv = nn(rows_two[0:br, 4 * WIDTH : 6 * WIDTH], right[0 : 2 * WIDTH]) + nn(
        rows_two[br : 2 * br, 0:WIDTH], right[2 * WIDTH :]
    )
    t_proj = nn(rows_two[br : 2 * br, WIDTH : 2 * WIDTH], bmodel[3].astype(bf16))
    right = bmodel[5].astype(bf16)
    t_down = [
        nn(rows_two[br : 2 * br, (2 + j) * WIDTH : (3 + j) * WIDTH], right) for j in range(4)
    ]
    t_head = nn(rows_head.astype(bf16), bmodel[0].astype(bf16))
    stage_one[...] = jnp.zeros_like(stage_one)
    for d in range(n_d):
        own = slice(d * bc, (d + 1) * bc)
        sizes.pack_blocks(
            stage_one,
            (
                t_head[0:bh, own],
                t_qkv[:, 3 * d * bc : 3 * (d + 1) * bc],
                t_proj[:, own],
                t_up[:, 4 * d * bc : 4 * (d + 1) * bc],
                jnp.concatenate([t[:, own] for t in t_down], 0),
            ),
        )
        t_send[d] = stage_one[...].astype(bf16)
    second = scatter("dp", lambda peer: t_send.at[peer], t_got.at[me_d])
    t_got[me_d] = t_send[me_d]

    arrived(vec_one)
    vsum = v_wide[0]
    for w in range(1, n_w):
        vsum += v_wide[w]
    arrived(second)
    turned = t_got[0].astype(f32)
    for d in range(1, n_d):
        turned += t_got[d].astype(f32)
    own_square = jnp.sum(jnp.sum(turned * turned, -1, keepdims=True), 0, keepdims=True)
    last_row = lax.broadcasted_iota(jnp.int32, vsum.shape, 0) == vsum.shape[0] - 1
    v_dp[me_d] = jnp.where(last_row, own_square, vsum)
    vec_two = scatter("dp", lambda peer: v_dp.at[me_d], v_dp.at[me_d])
    arrived(vec_two)
    vsum = v_dp[0]
    for d in range(1, n_d):
        vsum += v_dp[d]
    s_wide[me_w] = jnp.broadcast_to(vsum[23:24, 0:128], (8, 128))
    third = scatter("wide", lambda peer: s_wide.at[me_w], s_wide.at[me_w])
    vsum = jnp.where(last_row, 0.0, vsum)
    vtotal[...] = vsum
    vec_square = jnp.sum(jnp.sum(vsum * vsum, -1, keepdims=True), 0, keepdims=True)
    count = jnp.full((8, 128), step[0], jnp.int32).astype(f32)[0:1, 0:1]
    fix_one = 1.0 - jnp.exp(count * float(np.log(beta_one)))
    fix_two = 1.0 - jnp.exp(count * float(np.log(beta_two)))
    arrived(third)
    square = s_wide[0][0:1, 0:1]
    for w in range(1, n_w):
        square += s_wide[w][0:1, 0:1]
    norm = jnp.sqrt(square + vec_square)
    factor = jnp.minimum(1.0, clip_limit / (norm + 1e-06))
    which = lax.broadcasted_iota(jnp.int32, (8, 128), 1)
    scalars[...] = jnp.where(
        which == 0,
        norm,
        jnp.where(which == 1, factor, jnp.where(which == 2, fix_one, fix_two)),
    )

    turned = turned * factor
    moment = beta_one * mpack[0] + (1.0 - beta_one) * turned
    second_moment = beta_two * mpack[1] * mpack[1] + (1.0 - beta_two) * turned * turned
    states[0] = moment
    states[1] = jnp.sqrt(second_moment)
    direction = moment / fix_one / (jnp.sqrt(second_moment / fix_two) + adam_eps)
    dirs_got[me_d] = direction.astype(bf16)
    fourth = scatter("dp", lambda peer: dirs_got.at[me_d], dirs_got.at[me_d])
    arrived(fourth)
    for d in range(n_d):
        head, qkv, proj, up, down = sizes.unpack_blocks(dirs_got[d].astype(f32))
        row_head[0:bh, d * bc : (d + 1) * bc] = head
        row_qkv[:, 3 * d * bc : 3 * (d + 1) * bc] = qkv
        row_proj[:, d * bc : (d + 1) * bc] = proj
        row_up[:, 4 * d * bc : 4 * (d + 1) * bc] = up
        row_down[:, d * bc : (d + 1) * bc] = down

    def right_rows(ref, size):
        return ref[pl.ds(pl.multiple_of(me_d * size, 8), size), :].astype(bf16)

    stage_one[...] = jnp.zeros_like(stage_one)
    sizes.pack_blocks(
        stage_one,
        (
            nt(row_head[...].astype(bf16), right_rows(bmodel.at[0], bc))[0:bh],
            nt(row_qkv[...].astype(bf16), right_rows(bqkv, 3 * bc)),
            nt(row_proj[...].astype(bf16), right_rows(bmodel.at[3], bc)),
            nt(row_up[...].astype(bf16), right_rows(bhidden.at[0], 4 * bc)),
            nt(row_down[...].astype(bf16), right_rows(bmodel.at[5], bc)),
        ),
    )
    y_got[me_w] = stage_one[...].astype(bf16)
    fifth = scatter("wide", lambda peer: y_got.at[me_w], y_got.at[me_w])
    def left_rows(ref, size):
        if size % 8 == 0:
            return ref[pl.ds(pl.multiple_of(me_w * size, 8), size), :].astype(bf16)
        own = lax.broadcasted_iota(jnp.int32, (size, ref.shape[0]), 0) + me_w * size
        pick = own == lax.broadcasted_iota(jnp.int32, (size, ref.shape[0]), 1)
        return nn(pick.astype(bf16), ref[...].astype(bf16)).astype(bf16)

    lefts = (
        left_rows(binput, bh),
        left_rows(bmodel.at[1], br),
        left_rows(bmodel.at[2], br),
        left_rows(bmodel.at[4], br),
        left_rows(bhidden.at[1], 4 * br),
    )
    arrived(fifth)
    parts = [sizes.unpack_blocks(y_got[w].astype(f32)) for w in range(n_w)]
    update[...] = jnp.zeros_like(update)
    sizes.pack_blocks(
        update,
        [
            nn(
                lefts[member],
                jnp.concatenate([part[member] for part in parts], 0).astype(bf16),
            )
            for member in range(5)
        ],
    )
    for copies in (back, first, vec_one, second, vec_two, third, fourth, fifth):
        sent(copies)


def finish_kernel(
    sizes,
    mh,
    mqkv,
    mp,
    mu,
    md,
    vec,
    vmom,
    heads_big,
    heads_small,
    update,
    states,
    vtotal,
    scalars,
    dcls_big,
    dcls_small,
    norm,
    nvec,
    nvmom,
    *outs,
):
    norm[0] = scalars[0, 0]
    factor, fix_one, fix_two = (scalars[0, j] for j in (1, 2, 3))
    dcls_big[...] = jnp.transpose(heads_big[...])[0 : sizes.channels]
    dcls_small[...] = jnp.transpose(heads_small[...])[0 : sizes.channels]
    updates = sizes.unpack_blocks(update[...])
    firsts = sizes.unpack_blocks(states[0])
    seconds = sizes.unpack_blocks(states[1])
    for member, master in enumerate((mh, mqkv, mp, mu, md)):
        change, first, second = updates[member], firsts[member], seconds[member]
        if member == 4:
            change, first, second = (jnp.transpose(v) for v in (change, first, second))
        fresh = master[...] - rate_matrix * change
        outs[member][...] = fresh
        if member == 0:
            outs[5][:, 0, :] = first
            outs[5][:, 1, :] = second
        else:
            outs[5 + member][0] = first
            outs[5 + member][1] = second
        outs[10 + member][...] = fresh.astype(jnp.bfloat16)
    scaled = vtotal[0:23] * factor
    first = beta_one * vmom[:, 0, :] + (1.0 - beta_one) * scaled
    second = beta_two * vmom[:, 1, :] * vmom[:, 1, :] + (1.0 - beta_two) * scaled * scaled
    direction = first / fix_one / (jnp.sqrt(second / fix_two) + adam_eps)
    nvec[...] = vec[...] * (1.0 - rate_vector * decay_rate) - rate_vector * direction
    nvmom[:, 0, :] = first
    nvmom[:, 1, :] = jnp.sqrt(second)


VM = pl.BlockSpec(memory_space=pltpu.VMEM)
SM = pl.BlockSpec(memory_space=pltpu.SMEM)
HB = pl.BlockSpec(memory_space=pl.ANY)
LIMIT = 60 * 1024 * 1024


def dma_sems(*counts):
    return [pltpu.SemaphoreType.DMA((n,)) for n in counts]


def run_front(sizes, lens, acts, orders, vec, tables, perm, masters):
    bf16, f32 = jnp.bfloat16, jnp.float32
    w, d = sizes.wide, sizes.dp
    outs = [
        ((sizes.images, WIDTH, LANES), bf16),
        ((9, sizes.rows, LANES), bf16),
        ((9, sizes.small_rows, 128), bf16),
        ((WIDTH, WIDTH), bf16),
        ((3, WIDTH, WIDTH), bf16),
        ((WIDTH, WIDTH), bf16),
        ((WIDTH, 4 * WIDTH), bf16),
        ((4 * WIDTH, WIDTH), bf16),
    ]
    return pl.pallas_call(
        partial(front_kernel, sizes, lens),
        in_specs=[VM] * 6 + [SM] + [VM] * 8,
        out_specs=[VM] * len(outs),
        out_shape=[jax.ShapeDtypeStruct(s, t) for s, t in outs],
        scratch_shapes=[
            pltpu.VMEM((sizes.pair_rows, sizes.block_lanes), f32),
            pltpu.VMEM((sizes.pair_rows, 6 * WIDTH), f32),
            pltpu.VMEM((sizes.head_rows, WIDTH), f32),
            pltpu.VMEM((d, sizes.pair_rows, sizes.block_lanes), bf16),
            pltpu.VMEM((w, sizes.pair_rows, 6 * WIDTH), bf16),
            pltpu.VMEM((w, sizes.head_rows, WIDTH), bf16),
            pltpu.VMEM((w, sizes.piece_rows, LANES), bf16),
            pltpu.VMEM((w, sizes.piece_rows, LANES), bf16),
            pltpu.VMEM((2, sizes.rows, LANES), f32),
            pltpu.VMEM((2, sizes.small_rows, 128), f32),
        ]
        + dma_sems(d - 1, d - 1, w - 1, w - 1, w - 1, w - 1, w - 1, w - 1),
        compiler_params=pltpu.CompilerParams(
            collective_id=0, has_side_effects=True, vmem_limit_bytes=LIMIT
        ),
        name="front",
    )(*acts, *orders, vec, *tables, perm, *masters)


def run_tail(sizes, lens, grads, vec, orders, perm, step, moments, tables, wins, bases):
    bf16, f32 = jnp.bfloat16, jnp.float32
    w, d = sizes.wide, sizes.dp
    pack = (sizes.pair_rows, sizes.block_lanes)
    outs = [
        ((sizes.rows, tables[0].shape[1]), f32),
        ((sizes.small_rows, tables[1].shape[1]), f32),
        ((sizes.slots, 128), f32),
        ((sizes.small_slots, 128), f32),
        (pack, f32),
        ((2,) + pack, f32),
        ((24, WIDTH), f32),
        ((8, 128), f32),
    ]
    two = (sizes.pair_rows, 6 * WIDTH)
    head = (sizes.head_rows, WIDTH)
    piece = (w, sizes.piece_rows, LANES)
    return pl.pallas_call(
        partial(tail_kernel, sizes, lens),
        in_specs=[VM] * 8 + [SM] + [VM] * 3 + [SM] + [VM] * 5 + [HB] * 8,
        out_specs=[VM] * len(outs),
        out_shape=[jax.ShapeDtypeStruct(s, t) for s, t in outs],
        scratch_shapes=[pltpu.VMEM(a.shape, a.dtype) for a in (*tables, *wins, *bases)]
        + dma_sems(8)
        + [
            pltpu.VMEM(piece, bf16),
            pltpu.VMEM(piece, bf16),
            pltpu.VMEM((2, sizes.rows, LANES), f32),
            pltpu.VMEM((sizes.rows, 9 * LANES), bf16),
            pltpu.VMEM((sizes.small_rows, 9 * 128), bf16),
            pltpu.VMEM((10, 2, sizes.channels * 8, 128), f32),
            pltpu.VMEM(two, f32),
            pltpu.VMEM(head, f32),
            pltpu.VMEM((w,) + two, bf16),
            pltpu.VMEM((w,) + two, bf16),
            pltpu.VMEM((w,) + head, bf16),
            pltpu.VMEM((w,) + head, bf16),
            pltpu.VMEM(pack, f32),
            pltpu.VMEM((d,) + pack, bf16),
            pltpu.VMEM((d,) + pack, bf16),
            pltpu.VMEM((24, WIDTH), f32),
            pltpu.VMEM((w, 24, WIDTH), f32),
            pltpu.VMEM((d, 24, WIDTH), f32),
            pltpu.VMEM((w, 8, 128), f32),
            pltpu.VMEM((2,) + pack, f32),
            pltpu.VMEM((d,) + pack, bf16),
            pltpu.VMEM((sizes.bh, WIDTH), f32),
            pltpu.VMEM((sizes.br, 3 * WIDTH), f32),
            pltpu.VMEM((sizes.br, WIDTH), f32),
            pltpu.VMEM((sizes.br, 4 * WIDTH), f32),
            pltpu.VMEM((4 * sizes.br, WIDTH), f32),
            pltpu.VMEM((w,) + pack, bf16),
        ]
        + dma_sems(
            *(n - 1 for n in (w, w, w, w, w, w, w, w, d, d, d, d, w, w, d, d, w, w))
        ),
        compiler_params=pltpu.CompilerParams(
            collective_id=1, has_side_effects=True, vmem_limit_bytes=LIMIT
        ),
        name="tail",
    )(*grads, vec, *orders, perm, step, *moments, *tables, *wins, *bases)


def run_finish(sizes, masters, vec, vmom, moments, heads, packs):
    f32, bf16 = jnp.float32, jnp.bfloat16
    shapes = [m.shape for m in masters]
    outs = [((sizes.channels, h.shape[0]), f32) for h in heads]
    outs += [((1,), f32), (vec.shape, f32), (vmom.shape, f32)]
    outs += [(s, f32) for s in shapes] + [(m.shape, f32) for m in moments]
    outs += [(s, bf16) for s in shapes]
    return pl.pallas_call(
        partial(finish_kernel, sizes),
        in_specs=[VM] * 12 + [SM],
        out_specs=[VM, VM, SM] + [VM] * (len(outs) - 3),
        out_shape=[jax.ShapeDtypeStruct(s, t) for s, t in outs],
        name="finish",
    )(*masters, vec, vmom, *heads, *packs)


def pool_table(grid, side, lane, lanes):
    table = np.zeros((9, lanes, grid * grid), np.float32)
    for tap in range(9):
        for y in range(side):
            for x in range(side):
                sy, sx = 2 * y + tap // 3 - 1, 2 * x + tap % 3 - 1
                if 0 <= sy < grid and 0 <= sx < grid:
                    table[tap, lane + y * side + x, sy * grid + sx] = 1.0
    return jnp.asarray(table, jnp.bfloat16)


def per_device(
    wide_n,
    dp_n,
    big_act,
    big_cls,
    small_act,
    small_cls,
    big_order,
    small_order,
    big_cot,
    small_cot,
    vec_params,
    vec_moments,
    *rest,
):
    masters, moments, bases, step = list(rest[0:5]), list(rest[5:10]), rest[10:14], rest[14]
    channels = big_act.shape[1]
    images, small_images = big_cot.shape[0], small_cot.shape[0]
    lens = (big_cot.shape[1], small_cot.shape[1])
    sizes = Sizes(wide_n, dp_n, channels, images, small_images)
    side = lambda cells: round(cells**0.5)
    tables = (
        pool_table(side(big_act.shape[2]), side(lens[0] - 1), 1, LANES),
        pool_table(side(small_act.shape[2]), side(lens[1] - 1), SPLIT + 1 - 128, 128),
    )
    perm = row_permutation(channels, images)
    flip = lambda a, i, j: jnp.swapaxes(a, i, j)
    acts = [flip(a, 0, 1) for a in (big_act, small_act, big_cls, small_cls)]
    orders = (big_order, small_order)
    masters[4] = flip(masters[4], 0, 1)
    moments[0], moments[4] = flip(moments[0], 0, 1), flip(moments[4], 1, 2)
    vec_moments = flip(vec_moments, 0, 1)

    tok, wins_big, wins_small, wh, wqkv, wp, wu, wd = run_front(
        sizes, lens, acts, orders, vec_params, tables, perm, masters
    )
    block = run_block(tok, flip(big_cot, 1, 2), small_cot, vec_params, wh, wqkv, wp, wu, wd)
    flat = tuple(t.reshape(-1, t.shape[2]) for t in tables)
    dact_big, dact_small, *packs = run_tail(
        sizes,
        lens,
        block[2:],
        vec_params,
        orders,
        perm,
        step,
        moments,
        flat,
        (wins_big, wins_small),
        bases,
    )
    results = list(
        run_finish(sizes, masters, vec_params, vec_moments, moments, packs[0:2], packs[2:])
    )
    cls_big, cls_small, norm, new_vec, new_vec_moments = results[0:5]
    masters, moments, copies = results[5:10], results[10:15], results[15:20]
    masters[4], copies[4] = flip(masters[4], 0, 1), flip(copies[4], 0, 1)
    moments[0], moments[4] = flip(moments[0], 0, 1), flip(moments[4], 1, 2)
    return (
        flip(block[0], 1, 2),
        block[1],
        flip(dact_big.reshape(channels, sizes.slots, -1), 0, 1),
        flip(cls_big, 0, 1),
        flip(dact_small.reshape(channels, sizes.small_slots, -1), 0, 1),
        flip(cls_small, 0, 1),
        norm,
        new_vec,
        flip(new_vec_moments, 0, 1),
        *masters,
        *moments,
        *copies,
    )


def solution(mesh):
    split, wide_first, free = P("dp", "wide", None), P("wide", "dp"), P()
    moment = P(None, "wide", "dp")
    both = P(("dp", "wide"), None, None)
    acts = (split, P("dp", "wide"), split, P("dp", "wide"))
    in_specs = (
        acts
        + (P("dp", None), P("dp", None), both, both, free, free)
        + (wide_first,) * 5
        + (moment,) * 5
        + (free,) * 5
    )
    out_specs = (
        (both, both) + acts + (free,) * 3 + (wide_first,) * 5 + (moment,) * 5 + (wide_first,) * 5
    )
    return jax.shard_map(
        partial(per_device, mesh.shape["wide"], mesh.shape["dp"]),
        mesh=mesh,
        in_specs=in_specs,
        out_specs=out_specs,
        check_vma=False,
    )
```

```python
from functools import partial

import jax
import jax.numpy as jnp
import numpy as np
from jax import lax
from jax.experimental import pallas as pl
from jax.experimental.pallas import tpu as pltpu
from jax.sharding import PartitionSpec as P

HEADS = 4
HD = 48
beta_one = 0.9
beta_two = 0.999
adam_eps = 1e-08
norm_eps = 1e-06
rate_matrix = 0.08
rate_vector = 0.25
decay_rate = 0.05
clip_limit = 1.0
LANES = 256
SPLIT = 208
SCORE_SCALE = float(HD ** (-0.5) * np.log2(np.e))


def nt(a, b):
    return lax.dot_general(a, b, (((1,), (1,)), ((), ())), preferred_element_type=jnp.float32)


def tn(a, b):
    return lax.dot_general(a, b, (((0,), (0,)), ((), ())), preferred_element_type=jnp.float32)


def nn(a, b):
    return jnp.dot(a, b, preferred_element_type=jnp.float32)


def colsum(v):
    return jnp.sum(v, 0, keepdims=True)


def norm_forward(rows, gain, shift):
    centered = rows - jnp.mean(rows, -1, keepdims=True)
    scale = lax.rsqrt(jnp.mean(centered * centered, -1, keepdims=True) + norm_eps)
    hat = centered * scale
    return hat, scale, (hat * gain + shift).astype(jnp.bfloat16)


def norm_backward(grad, hat, scale, gain):
    inner = grad * gain
    mean_a = jnp.mean(inner, -1, keepdims=True)
    mean_b = jnp.mean(inner * hat, -1, keepdims=True)
    return scale * (inner - mean_a - hat * mean_b)


def block_start(big_len, small_len, vec, sums, bias, cot, ubias):
    for ref in sums:
        ref[...] = jnp.zeros_like(ref)
    cot[...] = jnp.zeros_like(cot)
    width = vec.shape[1]
    for j in range(4):
        ubias[:, j * width : (j + 1) * width] = vec[19 + j : 20 + j]
    key_id = lax.broadcasted_iota(jnp.int32, (LANES, LANES), 1)
    query_id = lax.broadcasted_iota(jnp.int32, (LANES, LANES), 0)
    keep_big = (query_id < SPLIT) & (key_id < big_len)
    keep_small = (query_id >= SPLIT) & (key_id >= SPLIT) & (key_id < SPLIT + small_len)
    bias[...] = jnp.where(keep_big | keep_small, 0.0, -1e30)


def block_step(image, raw, counts, bcot, scot, vec, weights, bout, sout, sums, scratch):
    pair, small_n, big_len, small_len = counts
    wh, wqkv, wp, wu, wd = weights
    gh, gqkv, gp, gu, gdt, gvec, gub = sums
    probs, bias, cot, ubias = scratch
    width = vec.shape[1]
    row_id = lax.broadcasted_iota(jnp.int32, (pair * LANES, 1), 0) % LANES
    lane_id = lax.broadcasted_iota(jnp.int32, (1, width), 1)
    for j in range(pair):
        base = j * LANES
        turned = jnp.transpose(bcot[image + j].astype(jnp.float32))
        cot[base : base + big_len] = turned.astype(jnp.bfloat16)
        small = scot[jnp.minimum(image + j, small_n - 1)].astype(jnp.float32)
        small = jnp.where(image + j < small_n, small, 0.0).astype(jnp.bfloat16)
        cot[base + SPLIT : base + SPLIT + small_len] = small
    raw_low = raw.astype(jnp.bfloat16)
    is_head = (row_id == 0) | (row_id == SPLIT)
    rows = jnp.where(is_head, nn(raw_low, wh[...]) + vec[10:11], raw)
    hat_one, scale_one, normed_one = norm_forward(rows, vec[11:12], vec[12:13])
    queries = (nn(normed_one, wqkv[0]) + vec[13:14]).astype(jnp.bfloat16)
    keys_in = nn(normed_one, wqkv[1]).astype(jnp.bfloat16)
    values = (nn(normed_one, wqkv[2]) + vec[14:15]).astype(jnp.bfloat16)
    zero = jnp.zeros((), jnp.bfloat16)
    in_head = [(lane_id >= h * HD) & (lane_id < (h + 1) * HD) for h in range(HEADS)]
    tiles = [slice(j * LANES, (j + 1) * LANES) for j in range(pair)]
    chains = [(j, h) for h in range(HEADS) for j in range(pair)]
    scores = {
        (j, h): nt(jnp.where(in_head[h], queries[tiles[j]], zero), keys_in[tiles[j]])
        for j, h in chains
    }
    low = {}
    for j, h in chains:
        value = scores[j, h] + bias[...]
        weights = jnp.exp2((value - jnp.max(value, -1, keepdims=True)) * SCORE_SCALE)
        probas = weights * (1.0 / jnp.sum(weights, -1, keepdims=True))
        probs[j, h] = probas
        low[j, h] = probas.astype(jnp.bfloat16)
    mixture = [
        nn(
            jnp.concatenate([low[j, h] for h in range(HEADS)], 1),
            jnp.concatenate([jnp.where(in_head[h], values[tiles[j]], zero) for h in range(HEADS)], 0),
        )
        for j in range(pair)
    ]
    mixture = jnp.concatenate(mixture, 0)
    mixture = mixture.astype(jnp.bfloat16)
    middle = rows + nn(mixture, wp[...]) + vec[15:16]
    hat_two, scale_two, normed_two = norm_forward(middle, vec[16:17], vec[17:18])
    pre = nn(normed_two, wu[...]) + ubias[...]
    cdf = 0.5 + 0.5 * lax.erf(pre * 0.7071067811865476)
    slope = cdf + pre * jnp.exp(pre * pre * -0.5) * 0.3989422804014327
    active = (pre * cdf).astype(jnp.bfloat16)
    result = middle + nn(active, wd[...]) + vec[18:19]
    for j in range(pair):
        bout[image + j] = jnp.transpose(result[tiles[j]])[:, :big_len]
        base = j * LANES + SPLIT
        sout[image + j] = result[base : base + small_len]
    cot_low = cot[...]
    cot_rows = cot_low.astype(jnp.float32)
    gdt[...] += tn(cot_low, active)
    gvec[8:9] += colsum(cot_rows)
    grad_pre = (nt(cot_low, wd[...]) * slope).astype(jnp.bfloat16)
    gu[...] += tn(normed_two, grad_pre)
    gub[...] += colsum(grad_pre.astype(jnp.float32))
    grad_two = nt(grad_pre, wu[...])
    gvec[6:7] += colsum(grad_two * hat_two)
    gvec[7:8] += colsum(grad_two)
    grad_mid = norm_backward(grad_two, hat_two, scale_two, vec[16:17]) + cot_rows
    branch = grad_mid.astype(jnp.bfloat16)
    gp[...] += tn(mixture, branch)
    gvec[5:6] += colsum(branch.astype(jnp.float32))
    grad_mix = nt(branch, wp[...]).astype(jnp.bfloat16)
    own = {(j, h): jnp.where(in_head[h], grad_mix[tiles[j]], zero) for j, h in chains}
    grad_probs = {(j, h): nt(own[j, h], values[tiles[j]]) for j, h in chains}
    grad_scores = {}
    for j, h in chains:
        probas = probs[j, h]
        inner = jnp.sum(probas * grad_probs[j, h], -1, keepdims=True)
        grad_scores[j, h] = (probas * (grad_probs[j, h] - inner)).astype(jnp.bfloat16)
    stack = lambda source: [
        jnp.concatenate([jnp.where(in_head[h], source[tile], zero) for h in range(HEADS)], 0)
        for tile in tiles
    ]
    wide_keys, wide_queries = stack(keys_in), stack(queries)
    all_scores = [jnp.concatenate([grad_scores[j, h] for h in range(HEADS)], 1) for j in range(pair)]
    tall_scores = [jnp.concatenate([grad_scores[j, h] for h in range(HEADS)], 0) for j in range(pair)]
    tall_probs = [
        jnp.concatenate([probs[j, h].astype(jnp.bfloat16) for h in range(HEADS)], 0)
        for j in range(pair)
    ]
    tall_own = [jnp.concatenate([own[j, h] for h in range(HEADS)], 0) for j in range(pair)]
    grad_q = jnp.concatenate([nn(all_scores[j], wide_keys[j]) for j in range(pair)], 0)
    grad_k = jnp.concatenate([tn(tall_scores[j], wide_queries[j]) for j in range(pair)], 0)
    grad_v = jnp.concatenate([tn(tall_probs[j], tall_own[j]) for j in range(pair)], 0)
    grad_q = (grad_q * HD ** (-0.5)).astype(jnp.bfloat16)
    grad_k = (grad_k * HD ** (-0.5)).astype(jnp.bfloat16)
    grad_v = grad_v.astype(jnp.bfloat16)
    gqkv[0] += tn(normed_one, grad_q)
    gqkv[1] += tn(normed_one, grad_k)
    gqkv[2] += tn(normed_one, grad_v)
    gvec[3:4] += colsum(grad_q.astype(jnp.float32))
    gvec[4:5] += colsum(grad_v.astype(jnp.float32))
    grad_one = nt(grad_q, wqkv[0]) + nt(grad_k, wqkv[1]) + nt(grad_v, wqkv[2])
    gvec[1:2] += colsum(grad_one * hat_one)
    gvec[2:3] += colsum(grad_one)
    grad_tok = norm_backward(grad_one, hat_one, scale_one, vec[11:12]) + grad_mid
    grad_head = jnp.where(is_head, grad_tok, 0.0).astype(jnp.bfloat16)
    gh[...] += tn(raw_low, grad_head)
    gvec[0:1] += colsum(grad_head.astype(jnp.float32))
    return jnp.where(is_head, nt(grad_head, wh[...]), grad_tok)


def row_permutation(channels, images):
    width = 192
    group = width // (2 * channels * images)
    table = np.zeros((width, width), np.float32)
    for s in range(group):
        for e in range(2):
            for c in range(channels):
                for i in range(images):
                    row = ((s * 2 + e) * channels + c) * images + i
                    table[row, i * (width // images) + s * 2 * channels + 2 * c + e] = 1.0
    return jnp.asarray(table, jnp.bfloat16)
MESH = pl.DeviceIdType.MESH
WIDTH = 192
PAIR = 2


def up_to(value, unit):
    return -(-value // unit) * unit


def links(axis, count, me, src_of, dst, send, recv, base=0):
    copies = []
    for k in range(1, count):
        peer = lax.rem(me + k, count)
        copies.append(
            pltpu.make_async_remote_copy(
                src_ref=src_of(peer),
                dst_ref=dst,
                send_sem=send.at[base + k - 1],
                recv_sem=recv.at[base + k - 1],
                device_id={axis: peer},
                device_id_type=MESH,
            )
        )
    return copies


def begin(copies):
    for copy in copies:
        copy.start()
    return copies


def arrived(copies):
    for copy in copies:
        copy.wait_recv()


def sent(copies):
    for copy in copies:
        copy.wait_send()


def greet(axes):
    barrier = pltpu.get_barrier_semaphore()
    total = 0
    for axis, count, me in axes:
        for k in range(1, count):
            pl.semaphore_signal(
                barrier,
                inc=1,
                device_id={axis: lax.rem(me + k, count)},
                device_id_type=MESH,
            )
        total += count - 1
    pl.semaphore_wait(barrier, total)


class Sizes:
    def __init__(self, wide, dp, channels, images, small_images):
        self.wide, self.dp = wide, dp
        self.channels, self.images, self.small_images = channels, images, small_images
        self.slots = wide * images
        self.rows = channels * self.slots
        self.small_slots = wide * small_images
        self.small_rows = channels * self.small_slots
        self.piece_rows = 2 * channels * images
        self.pairs = images // PAIR
        self.outputs = 2 * channels
        self.br = WIDTH // wide
        self.bh = self.br // 2
        self.bc = WIDTH // dp
        self.pair_rows = up_to(2 * self.br, 16)
        self.block_lanes = up_to(7 * self.bc, 128)
        self.head_rows = up_to(self.bh, 16)

    def block_places(self):
        br, bh, bc = self.br, self.bh, self.bc
        return (
            [(0, 6 * bc, bh, bc)],
            [(br, 0, br, 3 * bc)],
            [(br, 3 * bc, br, bc)],
            [(0, 0, br, 4 * bc)],
            [(0, 4 * bc, br, bc), (0, 5 * bc, br, bc), (br, 4 * bc, br, bc), (br, 5 * bc, br, bc)],
        )

    def pack_blocks(self, ref, blocks):
        for block, places in zip(blocks, self.block_places()):
            at = 0
            for row, lane, rows, lanes in places:
                ref[row : row + rows, lane : lane + lanes] = block[at : at + rows]
                at += rows

    def unpack_blocks(self, packed):
        result = []
        for places in self.block_places():
            parts = [packed[r : r + n, q : q + m] for r, q, n, m in places]
            result.append(parts[0] if len(parts) == 1 else jnp.concatenate(parts, 0))
        return result


def placements(order_big, order_small, sizes):
    n, m = sizes.slots, sizes.small_slots
    big = order_big[...] == lax.broadcasted_iota(jnp.int32, (n, n), 0)
    small = order_small[...] == lax.broadcasted_iota(jnp.int32, (m, m), 0)
    slot = lax.broadcasted_iota(jnp.int32, (m, n), 0)
    padded = lax.broadcasted_iota(jnp.int32, (m, n), 1)
    inside = padded % sizes.images
    spread_out = (slot == padded // sizes.images * sizes.small_images + inside) & (
        inside < sizes.small_images
    )
    one = lambda v: v.astype(jnp.float32).astype(jnp.bfloat16)
    return one(big), nn(one(small), one(spread_out)).astype(jnp.bfloat16)


def token_lanes(lens):
    low = lax.broadcasted_iota(jnp.int32, (1, LANES), 1)
    high = lax.broadcasted_iota(jnp.int32, (1, 128), 1) + 128
    return (low >= 1) & (low < lens[0]), (high > SPLIT) & (high < SPLIT + lens[1])


VM = pl.BlockSpec(memory_space=pltpu.VMEM)
SM = pl.BlockSpec(memory_space=pltpu.SMEM)
HB = pl.BlockSpec(memory_space=pl.ANY)
LIMIT = 62 * 1024 * 1024 + 512 * 1024


def dma_sems(*counts):
    return [pltpu.SemaphoreType.DMA((n,)) for n in counts]


class Names:
    def __init__(self, names, refs):
        self.__dict__.update(zip(names, refs))
        assert len(names) == len(refs), (len(names), len(refs))


IN_NAMES = [
    "act_small",
    "cls_big",
    "cls_small",
    "order_big",
    "order_small",
    "vec_s",
    "vec",
    "step",
    "perm",
    "table_small",
    "mh",
    "mqkv",
    "mp",
    "mu",
    "md",
    "sh",
    "sqkv",
    "sp",
    "su",
    "sd",
    "act_hbm",
    "table_hbm",
    "bcot_hbm",
    "scot_hbm",
    "binput_hbm",
    "bmodel_hbm",
    "bqkv_hbm",
    "bhidden_hbm",
]
OUT_NAMES = [
    "bout_hbm",
    "sout_hbm",
    "dact_hbm",
    "dsmall_hbm",
    "heads_big",
    "heads_small",
    "update",
    "states",
    "vtotal",
    "scalars",
]


def main_kernel(sizes, lens, scratch_names, *refs):
    bf16, f32 = jnp.bfloat16, jnp.float32
    r = Names(IN_NAMES + OUT_NAMES + scratch_names, refs)
    me_w, me_d = lax.axis_index("wide"), lax.axis_index("dp")
    n_w, n_d = sizes.wide, sizes.dp
    br, bh, bc = sizes.br, sizes.bh, sizes.bc
    half_w = n_w // 2
    partner = me_w + 1 - 2 * lax.rem(me_w, 2)
    n_big, n_small = sizes.slots, sizes.small_slots
    big_len, small_len = lens
    channels, images, outputs = sizes.channels, sizes.images, sizes.outputs

    loads = {}
    for at, name in enumerate(("act", "table", "bcot", "scot", "bmodel", "bhidden", "bqkv", "binput")):
        source = r.bhidden_hbm.at[1] if name == "bhidden" else getattr(r, name + "_hbm")
        loads[name] = pltpu.make_async_copy(source, getattr(r, name), r.load_sem.at[at])
        loads[name].start()

    r.stage_one[...] = jnp.zeros_like(r.stage_one)
    sizes.pack_blocks(
        r.stage_one, (r.mh[...], r.mqkv[...], r.mp[...], r.mu[...], jnp.transpose(r.md[...]))
    )
    r.got_all[me_w, me_d] = r.stage_one[...].astype(bf16)
    r.mpack[me_d] = jnp.zeros(r.mpack.shape[1:], f32)
    greet((("wide", n_w, me_w), ("dp", n_d, me_d)))

    def block_copy(row, column, target, send, recv):
        slot = r.got_all.at[row, column]
        return pltpu.make_async_remote_copy(
            src_ref=slot,
            dst_ref=slot,
            send_sem=send,
            recv_sem=recv,
            device_id=target,
            device_id_type=MESH,
        )

    columns = [lax.rem(me_d + n_d - k, n_d) for k in range(n_d)]
    same_core = [lax.rem(me_w + n_w - 2 * j, n_w) for j in range(half_w)]
    one = [
        block_copy(
            me_w, me_d, {"dp": lax.rem(me_d + k, n_d)}, r.one_send.at[k - 1], r.one_recv.at[k - 1]
        )
        for k in range(1, n_d)
    ]
    across = [
        [
            block_copy(
                me_w,
                columns[k],
                {"wide": lax.rem(me_w + 2 * j, n_w)},
                r.across_send.at[(j - 1) * n_d + k],
                r.across_recv.at[(j - 1) * n_d + k],
            )
            for j in range(1, half_w)
        ]
        for k in range(n_d)
    ]
    inside = [
        [
            block_copy(
                same_core[j],
                columns[k],
                {"wide": partner},
                r.inside_send.at[j * n_d + k],
                r.inside_recv.at[j * n_d + k],
            )
            for k in range(n_d)
        ]
        for j in range(half_w)
    ]
    begin(one)
    begin(across[0])
    inside[0][0].start()

    rows_small = r.act_small[...].reshape(sizes.small_rows, r.act_small.shape[2])

    def tap_value(row, c, e):
        return r.vec_s[row, 2 * (me_w * channels + c) + e]

    def pool(tap):
        rows_big = r.act[...].reshape(sizes.rows, r.act.shape[2])
        for rows, table, wins, sums, count in (
            (rows_big, r.table, r.wins_big, r.sum_big, n_big),
            (rows_small, r.table_small, r.wins_small, r.sum_small, n_small),
        ):
            win = nt(rows, table[tap])
            wins[tap] = win.astype(bf16)
            for c in range(channels):
                own = slice(c * count, (c + 1) * count)
                for e in range(2):
                    part = tap_value(tap, c, e) * win[own]
                    if tap == 0:
                        sums[e, own] = part
                    else:
                        sums[e, own] += part

    loads["act"].wait()
    loads["table"].wait()
    for tap in range(4):
        pool(tap)
    for k in range(1, n_d):
        one[k - 1].wait_recv()
        begin(across[k])
        inside[0][k].start()
    for tap in range(4, 9):
        pool(tap)

    put_big, put_small = placements(r.order_big, r.order_small, sizes)
    slot_big = jnp.transpose(put_big.astype(f32)).astype(bf16)
    slot_small = jnp.transpose(put_small.astype(f32)).astype(bf16)
    head_big, head_small = nt(slot_big, r.cls_big[...]), nt(slot_small, r.cls_small[...])
    token_big, token_small = token_lanes(lens)
    lane = lax.broadcasted_iota(jnp.int32, (1, 128), 1)
    for e in range(2):
        for c in range(channels):
            shift = tap_value(9, c, e)
            big = jnp.where(token_big, r.sum_big[e, c * n_big : (c + 1) * n_big] + shift, 0.0)
            small = jnp.where(
                token_small, r.sum_small[e, c * n_small : (c + 1) * n_small] + shift, 0.0
            )
            big = nn(slot_big, big.astype(bf16))
            low, high = big[:, 0:128], big[:, 128:256] + nn(slot_small, small.astype(bf16))
            if e == 0:
                low = jnp.where(lane == 0, head_big[:, c : c + 1], low)
                high = jnp.where(lane == SPLIT - 128, head_small[:, c : c + 1], high)
            at = (e * channels + c) * images
            for half, value in enumerate((low, high)):
                value = value.reshape(n_w, images, 128).astype(bf16)
                r.swap[:, at : at + images, half * 128 : half * 128 + 128] = value
    per_group = WIDTH // sizes.piece_rows
    piece = WIDTH // images
    for group in range(n_w // per_group):
        block = r.swap[group * per_group : (group + 1) * per_group].reshape(WIDTH, LANES)
        moved = tn(r.perm[...], block).astype(bf16).astype(f32)
        for i in range(images):
            for s in range(per_group):
                at, to = i * piece + s * outputs, i % PAIR * outputs
                r.pooled[i // PAIR, group * per_group + s, to : to + outputs] = moved[
                    at : at + outputs
                ].astype(bf16)

    def forward_links(p):
        return links(
            "wide",
            n_w,
            me_w,
            lambda peer: r.pooled.at[p, peer],
            r.received.at[p, me_w],
            r.act_send,
            r.act_recv,
            p * (n_w - 1),
        )

    def backward_links(p):
        return links(
            "wide",
            n_w,
            me_w,
            lambda peer: r.pooled.at[p, peer],
            r.returned.at[p, me_w],
            r.back_send,
            r.back_recv,
            p * (n_w - 1),
        )

    for p in range(sizes.pairs):
        begin(forward_links(p))
        r.received[p, me_w] = r.pooled[p, me_w]

    for half in range(2):
        sizes.pack_blocks(
            r.mpack.at[me_d, half],
            (r.sh[:, half, :], r.sqkv[half], r.sp[half], r.su[half], jnp.transpose(r.sd[half])),
        )
    moments = begin(
        links("dp", n_d, me_d, lambda p: r.mpack.at[me_d], r.mpack.at[me_d], r.mom_send, r.mom_recv)
    )

    def assemble(w, row):
        for d in range(n_d):
            head, qkv, proj, up, down = sizes.unpack_blocks(r.got_all[w, d].astype(f32))
            r.gu[row(br), d * 4 * bc : (d + 1) * 4 * bc] = up
            for part in range(3):
                low, high = d * 3 * bc, (d + 1) * 3 * bc
                a, b = max(low, part * WIDTH), min(high, (part + 1) * WIDTH)
                if a < b:
                    base = part * WIDTH
                    r.gqkv[part, row(br), a - base : b - base] = qkv[:, a - low : b - low]
            r.gp[row(br), d * bc : (d + 1) * bc] = proj
            r.dact[row(4 * br), d * bc : (d + 1) * bc] = down

    def at_row(w):
        return lambda size: pl.ds(pl.multiple_of(w * size, 8), size)

    aligned = br % 8 == 0
    if aligned:
        assemble(me_w, at_row(me_w))
    for j in range(1, half_w):
        for k in range(n_d):
            across[k][j - 1].wait_recv()
            inside[j][k].start()
        if aligned:
            assemble(same_core[j], at_row(same_core[j]))
    for name in ("bmodel", "bhidden", "bqkv", "binput"):
        loads[name].wait()
    for i in range(6):
        r.bmodel_low[i] = r.bmodel[i].astype(bf16)
    r.bhidden_low[1] = r.bhidden[...].astype(bf16)
    second_hidden = pltpu.make_async_copy(r.bhidden_hbm.at[0], r.bhidden, r.load_sem.at[8])
    second_hidden.start()
    r.bqkv_low[...] = r.bqkv[...].astype(bf16)
    r.binput_low[...] = r.binput[...].astype(bf16)
    for j in range(half_w):
        arrived(inside[j])
        if aligned:
            other = lax.rem(partner + n_w - 2 * j, n_w)
            assemble(other, at_row(other))
    for w in range(n_w):
        if not aligned:
            assemble(w, lambda size: slice(w * size, (w + 1) * size))
        row, lane_at, rows, lanes = sizes.block_places()[0][0]
        for d in range(n_d):
            piece = r.got_all[w, d].astype(f32)
            r.gh[w * bh : (w + 1) * bh, d * bc : (d + 1) * bc] = piece[
                row : row + rows, lane_at : lane_at + lanes
            ]
    even = (
        lax.broadcasted_iota(jnp.int32, (WIDTH // 2, WIDTH), 1)
        == 2 * lax.broadcasted_iota(jnp.int32, (WIDTH // 2, WIDTH), 0)
    ).astype(f32).astype(bf16)
    second_hidden.wait()
    r.bhidden_low[0] = r.bhidden[...].astype(bf16)
    r.wh[...] = tn(even, r.gh[0 : WIDTH // 2].astype(bf16)).astype(bf16)
    r.wqkv[...] = r.gqkv[...].astype(bf16)
    r.wp[...] = r.gp[...].astype(bf16)
    r.wu[...] = r.gu[...].astype(bf16)
    r.wd[...] = r.dact[:, 0:WIDTH].astype(bf16)
    sums = (r.gh, r.gqkv, r.gp, r.gu, r.gdt, r.gvec, r.gub)
    block_start(big_len, small_len, r.vec, sums, r.bias, r.cot, r.ubias)
    loads["bcot"].wait()
    loads["scot"].wait()

    def out_copy(p):
        at = pl.ds(p * PAIR, PAIR)
        return pltpu.make_async_copy(r.bout.at[at], r.bout_hbm.at[at], r.out_sem.at[p])

    @pl.loop(0, sizes.pairs)
    def _(p):
        arrived(forward_links(p))
        block = r.received[p].astype(f32)
        raw = [
            jnp.concatenate([block[w, j * outputs : (j + 1) * outputs] for w in range(n_w)], 0)
            for j in range(PAIR)
        ]
        raw = jnp.concatenate([jnp.transpose(v) for v in raw], 0)
        grad = block_step(
            p * PAIR,
            raw,
            (PAIR, sizes.small_images, big_len, small_len),
            r.bcot,
            r.scot,
            r.vec,
            (r.wh, r.wqkv, r.wp, r.wu, r.wd),
            r.bout,
            r.sout,
            sums,
            (r.probs, r.bias, r.cot, r.ubias),
        )
        sent(forward_links(p))
        for j in range(PAIR):
            turned = jnp.transpose(grad[j * LANES : (j + 1) * LANES])
            for w in range(n_w):
                r.pooled[p, w, j * outputs : (j + 1) * outputs] = turned[
                    w * outputs : (w + 1) * outputs
                ].astype(bf16)
        begin(backward_links(p))
        r.returned[p, me_w] = r.pooled[p, me_w]
        out_copy(p).start()

    small_out = pltpu.make_async_copy(
        r.sout.at[pl.ds(0, sizes.small_images)], r.sout_hbm, r.out_sem.at[sizes.pairs]
    )
    small_out.start()

    u_head = tn(r.binput_low[...], nn(even, r.gh[...].astype(bf16)).astype(bf16))
    u_qkv = [tn(r.bmodel_low[1], r.gqkv[part].astype(bf16)) for part in range(3)]
    u_proj = tn(r.bmodel_low[2], r.gp[...].astype(bf16))
    u_up = tn(r.bmodel_low[4], r.gu[...].astype(bf16))
    u_down = jnp.transpose(nn(r.gdt[...].astype(bf16), r.bhidden_low[1]))
    for copies in (*across, *inside):
        sent(copies)
    r.stage_two[...] = jnp.zeros_like(r.stage_two)
    r.stage_head[...] = jnp.zeros_like(r.stage_head)
    for w in range(n_w):
        at = w * br
        r.stage_two[0:br, 0 : 4 * WIDTH] = u_up[at : at + br]
        for part in range(2):
            r.stage_two[0:br, (4 + part) * WIDTH : (5 + part) * WIDTH] = u_qkv[part][at : at + br]
        r.stage_two[br : 2 * br, 0:WIDTH] = u_qkv[2][at : at + br]
        r.stage_two[br : 2 * br, WIDTH : 2 * WIDTH] = u_proj[at : at + br]
        for j in range(4):
            r.stage_two[br : 2 * br, (2 + j) * WIDTH : (3 + j) * WIDTH] = u_down[
                4 * at + j * br : 4 * at + (j + 1) * br
            ]
        r.stage_head[0:bh] = u_head[w * bh : (w + 1) * bh]
        r.rs_send[w] = r.stage_two[...].astype(bf16)
        r.rsh_send[w] = r.stage_head[...].astype(bf16)
    first = begin(
        links("wide", n_w, me_w, lambda p: r.rs_send.at[p], r.rs_got.at[me_w], r.rs_ss, r.rs_rs)
        + links("wide", n_w, me_w, lambda p: r.rsh_send.at[p], r.rsh_got.at[me_w], r.rsh_ss, r.rsh_rs)
    )
    r.rs_got[me_w] = r.rs_send[me_w]
    r.rsh_got[me_w] = r.rsh_send[me_w]

    for p in range(sizes.pairs):
        arrived(backward_links(p))
    for group in range(n_w // per_group):
        parts = [
            r.returned[i // PAIR, group * per_group + s].astype(f32)[
                i % PAIR * outputs : (i % PAIR + 1) * outputs
            ]
            for i in range(images)
            for s in range(per_group)
        ]
        moved = nn(r.perm[...], jnp.concatenate(parts, 0).astype(bf16))
        for s in range(per_group):
            for e in range(2):
                for c in range(channels):
                    at = s * sizes.piece_rows + (e * channels + c) * images
                    to = (c * n_w + group * per_group + s) * images
                    r.sum_big[e, to : to + images] = moved[at : at + images]

    def fold(big, small):
        value = jnp.sum(big.reshape(n_big // 8, 8, LANES), 0)
        return value[:, 0:128] + value[:, 128:256] + jnp.sum(small.reshape(n_small // 8, 8, 128), 0)

    columns_big = jnp.zeros((n_big, 128), f32)
    columns_small = jnp.zeros((n_small, 128), f32)
    put_big, put_small = placements(r.order_big, r.order_small, sizes)
    for c in range(channels):
        own_big, own_small = slice(c * n_big, (c + 1) * n_big), slice(c * n_small, (c + 1) * n_small)
        group = slice(c * 8, (c + 1) * 8)
        pair = []
        for e in range(2):
            block = r.sum_big[e, own_big].astype(bf16)
            pair.append((nn(put_big, block), nn(put_small, block[:, 128:256])))
            r.taps[9, e, group] = fold(
                jnp.where(token_big, pair[e][0], 0.0), jnp.where(token_small, pair[e][1], 0.0)
            )
        columns_big = jnp.where(lane == c, pair[0][0][:, 0:1], columns_big)
        columns_small = jnp.where(lane == c, pair[0][1][:, SPLIT - 128 : SPLIT - 127], columns_small)
        for tap in range(9):
            big, small = r.wins_big[tap, own_big].astype(f32), r.wins_small[tap, own_small].astype(f32)
            for e in range(2):
                r.taps[tap, e, group] = fold(pair[e][0] * big, pair[e][1] * small)
            up, down = (tap_value(tap, c, e) for e in range(2))
            r.wins_big[tap, own_big] = (up * pair[0][0] + down * pair[1][0]).astype(bf16)
            r.wins_small[tap, own_small] = (up * pair[0][1] + down * pair[1][1]).astype(bf16)
    r.heads_big[...] = columns_big
    r.heads_small[...] = columns_small

    r.vpart[...] = jnp.zeros_like(r.vpart)
    half_rows = channels * 8
    own_channel = lax.broadcasted_iota(jnp.int32, (half_rows, WIDTH), 0) // 8
    own_lane = lax.broadcasted_iota(jnp.int32, (half_rows, WIDTH), 1)
    conv = jnp.zeros((128, WIDTH), f32)
    for e in range(2):
        place = (own_lane == 2 * (me_w * channels + own_channel) + e).astype(f32)
        part = jnp.zeros((half_rows, 128), f32)
        for tap in range(10):
            part = jnp.where(lane == tap, jnp.sum(r.taps[tap, e], -1, keepdims=True), part)
        conv += lax.dot_general(
            part,
            place,
            (((0,), (0,)), ((), ())),
            precision=lax.Precision.HIGHEST,
            preferred_element_type=f32,
        )
    r.vpart[0:10] = conv[0:10]
    r.vpart[10:19] = r.gvec[0:9]
    for j in range(4):
        r.vpart[19 + j : 20 + j] = r.gub[:, j * WIDTH : (j + 1) * WIDTH]
    r.v_wide[me_w] = r.vpart[...]
    vec_one = begin(
        links("wide", n_w, me_w, lambda p: r.v_wide.at[me_w], r.v_wide.at[me_w], r.v1_s, r.v1_r)
    )

    arrived(first)
    rows_two = r.rs_got[0].astype(f32)
    rows_head = r.rsh_got[0].astype(f32)
    for w in range(1, n_w):
        rows_two += r.rs_got[w].astype(f32)
        rows_head += r.rsh_got[w].astype(f32)
    rows_two = rows_two.astype(bf16)
    t_up = nn(rows_two[0:br, 0 : 4 * WIDTH], r.bhidden_low[0])
    t_qkv = nn(rows_two[0:br, 4 * WIDTH : 6 * WIDTH], r.bqkv_low[0 : 2 * WIDTH]) + nn(
        rows_two[br : 2 * br, 0:WIDTH], r.bqkv_low[2 * WIDTH :]
    )
    t_proj = nn(rows_two[br : 2 * br, WIDTH : 2 * WIDTH], r.bmodel_low[3])
    t_down = [
        nn(rows_two[br : 2 * br, (2 + j) * WIDTH : (3 + j) * WIDTH], r.bmodel_low[5])
        for j in range(4)
    ]
    t_head = nn(rows_head.astype(bf16), r.bmodel_low[0])
    for d in range(n_d):
        own = slice(d * bc, (d + 1) * bc)
        sizes.pack_blocks(
            r.stage_one,
            (
                t_head[0:bh, own],
                t_qkv[:, 3 * d * bc : 3 * (d + 1) * bc],
                t_proj[:, own],
                t_up[:, 4 * d * bc : 4 * (d + 1) * bc],
                jnp.concatenate([t[:, own] for t in t_down], 0),
            ),
        )
        r.t_send[d] = r.stage_one[...].astype(bf16)
    second = begin(
        links("dp", n_d, me_d, lambda p: r.t_send.at[p], r.t_got.at[me_d], r.t_ss, r.t_rs)
    )
    r.t_got[me_d] = r.t_send[me_d]
    arrived(vec_one)
    vsum = r.v_wide[0]
    for w in range(1, n_w):
        vsum += r.v_wide[w]
    r.v_dp[me_d] = vsum
    vec_two = begin(links("dp", n_d, me_d, lambda p: r.v_dp.at[me_d], r.v_dp.at[me_d], r.v2_s, r.v2_r))

    def act_part(chunk):
        at = pl.ds(chunk * 256, 256)
        table = r.table[...].reshape(9 * LANES, r.table.shape[2])
        mixed = jnp.concatenate([r.wins_big[tap, at, :] for tap in range(9)], 1)
        r.dact[at, :] = nn(mixed, table)
        copy = pltpu.make_async_copy(
            r.dact.at[at], r.dact_hbm.at[at], r.out_sem.at[sizes.pairs + 2 + chunk]
        )
        copy.start()
        return copy

    chunks = list(range(sizes.rows // 256))
    act_out = [act_part(chunk) for chunk in chunks[:1]]
    arrived(second)
    turned = r.t_got[0].astype(f32)
    for d in range(1, n_d):
        turned += r.t_got[d].astype(f32)
    r.full_got[me_d] = turned.astype(bf16)
    third = begin(
        links("dp", n_d, me_d, lambda p: r.full_got.at[me_d], r.full_got.at[me_d], r.d_s, r.d_r)
    )
    act_out += [act_part(chunk) for chunk in chunks[1:2]]
    arrived(vec_two)
    vsum = r.v_dp[0]
    for d in range(1, n_d):
        vsum += r.v_dp[d]
    r.vtotal[...] = vsum

    def total(value):
        return jnp.sum(jnp.sum(value * value, 0, keepdims=True), -1, keepdims=True)

    vec_square = total(vsum)
    count = jnp.full((8, 128), r.step[0], jnp.int32).astype(f32)[0:1, 0:1]
    fix_one = 1.0 - jnp.exp(count * float(np.log(beta_one)))
    fix_two = 1.0 - jnp.exp(count * float(np.log(beta_two)))
    arrived(third)
    squares = jnp.zeros(r.stage_one.shape, f32)
    for d in range(n_d):
        part = r.full_got[d].astype(f32)
        squares += part * part
    square = jnp.sum(jnp.sum(squares, 0, keepdims=True), -1, keepdims=True)
    r.s_wide[me_w] = jnp.broadcast_to(square, (8, 128))
    fourth = begin(
        links("wide", n_w, me_w, lambda p: r.s_wide.at[me_w], r.s_wide.at[me_w], r.s_s, r.s_r)
    )
    act_out += [act_part(chunk) for chunk in chunks[2:]]
    mixed = jnp.concatenate([r.wins_small[tap] for tap in range(9)], 1)
    r.dsmall[...] = nn(mixed, r.table_small[...].reshape(9 * 128, r.table_small.shape[2]))
    act_out.append(pltpu.make_async_copy(r.dsmall, r.dsmall_hbm, r.out_sem.at[sizes.pairs + 1]))
    act_out[-1].start()
    arrived(moments)
    arrived(fourth)
    square = r.s_wide[0][0:1, 0:1]
    for w in range(1, n_w):
        square += r.s_wide[w][0:1, 0:1]
    norm = jnp.sqrt(square + vec_square)
    factor = jnp.minimum(1.0, clip_limit / (norm + 1e-06))
    which = lax.broadcasted_iota(jnp.int32, (8, 128), 1)
    r.scalars[...] = jnp.where(
        which == 0,
        norm,
        jnp.where(which == 1, factor, jnp.where(which == 2, fix_one, fix_two)),
    )

    def adam(gradient, old):
        scaled = gradient * factor
        moment = beta_one * old[0] + (1.0 - beta_one) * scaled
        second_moment = beta_two * old[1] * old[1] + (1.0 - beta_two) * scaled * scaled
        return moment, second_moment

    for d in range(n_d):
        moment, second_moment = adam(r.full_got[d].astype(f32), r.mpack[d])
        direction = moment / fix_one / (jnp.sqrt(second_moment / fix_two) + adam_eps)
        head, qkv, proj, up, down = sizes.unpack_blocks(direction)
        r.row_head[0:bh, d * bc : (d + 1) * bc] = head
        r.row_qkv[:, 3 * d * bc : 3 * (d + 1) * bc] = qkv
        r.row_proj[:, d * bc : (d + 1) * bc] = proj
        r.row_up[:, 4 * d * bc : 4 * (d + 1) * bc] = up
        r.row_down[:, d * bc : (d + 1) * bc] = down

    def right_rows(ref, size, unit=8):
        return ref[pl.ds(pl.multiple_of(me_d * size, unit), size), :].astype(bf16)

    sizes.pack_blocks(
        r.stage_one,
        (
            nt(r.row_head[...].astype(bf16), right_rows(r.bmodel.at[0], bc))[0:bh],
            nt(r.row_qkv[...].astype(bf16), right_rows(r.bqkv, 3 * bc)),
            nt(r.row_proj[...].astype(bf16), right_rows(r.bmodel.at[3], bc)),
            nt(r.row_up[...].astype(bf16), right_rows(r.bhidden_low.at[0], 4 * bc, 16)),
            nt(r.row_down[...].astype(bf16), right_rows(r.bmodel.at[5], bc)),
        ),
    )
    r.y_got[me_w] = r.stage_one[...].astype(bf16)
    fifth = begin(
        links("wide", n_w, me_w, lambda p: r.y_got.at[me_w], r.y_got.at[me_w], r.y_s, r.y_r)
    )
    moment, second_moment = adam(turned, r.mpack[me_d])
    r.states[0] = moment
    r.states[1] = jnp.sqrt(second_moment)

    def left_rows(ref, size, unit=8):
        if size % unit == 0:
            return ref[pl.ds(pl.multiple_of(me_w * size, unit), size), :].astype(bf16)
        own = lax.broadcasted_iota(jnp.int32, (size, ref.shape[0]), 0) + me_w * size
        pick = own == lax.broadcasted_iota(jnp.int32, (size, ref.shape[0]), 1)
        return nn(pick.astype(f32).astype(bf16), ref[...].astype(bf16)).astype(bf16)

    lefts = (
        left_rows(r.binput, bh),
        left_rows(r.bmodel.at[1], br),
        left_rows(r.bmodel.at[2], br),
        left_rows(r.bmodel.at[4], br),
        left_rows(r.bhidden_low.at[1], 4 * br, 16),
    )
    r.update[...] = jnp.zeros_like(r.update)
    arrived(fifth)
    parts = [sizes.unpack_blocks(r.y_got[w].astype(f32)) for w in range(n_w)]
    sizes.pack_blocks(
        r.update,
        [
            nn(lefts[m], jnp.concatenate([part[m] for part in parts], 0).astype(bf16))
            for m in range(5)
        ],
    )
    for p in range(sizes.pairs):
        sent(backward_links(p))
        out_copy(p).wait()
    small_out.wait()
    for copy in act_out:
        copy.wait()
    for copies in (one, moments, first, vec_one, second, vec_two, third, fourth, fifth):
        sent(copies)


def finish_kernel(
    sizes,
    mh,
    mqkv,
    mp,
    mu,
    md,
    vec,
    vmom,
    heads_big,
    heads_small,
    update,
    states,
    vtotal,
    scalars,
    big_from,
    small_from,
    act_from,
    act_small_from,
    big_to,
    small_to,
    act_to,
    act_small_to,
    dcls_big,
    dcls_small,
    norm,
    nvec,
    nvmom,
    *outs,
):
    outs, (hold_big, hold_small, hold_act, hold_act_small, sem) = outs[:-5], outs[-5:]
    moves = []
    for source, hold, target, parts in (
        (act_from, hold_act, act_to, 4),
        (big_from, hold_big, big_to, 4),
        (act_small_from, hold_act_small, act_small_to, 1),
        (small_from, hold_small, small_to, 1),
    ):
        size = source.shape[0] // parts
        for part in range(parts):
            at = pl.ds(part * size, size)
            pair = [(source.at[at], hold.at[at]), (hold.at[at], target.at[at])]
            moves.append(
                [
                    pltpu.make_async_copy(src, dst, sem.at[which, len(moves)])
                    for which, (src, dst) in enumerate(pair)
                ]
            )
    for move in moves:
        move[0].start()
    norm[0] = scalars[0, 0]
    factor, fix_one, fix_two = (scalars[0, j] for j in (1, 2, 3))
    for move in moves:
        move[0].wait()
        move[1].start()
    dcls_big[...] = jnp.transpose(heads_big[...])[0 : sizes.channels]
    dcls_small[...] = jnp.transpose(heads_small[...])[0 : sizes.channels]
    updates = sizes.unpack_blocks(update[...])
    firsts = sizes.unpack_blocks(states[0])
    seconds = sizes.unpack_blocks(states[1])
    for member, master in enumerate((mh, mqkv, mp, mu, md)):
        change, first, second = updates[member], firsts[member], seconds[member]
        if member == 4:
            change, first, second = (jnp.transpose(v) for v in (change, first, second))
        fresh = master[...] - rate_matrix * change
        outs[member][...] = fresh
        if member == 0:
            outs[5][:, 0, :] = first
            outs[5][:, 1, :] = second
        else:
            outs[5 + member][0] = first
            outs[5 + member][1] = second
        outs[10 + member][...] = fresh.astype(jnp.bfloat16)
    scaled = vtotal[0:23] * factor
    first = beta_one * vmom[:, 0, :] + (1.0 - beta_one) * scaled
    second = beta_two * vmom[:, 1, :] * vmom[:, 1, :] + (1.0 - beta_two) * scaled * scaled
    direction = first / fix_one / (jnp.sqrt(second / fix_two) + adam_eps)
    nvec[...] = vec[...] * (1.0 - rate_vector * decay_rate) - rate_vector * direction
    nvmom[:, 0, :] = first
    nvmom[:, 1, :] = jnp.sqrt(second)

    for move in moves:
        move[1].wait()


def run_main(sizes, lens, ins, hbm):
    bf16, f32 = jnp.bfloat16, jnp.float32
    w, d = sizes.wide, sizes.dp
    images, pairs = sizes.images, sizes.pairs
    act, table, bcot, scot, binput, bmodel, bqkv, bhidden = hbm
    table_small = ins[9]
    small_cells = table_small.shape[2]
    hidden = 4 * WIDTH
    pack = (sizes.pair_rows, sizes.block_lanes)
    two = (sizes.pair_rows, 6 * WIDTH)
    head = (sizes.head_rows, WIDTH)
    swap = (pairs, w, PAIR * sizes.outputs, LANES)
    big, small = sizes.rows, sizes.small_rows
    outs = [
        (bcot.shape, f32),
        (scot.shape, f32),
        ((big, act.shape[2]), f32),
        ((small, small_cells), f32),
        ((sizes.slots, 128), f32),
        ((sizes.small_slots, 128), f32),
        (pack, f32),
        ((2,) + pack, f32),
        ((24, WIDTH), f32),
        ((8, 128), f32),
    ]
    scratch = dict(
        act=(act.shape, bf16),
        table=(table.shape, bf16),
        bcot=(bcot.shape, bf16),
        scot=(scot.shape, bf16),
        binput=(binput.shape, f32),
        bmodel=(bmodel.shape, f32),
        bqkv=(bqkv.shape, f32),
        bhidden=(bhidden.shape[1:], f32),
        binput_low=(binput.shape, bf16),
        bmodel_low=(bmodel.shape, bf16),
        bqkv_low=(bqkv.shape, bf16),
        bhidden_low=(bhidden.shape, bf16),
        stage_one=(pack, f32),
        stage_two=(two, f32),
        stage_head=(head, f32),
        got_all=((w, d) + pack, bf16),
        rs_send=((w,) + two, bf16),
        rsh_send=((w,) + head, bf16),
        mpack=((d, 2) + pack, f32),
        wins_big=((9, big, LANES), bf16),
        wins_small=((9, small, 128), bf16),
        sum_big=((2, big, LANES), f32),
        sum_small=((2, small, 128), f32),
        swap=((w, sizes.piece_rows, LANES), bf16),
        pooled=(swap, bf16),
        received=(swap, bf16),
        returned=(swap, bf16),
        wh=((WIDTH, WIDTH), bf16),
        wqkv=((3, WIDTH, WIDTH), bf16),
        wp=((WIDTH, WIDTH), bf16),
        wu=((WIDTH, hidden), bf16),
        wd=((hidden, WIDTH), bf16),
        gh=((WIDTH, WIDTH), f32),
        gqkv=((3, WIDTH, WIDTH), f32),
        gp=((WIDTH, WIDTH), f32),
        gu=((WIDTH, hidden), f32),
        gdt=((WIDTH, hidden), f32),
        gvec=((16, WIDTH), f32),
        gub=((1, hidden), f32),
        probs=((PAIR, HEADS, LANES, LANES), f32),
        bias=((LANES, LANES), f32),
        cot=((PAIR * LANES, WIDTH), bf16),
        ubias=((1, hidden), f32),
        bout=(bcot.shape, f32),
        sout=((images,) + scot.shape[1:], f32),
        rs_got=((w,) + two, bf16),
        rsh_got=((w,) + head, bf16),
        taps=((10, 2, sizes.channels * 8, 128), f32),
        dact=((big, act.shape[2]), f32),
        dsmall=((small, small_cells), f32),
        vpart=((24, WIDTH), f32),
        v_wide=((w, 24, WIDTH), f32),
        v_dp=((d, 24, WIDTH), f32),
        t_send=((d,) + pack, bf16),
        t_got=((d,) + pack, bf16),
        full_got=((d,) + pack, bf16),
        s_wide=((w, 8, 128), f32),
        row_head=((sizes.bh, WIDTH), f32),
        row_qkv=((sizes.br, 3 * WIDTH), f32),
        row_proj=((sizes.br, WIDTH), f32),
        row_up=((sizes.br, hidden), f32),
        row_down=((4 * sizes.br, WIDTH), f32),
        y_got=((w,) + pack, bf16),
    )
    sems = dict(
        load_sem=9,
        out_sem=pairs + 2 + big // 256,
        one_send=d - 1,
        one_recv=d - 1,
        across_send=(w // 2 - 1) * d,
        across_recv=(w // 2 - 1) * d,
        inside_send=w // 2 * d,
        inside_recv=w // 2 * d,
        act_send=pairs * (w - 1),
        act_recv=pairs * (w - 1),
        back_send=pairs * (w - 1),
        back_recv=pairs * (w - 1),
        mom_send=d - 1,
        mom_recv=d - 1,
    )
    for name in ("rs_ss", "rs_rs", "rsh_ss", "rsh_rs", "v1_s", "v1_r", "s_s", "s_r", "y_s", "y_r"):
        sems[name] = w - 1
    for name in ("t_ss", "t_rs", "v2_s", "v2_r", "d_s", "d_r"):
        sems[name] = d - 1
    return pl.pallas_call(
        partial(main_kernel, sizes, lens, list(scratch) + list(sems)),
        in_specs=[VM] * 5 + [SM, VM, SM] + [VM] * 12 + [HB] * 8,
        out_specs=[HB] * 4 + [VM] * 6,
        out_shape=[jax.ShapeDtypeStruct(s, t) for s, t in outs],
        scratch_shapes=[pltpu.VMEM(s, t) for s, t in scratch.values()] + dma_sems(*sems.values()),
        compiler_params=pltpu.CompilerParams(
            collective_id=0, has_side_effects=True, vmem_limit_bytes=LIMIT
        ),
        name="main",
    )(*ins, *hbm)


def run_finish(sizes, masters, vec, vmom, moments, heads, packs, large):
    f32, bf16 = jnp.float32, jnp.bfloat16
    shapes = [m.shape for m in masters]
    outs = [(a.shape, f32) for a in large]
    outs += [((sizes.channels, h.shape[0]), f32) for h in heads]
    outs += [((1,), f32), (vec.shape, f32), (vmom.shape, f32)]
    outs += [(s, f32) for s in shapes] + [(m.shape, f32) for m in moments]
    outs += [(s, bf16) for s in shapes]
    return pl.pallas_call(
        partial(finish_kernel, sizes),
        in_specs=[VM] * 12 + [SM] + [HB] * 4,
        out_specs=[HB] * 4 + [VM, VM, SM] + [VM] * (len(outs) - 7),
        out_shape=[jax.ShapeDtypeStruct(s, t) for s, t in outs],
        scratch_shapes=[pltpu.VMEM(large[i].shape, f32) for i in range(4)]
        + [pltpu.SemaphoreType.DMA((2, 10))],
        compiler_params=pltpu.CompilerParams(vmem_limit_bytes=LIMIT),
        name="finish",
    )(*masters, vec, vmom, *heads, *packs, *large)


def pool_table(grid, side, lane, lanes):
    table = np.zeros((9, lanes, grid * grid), np.float32)
    for tap in range(9):
        for y in range(side):
            for x in range(side):
                sy, sx = 2 * y + tap // 3 - 1, 2 * x + tap % 3 - 1
                if 0 <= sy < grid and 0 <= sx < grid:
                    table[tap, lane + y * side + x, sy * grid + sx] = 1.0
    return jnp.asarray(table, jnp.bfloat16)


def per_device(
    wide_n,
    dp_n,
    big_act,
    big_cls,
    small_act,
    small_cls,
    big_order,
    small_order,
    big_cot,
    small_cot,
    vec_params,
    vec_moments,
    *rest,
):
    masters, moments, bases, step = list(rest[0:5]), list(rest[5:10]), rest[10:14], rest[14]
    channels = big_act.shape[1]
    images, small_images = big_cot.shape[0], small_cot.shape[0]
    lens = (big_cot.shape[1], small_cot.shape[1])
    sizes = Sizes(wide_n, dp_n, channels, images, small_images)
    side = lambda cells: round(cells**0.5)
    tables = (
        pool_table(side(big_act.shape[2]), side(lens[0] - 1), 1, LANES),
        pool_table(side(small_act.shape[2]), side(lens[1] - 1), SPLIT + 1 - 128, 128),
    )
    perm = row_permutation(channels, images)
    flip = lambda a, i, j: jnp.swapaxes(a, i, j)
    acts = [flip(a, 0, 1) for a in (big_act, small_act, big_cls, small_cls)]
    orders = (big_order, small_order)
    masters[4] = flip(masters[4], 0, 1)
    moments[0], moments[4] = flip(moments[0], 0, 1), flip(moments[4], 1, 2)
    vec_moments = flip(vec_moments, 0, 1)

    ins = (*acts[1:], *orders, vec_params, vec_params, step, perm, tables[1], *masters, *moments)
    hbm = (acts[0], tables[0], flip(big_cot, 1, 2), small_cot, *bases)
    *large, heads_big, heads_small, update, states, vtotal, scalars = run_main(
        sizes, lens, ins, hbm
    )
    packs = (update, states, vtotal, scalars)
    results = list(
        run_finish(
            sizes, masters, vec_params, vec_moments, moments, (heads_big, heads_small), packs, large
        )
    )
    big_out, small_out, dact_big, dact_small = results[0:4]
    results = results[4:]
    cls_big, cls_small, norm, new_vec, new_vec_moments = results[0:5]
    masters, moments, copies = results[5:10], results[10:15], results[15:20]
    masters[4], copies[4] = flip(masters[4], 0, 1), flip(copies[4], 0, 1)
    moments[0], moments[4] = flip(moments[0], 0, 1), flip(moments[4], 1, 2)
    return (
        flip(big_out, 1, 2),
        small_out,
        flip(dact_big.reshape(channels, sizes.slots, -1), 0, 1),
        flip(cls_big, 0, 1),
        flip(dact_small.reshape(channels, sizes.small_slots, -1), 0, 1),
        flip(cls_small, 0, 1),
        norm,
        new_vec,
        flip(new_vec_moments, 0, 1),
        *masters,
        *moments,
        *copies,
    )


def solution(mesh):
    split, wide_first, free = P("dp", "wide", None), P("wide", "dp"), P()
    moment = P(None, "wide", "dp")
    both = P(("dp", "wide"), None, None)
    acts = (split, P("dp", "wide"), split, P("dp", "wide"))
    in_specs = (
        acts
        + (P("dp", None), P("dp", None), both, both, free, free)
        + (wide_first,) * 5
        + (moment,) * 5
        + (free,) * 5
    )
    out_specs = (
        (both, both) + acts + (free,) * 3 + (wide_first,) * 5 + (moment,) * 5 + (wide_first,) * 5
    )
    return jax.shard_map(
        partial(per_device, mesh.shape["wide"], mesh.shape["dp"]),
        mesh=mesh,
        in_specs=in_specs,
        out_specs=out_specs,
        check_vma=False,
    )
```

```python
from functools import partial

import jax
import jax.numpy as jnp
import numpy as np
from jax import lax
from jax.experimental import pallas as pl
from jax.experimental.pallas import tpu as pltpu
from jax.sharding import PartitionSpec as P

HEADS = 4
HD = 48
beta_one = 0.9
beta_two = 0.999
adam_eps = 1e-08
norm_eps = 1e-06
rate_matrix = 0.08
rate_vector = 0.25
decay_rate = 0.05
clip_limit = 1.0
LANES = 256
SPLIT = 208
SCORE_SCALE = float(HD ** (-0.5) * np.log2(np.e))


def nt(a, b):
    return lax.dot_general(a, b, (((1,), (1,)), ((), ())), preferred_element_type=jnp.float32)


def tn(a, b):
    return lax.dot_general(a, b, (((0,), (0,)), ((), ())), preferred_element_type=jnp.float32)


def nn(a, b):
    return jnp.dot(a, b, preferred_element_type=jnp.float32)


def colsum(v):
    return jnp.sum(v, 0, keepdims=True)


def norm_forward(rows, gain, shift):
    centered = rows - jnp.mean(rows, -1, keepdims=True)
    scale = lax.rsqrt(jnp.mean(centered * centered, -1, keepdims=True) + norm_eps)
    hat = centered * scale
    return hat, scale, (hat * gain + shift).astype(jnp.bfloat16)


def norm_backward(grad, hat, scale, gain):
    inner = grad * gain
    mean_a = jnp.mean(inner, -1, keepdims=True)
    mean_b = jnp.mean(inner * hat, -1, keepdims=True)
    return scale * (inner - mean_a - hat * mean_b)


def block_start(big_len, small_len, vec, sums, bias, cot, ubias):
    for ref in sums:
        ref[...] = jnp.zeros_like(ref)
    cot[...] = jnp.zeros_like(cot)
    width = vec.shape[1]
    for j in range(4):
        ubias[:, j * width : (j + 1) * width] = vec[19 + j : 20 + j]
    key_id = lax.broadcasted_iota(jnp.int32, (LANES, LANES), 1)
    query_id = lax.broadcasted_iota(jnp.int32, (LANES, LANES), 0)
    keep_big = (query_id < SPLIT) & (key_id < big_len)
    keep_small = (query_id >= SPLIT) & (key_id >= SPLIT) & (key_id < SPLIT + small_len)
    bias[...] = jnp.where(keep_big | keep_small, 0.0, -1e30)


def block_step(image, raw, counts, bcot, scot, vec, weights, bout, sout, sums, scratch):
    pair, small_n, big_len, small_len = counts
    wh, wqkv, wp, wu, wd = weights
    gh, gqkv, gp, gu, gdt, gvec, gub = sums
    probs, bias, cot, ubias = scratch
    width = vec.shape[1]
    row_id = lax.broadcasted_iota(jnp.int32, (pair * LANES, 1), 0) % LANES
    lane_id = lax.broadcasted_iota(jnp.int32, (1, width), 1)
    for j in range(pair):
        base = j * LANES
        turned = jnp.transpose(bcot[image + j].astype(jnp.float32))
        cot[base : base + big_len] = turned.astype(jnp.bfloat16)
        small = scot[jnp.minimum(image + j, small_n - 1)].astype(jnp.float32)
        small = jnp.where(image + j < small_n, small, 0.0).astype(jnp.bfloat16)
        cot[base + SPLIT : base + SPLIT + small_len] = small
    raw_low = raw.astype(jnp.bfloat16)
    is_head = (row_id == 0) | (row_id == SPLIT)
    rows = jnp.where(is_head, nn(raw_low, wh[...]) + vec[10:11], raw)
    hat_one, scale_one, normed_one = norm_forward(rows, vec[11:12], vec[12:13])
    queries = (nn(normed_one, wqkv[0]) + vec[13:14]).astype(jnp.bfloat16)
    keys_in = nn(normed_one, wqkv[1]).astype(jnp.bfloat16)
    values = (nn(normed_one, wqkv[2]) + vec[14:15]).astype(jnp.bfloat16)
    zero = jnp.zeros((), jnp.bfloat16)
    in_head = [(lane_id >= h * HD) & (lane_id < (h + 1) * HD) for h in range(HEADS)]
    tiles = [slice(j * LANES, (j + 1) * LANES) for j in range(pair)]
    chains = [(j, h) for h in range(HEADS) for j in range(pair)]
    scores = {
        (j, h): nt(jnp.where(in_head[h], queries[tiles[j]], zero), keys_in[tiles[j]])
        for j, h in chains
    }
    low = {}
    for j, h in chains:
        value = scores[j, h] + bias[...]
        weights = jnp.exp2((value - jnp.max(value, -1, keepdims=True)) * SCORE_SCALE)
        probas = weights * (1.0 / jnp.sum(weights, -1, keepdims=True))
        probs[j, h] = probas
        low[j, h] = probas.astype(jnp.bfloat16)
    mixture = [
        nn(
            jnp.concatenate([low[j, h] for h in range(HEADS)], 1),
            jnp.concatenate([jnp.where(in_head[h], values[tiles[j]], zero) for h in range(HEADS)], 0),
        )
        for j in range(pair)
    ]
    mixture = jnp.concatenate(mixture, 0)
    mixture = mixture.astype(jnp.bfloat16)
    middle = rows + nn(mixture, wp[...]) + vec[15:16]
    hat_two, scale_two, normed_two = norm_forward(middle, vec[16:17], vec[17:18])
    pre = nn(normed_two, wu[...]) + ubias[...]
    cdf = 0.5 + 0.5 * lax.erf(pre * 0.7071067811865476)
    slope = cdf + pre * jnp.exp(pre * pre * -0.5) * 0.3989422804014327
    active = (pre * cdf).astype(jnp.bfloat16)
    result = middle + nn(active, wd[...]) + vec[18:19]
    for j in range(pair):
        bout[image + j] = jnp.transpose(result[tiles[j]])[:, :big_len]
        base = j * LANES + SPLIT
        sout[image + j] = result[base : base + small_len]
    cot_low = cot[...]
    cot_rows = cot_low.astype(jnp.float32)
    gdt[...] += tn(cot_low, active)
    gvec[8:9] += colsum(cot_rows)
    grad_pre = (nt(cot_low, wd[...]) * slope).astype(jnp.bfloat16)
    gu[...] += tn(normed_two, grad_pre)
    gub[...] += colsum(grad_pre.astype(jnp.float32))
    grad_two = nt(grad_pre, wu[...])
    gvec[6:7] += colsum(grad_two * hat_two)
    gvec[7:8] += colsum(grad_two)
    grad_mid = norm_backward(grad_two, hat_two, scale_two, vec[16:17]) + cot_rows
    branch = grad_mid.astype(jnp.bfloat16)
    gp[...] += tn(mixture, branch)
    gvec[5:6] += colsum(branch.astype(jnp.float32))
    grad_mix = nt(branch, wp[...]).astype(jnp.bfloat16)
    own = {(j, h): jnp.where(in_head[h], grad_mix[tiles[j]], zero) for j, h in chains}
    grad_probs = {(j, h): nt(own[j, h], values[tiles[j]]) for j, h in chains}
    grad_scores = {}
    for j, h in chains:
        probas = probs[j, h]
        inner = jnp.sum(probas * grad_probs[j, h], -1, keepdims=True)
        grad_scores[j, h] = (probas * (grad_probs[j, h] - inner)).astype(jnp.bfloat16)
    stack = lambda source: [
        jnp.concatenate([jnp.where(in_head[h], source[tile], zero) for h in range(HEADS)], 0)
        for tile in tiles
    ]
    wide_keys, wide_queries = stack(keys_in), stack(queries)
    all_scores = [jnp.concatenate([grad_scores[j, h] for h in range(HEADS)], 1) for j in range(pair)]
    tall_scores = [jnp.concatenate([grad_scores[j, h] for h in range(HEADS)], 0) for j in range(pair)]
    tall_probs = [
        jnp.concatenate([probs[j, h].astype(jnp.bfloat16) for h in range(HEADS)], 0)
        for j in range(pair)
    ]
    tall_own = [jnp.concatenate([own[j, h] for h in range(HEADS)], 0) for j in range(pair)]
    grad_q = jnp.concatenate([nn(all_scores[j], wide_keys[j]) for j in range(pair)], 0)
    grad_k = jnp.concatenate([tn(tall_scores[j], wide_queries[j]) for j in range(pair)], 0)
    grad_v = jnp.concatenate([tn(tall_probs[j], tall_own[j]) for j in range(pair)], 0)
    grad_q = (grad_q * HD ** (-0.5)).astype(jnp.bfloat16)
    grad_k = (grad_k * HD ** (-0.5)).astype(jnp.bfloat16)
    grad_v = grad_v.astype(jnp.bfloat16)
    gqkv[0] += tn(normed_one, grad_q)
    gqkv[1] += tn(normed_one, grad_k)
    gqkv[2] += tn(normed_one, grad_v)
    gvec[3:4] += colsum(grad_q.astype(jnp.float32))
    gvec[4:5] += colsum(grad_v.astype(jnp.float32))
    grad_one = nt(grad_q, wqkv[0]) + nt(grad_k, wqkv[1]) + nt(grad_v, wqkv[2])
    gvec[1:2] += colsum(grad_one * hat_one)
    gvec[2:3] += colsum(grad_one)
    grad_tok = norm_backward(grad_one, hat_one, scale_one, vec[11:12]) + grad_mid
    grad_head = jnp.where(is_head, grad_tok, 0.0).astype(jnp.bfloat16)
    gh[...] += tn(raw_low, grad_head)
    gvec[0:1] += colsum(grad_head.astype(jnp.float32))
    return jnp.where(is_head, nt(grad_head, wh[...]), grad_tok)


def row_permutation(channels, images):
    width = 192
    group = width // (2 * channels * images)
    table = np.zeros((width, width), np.float32)
    for s in range(group):
        for e in range(2):
            for c in range(channels):
                for i in range(images):
                    row = ((s * 2 + e) * channels + c) * images + i
                    table[row, i * (width // images) + s * 2 * channels + 2 * c + e] = 1.0
    return jnp.asarray(table, jnp.bfloat16)
MESH = pl.DeviceIdType.MESH
WIDTH = 192
PAIR = 2


def up_to(value, unit):
    return -(-value // unit) * unit


def links(axis, count, me, src_of, dst, send, recv, base=0):
    copies = []
    for k in range(1, count):
        peer = lax.rem(me + k, count)
        copies.append(
            pltpu.make_async_remote_copy(
                src_ref=src_of(peer),
                dst_ref=dst,
                send_sem=send.at[base + k - 1],
                recv_sem=recv.at[base + k - 1],
                device_id={axis: peer},
                device_id_type=MESH,
            )
        )
    return copies


def begin(copies):
    for copy in copies:
        copy.start()
    return copies


def arrived(copies):
    for copy in copies:
        copy.wait_recv()


def sent(copies):
    for copy in copies:
        copy.wait_send()


def greet(axes):
    barrier = pltpu.get_barrier_semaphore()
    total = 0
    for axis, count, me in axes:
        for k in range(1, count):
            pl.semaphore_signal(
                barrier,
                inc=1,
                device_id={axis: lax.rem(me + k, count)},
                device_id_type=MESH,
            )
        total += count - 1
    pl.semaphore_wait(barrier, total)


class Sizes:
    def __init__(self, wide, dp, channels, images, small_images):
        self.wide, self.dp = wide, dp
        self.channels, self.images, self.small_images = channels, images, small_images
        self.slots = wide * images
        self.rows = channels * self.slots
        self.small_slots = wide * small_images
        self.small_rows = channels * self.small_slots
        self.piece_rows = 2 * channels * images
        self.pairs = images // PAIR
        self.outputs = 2 * channels
        self.vec_share = up_to(24, wide) // wide
        self.br = WIDTH // wide
        self.bh = self.br // 2
        self.bc = WIDTH // dp
        self.pair_rows = up_to(2 * self.br, 16)
        self.block_lanes = up_to(7 * self.bc, 128)
        self.head_rows = up_to(self.bh, 16)

    def block_places(self):
        br, bh, bc = self.br, self.bh, self.bc
        return (
            [(0, 6 * bc, bh, bc)],
            [(br, 0, br, 3 * bc)],
            [(br, 3 * bc, br, bc)],
            [(0, 0, br, 4 * bc)],
            [(0, 4 * bc, br, bc), (0, 5 * bc, br, bc), (br, 4 * bc, br, bc), (br, 5 * bc, br, bc)],
        )

    def pack_blocks(self, ref, blocks):
        for block, places in zip(blocks, self.block_places()):
            at = 0
            for row, lane, rows, lanes in places:
                ref[row : row + rows, lane : lane + lanes] = block[at : at + rows]
                at += rows

    def unpack_blocks(self, packed):
        result = []
        for places in self.block_places():
            parts = [packed[r : r + n, q : q + m] for r, q, n, m in places]
            result.append(parts[0] if len(parts) == 1 else jnp.concatenate(parts, 0))
        return result


def placements(order_big, order_small, sizes):
    n, m = sizes.slots, sizes.small_slots
    big = order_big[...] == lax.broadcasted_iota(jnp.int32, (n, n), 0)
    small = order_small[...] == lax.broadcasted_iota(jnp.int32, (m, m), 0)
    slot = lax.broadcasted_iota(jnp.int32, (m, n), 0)
    padded = lax.broadcasted_iota(jnp.int32, (m, n), 1)
    inside = padded % sizes.images
    spread_out = (slot == padded // sizes.images * sizes.small_images + inside) & (
        inside < sizes.small_images
    )
    one = lambda v: v.astype(jnp.float32).astype(jnp.bfloat16)
    return one(big), nn(one(small), one(spread_out)).astype(jnp.bfloat16)


def token_lanes(lens):
    low = lax.broadcasted_iota(jnp.int32, (1, LANES), 1)
    high = lax.broadcasted_iota(jnp.int32, (1, 128), 1) + 128
    return (low >= 1) & (low < lens[0]), (high > SPLIT) & (high < SPLIT + lens[1])


VM = pl.BlockSpec(memory_space=pltpu.VMEM)
SM = pl.BlockSpec(memory_space=pltpu.SMEM)
HB = pl.BlockSpec(memory_space=pl.ANY)
LIMIT = 62 * 1024 * 1024 + 512 * 1024


def dma_sems(*counts):
    return [pltpu.SemaphoreType.DMA((n,)) for n in counts]


class Names:
    def __init__(self, names, refs):
        self.__dict__.update(zip(names, refs))
        assert len(names) == len(refs), (len(names), len(refs))


IN_NAMES = [
    "act_small",
    "cls_big",
    "cls_small",
    "order_big",
    "order_small",
    "vec_s",
    "vec",
    "step",
    "perm",
    "table_small",
    "mh",
    "mqkv",
    "mp",
    "mu",
    "md",
    "sh",
    "sqkv",
    "sp",
    "su",
    "sd",
    "act_hbm",
    "table_hbm",
    "bcot_hbm",
    "scot_hbm",
    "binput_hbm",
    "bmodel_hbm",
    "bqkv_hbm",
    "bhidden_hbm",
]
OUT_NAMES = [
    "bout_hbm",
    "sout_hbm",
    "dact_hbm",
    "dsmall_hbm",
    "heads_big",
    "heads_small",
    "update",
    "states",
    "vtotal",
    "scalars",
]


def main_kernel(sizes, lens, scratch_names, *refs):
    bf16, f32 = jnp.bfloat16, jnp.float32
    r = Names(IN_NAMES + OUT_NAMES + scratch_names, refs)
    me_w, me_d = lax.axis_index("wide"), lax.axis_index("dp")
    n_w, n_d = sizes.wide, sizes.dp
    br, bh, bc = sizes.br, sizes.bh, sizes.bc
    half_w = n_w // 2
    partner = me_w + 1 - 2 * lax.rem(me_w, 2)
    n_big, n_small = sizes.slots, sizes.small_slots
    big_len, small_len = lens
    channels, images, outputs = sizes.channels, sizes.images, sizes.outputs

    loads = {}
    for at, name in enumerate(("act", "table", "bcot", "scot", "bmodel", "bhidden", "bqkv", "binput")):
        source = r.bhidden_hbm.at[1] if name == "bhidden" else getattr(r, name + "_hbm")
        loads[name] = pltpu.make_async_copy(source, getattr(r, name), r.load_sem.at[at])
        loads[name].start()

    r.stage_one[...] = jnp.zeros_like(r.stage_one)
    sizes.pack_blocks(
        r.stage_one, (r.mh[...], r.mqkv[...], r.mp[...], r.mu[...], jnp.transpose(r.md[...]))
    )
    r.got_all[me_w, me_d] = r.stage_one[...].astype(bf16)
    r.mpack[me_d] = jnp.zeros(r.mpack.shape[1:], f32)
    greet((("wide", n_w, me_w), ("dp", n_d, me_d)))

    def block_copy(row, column, target, send, recv):
        slot = r.got_all.at[row, column]
        return pltpu.make_async_remote_copy(
            src_ref=slot,
            dst_ref=slot,
            send_sem=send,
            recv_sem=recv,
            device_id=target,
            device_id_type=MESH,
        )

    columns = [lax.rem(me_d + n_d - k, n_d) for k in range(n_d)]
    same_core = [lax.rem(me_w + n_w - 2 * j, n_w) for j in range(half_w)]
    one = [
        block_copy(
            me_w, me_d, {"dp": lax.rem(me_d + k, n_d)}, r.one_send.at[k - 1], r.one_recv.at[k - 1]
        )
        for k in range(1, n_d)
    ]
    across = [
        [
            block_copy(
                me_w,
                columns[k],
                {"wide": lax.rem(me_w + 2 * j, n_w)},
                r.across_send.at[(j - 1) * n_d + k],
                r.across_recv.at[(j - 1) * n_d + k],
            )
            for j in range(1, half_w)
        ]
        for k in range(n_d)
    ]
    inside = [
        [
            block_copy(
                same_core[j],
                columns[k],
                {"wide": partner},
                r.inside_send.at[j * n_d + k],
                r.inside_recv.at[j * n_d + k],
            )
            for k in range(n_d)
        ]
        for j in range(half_w)
    ]
    begin(one)
    begin(across[0])
    inside[0][0].start()

    rows_small = r.act_small[...].reshape(sizes.small_rows, r.act_small.shape[2])

    def tap_value(row, c, e):
        return r.vec_s[row, 2 * (me_w * channels + c) + e]

    def pool(tap):
        rows_big = r.act[...].reshape(sizes.rows, r.act.shape[2])
        for rows, table, wins, sums, count in (
            (rows_big, r.table, r.wins_big, r.sum_big, n_big),
            (rows_small, r.table_small, r.wins_small, r.sum_small, n_small),
        ):
            win = nt(rows, table[tap])
            wins[tap] = win.astype(bf16)
            for c in range(channels):
                own = slice(c * count, (c + 1) * count)
                for e in range(2):
                    part = tap_value(tap, c, e) * win[own]
                    if tap == 0:
                        sums[e, own] = part
                    else:
                        sums[e, own] += part

    loads["act"].wait()
    loads["table"].wait()
    for tap in range(4):
        pool(tap)
    for k in range(1, n_d):
        one[k - 1].wait_recv()
        begin(across[k])
        inside[0][k].start()
    for tap in range(4, 9):
        pool(tap)

    put_big, put_small = placements(r.order_big, r.order_small, sizes)
    slot_big = jnp.transpose(put_big.astype(f32)).astype(bf16)
    slot_small = jnp.transpose(put_small.astype(f32)).astype(bf16)
    head_big, head_small = nt(slot_big, r.cls_big[...]), nt(slot_small, r.cls_small[...])
    token_big, token_small = token_lanes(lens)
    lane = lax.broadcasted_iota(jnp.int32, (1, 128), 1)
    for e in range(2):
        for c in range(channels):
            shift = tap_value(9, c, e)
            big = jnp.where(token_big, r.sum_big[e, c * n_big : (c + 1) * n_big] + shift, 0.0)
            small = jnp.where(
                token_small, r.sum_small[e, c * n_small : (c + 1) * n_small] + shift, 0.0
            )
            big = nn(slot_big, big.astype(bf16))
            low, high = big[:, 0:128], big[:, 128:256] + nn(slot_small, small.astype(bf16))
            if e == 0:
                low = jnp.where(lane == 0, head_big[:, c : c + 1], low)
                high = jnp.where(lane == SPLIT - 128, head_small[:, c : c + 1], high)
            at = (e * channels + c) * images
            for half, value in enumerate((low, high)):
                value = value.reshape(n_w, images, 128).astype(bf16)
                r.swap[:, at : at + images, half * 128 : half * 128 + 128] = value
    per_group = WIDTH // sizes.piece_rows
    piece = WIDTH // images
    for group in range(n_w // per_group):
        block = r.swap[group * per_group : (group + 1) * per_group].reshape(WIDTH, LANES)
        moved = tn(r.perm[...], block).astype(bf16).astype(f32)
        for i in range(images):
            for s in range(per_group):
                at, to = i * piece + s * outputs, i % PAIR * outputs
                r.pooled[i // PAIR, group * per_group + s, to : to + outputs] = moved[
                    at : at + outputs
                ].astype(bf16)

    def forward_links(p):
        return links(
            "wide",
            n_w,
            me_w,
            lambda peer: r.pooled.at[p, peer],
            r.received.at[p, me_w],
            r.act_send,
            r.act_recv,
            p * (n_w - 1),
        )

    def backward_links(p):
        return links(
            "wide",
            n_w,
            me_w,
            lambda peer: r.pooled.at[p, peer],
            r.returned.at[p, me_w],
            r.back_send,
            r.back_recv,
            p * (n_w - 1),
        )

    for p in range(sizes.pairs):
        begin(forward_links(p))
        r.received[p, me_w] = r.pooled[p, me_w]

    for half in range(2):
        sizes.pack_blocks(
            r.mpack.at[me_d, half],
            (r.sh[:, half, :], r.sqkv[half], r.sp[half], r.su[half], jnp.transpose(r.sd[half])),
        )
    moments = begin(
        links("dp", n_d, me_d, lambda p: r.mpack.at[me_d], r.mpack.at[me_d], r.mom_send, r.mom_recv)
    )

    def assemble(w, row):
        for d in range(n_d):
            head, qkv, proj, up, down = sizes.unpack_blocks(r.got_all[w, d].astype(f32))
            r.gu[row(br), d * 4 * bc : (d + 1) * 4 * bc] = up
            for part in range(3):
                low, high = d * 3 * bc, (d + 1) * 3 * bc
                a, b = max(low, part * WIDTH), min(high, (part + 1) * WIDTH)
                if a < b:
                    base = part * WIDTH
                    r.gqkv[part, row(br), a - base : b - base] = qkv[:, a - low : b - low]
            r.gp[row(br), d * bc : (d + 1) * bc] = proj
            r.dact[row(4 * br), d * bc : (d + 1) * bc] = down

    def at_row(w):
        return lambda size: pl.ds(pl.multiple_of(w * size, 8), size)

    aligned = br % 8 == 0
    if aligned:
        assemble(me_w, at_row(me_w))
    for j in range(1, half_w):
        for k in range(n_d):
            across[k][j - 1].wait_recv()
            inside[j][k].start()
        if aligned:
            assemble(same_core[j], at_row(same_core[j]))
    for name in ("bmodel", "bhidden", "bqkv", "binput"):
        loads[name].wait()
    for i in range(6):
        r.bmodel_low[i] = r.bmodel[i].astype(bf16)
    r.bhidden_low[1] = r.bhidden[...].astype(bf16)
    second_hidden = pltpu.make_async_copy(r.bhidden_hbm.at[0], r.bhidden, r.load_sem.at[8])
    second_hidden.start()
    r.bqkv_low[...] = r.bqkv[...].astype(bf16)
    r.binput_low[...] = r.binput[...].astype(bf16)
    for j in range(half_w):
        arrived(inside[j])
        if aligned:
            other = lax.rem(partner + n_w - 2 * j, n_w)
            assemble(other, at_row(other))
    for w in range(n_w):
        if not aligned:
            assemble(w, lambda size: slice(w * size, (w + 1) * size))
        row, lane_at, rows, lanes = sizes.block_places()[0][0]
        for d in range(n_d):
            piece = r.got_all[w, d].astype(f32)
            r.gh[w * bh : (w + 1) * bh, d * bc : (d + 1) * bc] = piece[
                row : row + rows, lane_at : lane_at + lanes
            ]
    even = (
        lax.broadcasted_iota(jnp.int32, (WIDTH // 2, WIDTH), 1)
        == 2 * lax.broadcasted_iota(jnp.int32, (WIDTH // 2, WIDTH), 0)
    ).astype(f32).astype(bf16)
    second_hidden.wait()
    r.bhidden_low[0] = r.bhidden[...].astype(bf16)
    r.wh[...] = tn(even, r.gh[0 : WIDTH // 2].astype(bf16)).astype(bf16)
    r.wqkv[...] = r.gqkv[...].astype(bf16)
    r.wp[...] = r.gp[...].astype(bf16)
    r.wu[...] = r.gu[...].astype(bf16)
    r.wd[...] = r.dact[:, 0:WIDTH].astype(bf16)
    sums = (r.gh, r.gqkv, r.gp, r.gu, r.gdt, r.gvec, r.gub)
    block_start(big_len, small_len, r.vec, sums, r.bias, r.cot, r.ubias)
    loads["bcot"].wait()
    loads["scot"].wait()

    def out_copy(p):
        at = pl.ds(p * PAIR, PAIR)
        return pltpu.make_async_copy(r.bout.at[at], r.bout_hbm.at[at], r.out_sem.at[p])

    @pl.loop(0, sizes.pairs)
    def _(p):
        arrived(forward_links(p))
        block = r.received[p].astype(f32)
        raw = [
            jnp.concatenate([block[w, j * outputs : (j + 1) * outputs] for w in range(n_w)], 0)
            for j in range(PAIR)
        ]
        raw = jnp.concatenate([jnp.transpose(v) for v in raw], 0)
        grad = block_step(
            p * PAIR,
            raw,
            (PAIR, sizes.small_images, big_len, small_len),
            r.bcot,
            r.scot,
            r.vec,
            (r.wh, r.wqkv, r.wp, r.wu, r.wd),
            r.bout,
            r.sout,
            sums,
            (r.probs, r.bias, r.cot, r.ubias),
        )
        sent(forward_links(p))
        for j in range(PAIR):
            turned = jnp.transpose(grad[j * LANES : (j + 1) * LANES])
            for w in range(n_w):
                r.pooled[p, w, j * outputs : (j + 1) * outputs] = turned[
                    w * outputs : (w + 1) * outputs
                ].astype(bf16)
        begin(backward_links(p))
        r.returned[p, me_w] = r.pooled[p, me_w]
        out_copy(p).start()

    small_out = pltpu.make_async_copy(
        r.sout.at[pl.ds(0, sizes.small_images)], r.sout_hbm, r.out_sem.at[sizes.pairs]
    )
    small_out.start()

    u_head = tn(r.binput_low[...], nn(even, r.gh[...].astype(bf16)).astype(bf16))
    u_qkv = [tn(r.bmodel_low[1], r.gqkv[part].astype(bf16)) for part in range(3)]
    u_proj = tn(r.bmodel_low[2], r.gp[...].astype(bf16))
    u_up = tn(r.bmodel_low[4], r.gu[...].astype(bf16))
    u_down = jnp.transpose(nn(r.gdt[...].astype(bf16), r.bhidden_low[1]))
    for copies in (*across, *inside):
        sent(copies)
    r.stage_two[...] = jnp.zeros_like(r.stage_two)
    r.stage_head[...] = jnp.zeros_like(r.stage_head)
    for w in range(n_w):
        at = w * br
        r.stage_two[0:br, 0 : 4 * WIDTH] = u_up[at : at + br]
        for part in range(2):
            r.stage_two[0:br, (4 + part) * WIDTH : (5 + part) * WIDTH] = u_qkv[part][at : at + br]
        r.stage_two[br : 2 * br, 0:WIDTH] = u_qkv[2][at : at + br]
        r.stage_two[br : 2 * br, WIDTH : 2 * WIDTH] = u_proj[at : at + br]
        for j in range(4):
            r.stage_two[br : 2 * br, (2 + j) * WIDTH : (3 + j) * WIDTH] = u_down[
                4 * at + j * br : 4 * at + (j + 1) * br
            ]
        r.stage_head[0:bh] = u_head[w * bh : (w + 1) * bh]
        r.rs_send[w] = r.stage_two[...].astype(bf16)
        r.rsh_send[w] = r.stage_head[...].astype(bf16)
    def pair_copy(source, target, send, recv):
        return pltpu.make_async_remote_copy(
            src_ref=source,
            dst_ref=target,
            send_sem=send,
            recv_sem=recv,
            device_id={"wide": partner},
            device_id_type=MESH,
        )

    buffers = ((r.rs_send, r.pair_got, r.rs_got), (r.rsh_send, r.pairh_got, r.rsh_got))
    targets = [lax.rem(me_w + 2 * j, n_w) for j in range(half_w)]
    pairs = begin(
        [
            pair_copy(
                source.at[lax.rem(partner + 2 * j, n_w)],
                got.at[j],
                r.pair_send.at[which * half_w + j],
                r.pair_recv.at[which * half_w + j],
            )
            for which, (source, got, _) in enumerate(buffers)
            for j in range(half_w)
        ]
    )

    for p in range(sizes.pairs):
        arrived(backward_links(p))
    for group in range(n_w // per_group):
        parts = [
            r.returned[i // PAIR, group * per_group + s].astype(f32)[
                i % PAIR * outputs : (i % PAIR + 1) * outputs
            ]
            for i in range(images)
            for s in range(per_group)
        ]
        moved = nn(r.perm[...], jnp.concatenate(parts, 0).astype(bf16))
        for s in range(per_group):
            for e in range(2):
                for c in range(channels):
                    at = s * sizes.piece_rows + (e * channels + c) * images
                    to = (c * n_w + group * per_group + s) * images
                    r.sum_big[e, to : to + images] = moved[at : at + images]

    arrived(pairs)
    first = []
    for j in range(1, half_w):
        for which, (source, got, final) in enumerate(buffers):
            source[targets[j]] = (source[targets[j]].astype(f32) + got[j].astype(f32)).astype(bf16)
            at = which * (half_w - 1) + j - 1
            first.append(
                pltpu.make_async_remote_copy(
                    src_ref=source.at[targets[j]],
                    dst_ref=final.at[j],
                    send_sem=r.first_send.at[at],
                    recv_sem=r.first_recv.at[at],
                    device_id={"wide": targets[j]},
                    device_id_type=MESH,
                )
            )
            first[-1].start()

    def fold(big, small):
        value = jnp.sum(big.reshape(n_big // 8, 8, LANES), 0)
        return value[:, 0:128] + value[:, 128:256] + jnp.sum(small.reshape(n_small // 8, 8, 128), 0)

    columns_big = jnp.zeros((n_big, 128), f32)
    columns_small = jnp.zeros((n_small, 128), f32)
    put_big, put_small = placements(r.order_big, r.order_small, sizes)
    for c in range(channels):
        own_big, own_small = slice(c * n_big, (c + 1) * n_big), slice(c * n_small, (c + 1) * n_small)
        group = slice(c * 8, (c + 1) * 8)
        pair = []
        for e in range(2):
            block = r.sum_big[e, own_big].astype(bf16)
            pair.append((nn(put_big, block), nn(put_small, block[:, 128:256])))
            r.taps[9, e, group] = fold(
                jnp.where(token_big, pair[e][0], 0.0), jnp.where(token_small, pair[e][1], 0.0)
            )
        columns_big = jnp.where(lane == c, pair[0][0][:, 0:1], columns_big)
        columns_small = jnp.where(lane == c, pair[0][1][:, SPLIT - 128 : SPLIT - 127], columns_small)
        for tap in range(9):
            big, small = r.wins_big[tap, own_big].astype(f32), r.wins_small[tap, own_small].astype(f32)
            for e in range(2):
                r.taps[tap, e, group] = fold(pair[e][0] * big, pair[e][1] * small)
            up, down = (tap_value(tap, c, e) for e in range(2))
            r.wins_big[tap, own_big] = (up * pair[0][0] + down * pair[1][0]).astype(bf16)
            r.wins_small[tap, own_small] = (up * pair[0][1] + down * pair[1][1]).astype(bf16)
    r.heads_big[...] = columns_big
    r.heads_small[...] = columns_small

    r.vpart[...] = jnp.zeros_like(r.vpart)
    half_rows = channels * 8
    own_channel = lax.broadcasted_iota(jnp.int32, (half_rows, WIDTH), 0) // 8
    own_lane = lax.broadcasted_iota(jnp.int32, (half_rows, WIDTH), 1)
    conv = jnp.zeros((128, WIDTH), f32)
    for e in range(2):
        place = (own_lane == 2 * (me_w * channels + own_channel) + e).astype(f32)
        part = jnp.zeros((half_rows, 128), f32)
        for tap in range(10):
            part = jnp.where(lane == tap, jnp.sum(r.taps[tap, e], -1, keepdims=True), part)
        conv += lax.dot_general(
            part,
            place,
            (((0,), (0,)), ((), ())),
            precision=lax.Precision.HIGHEST,
            preferred_element_type=f32,
        )
    r.vpart[0:10] = conv[0:10]
    r.vpart[10:19] = r.gvec[0:9]
    for j in range(4):
        r.vpart[19 + j : 20 + j] = r.gub[:, j * WIDTH : (j + 1) * WIDTH]
    r.v_send[...] = jnp.zeros_like(r.v_send)
    share = sizes.vec_share
    for w in range(n_w):
        r.v_send[w, 0:share] = r.vpart[w * share : (w + 1) * share]
    vec_one = begin(
        links("wide", n_w, me_w, lambda p: r.v_send.at[p], r.v_wide.at[me_w], r.v1_s, r.v1_r)
    )
    r.v_wide[me_w] = r.v_send[me_w]

    arrived(first)
    sums_two = []
    for source, got, final in buffers:
        rows = source[me_w].astype(f32) + got[0].astype(f32)
        for j in range(1, half_w):
            rows += final[j].astype(f32)
        sums_two.append(rows)
    rows_two, rows_head = sums_two
    rows_two = rows_two.astype(bf16)
    t_up = nn(rows_two[0:br, 0 : 4 * WIDTH], r.bhidden_low[0])
    t_qkv = nn(rows_two[0:br, 4 * WIDTH : 6 * WIDTH], r.bqkv_low[0 : 2 * WIDTH]) + nn(
        rows_two[br : 2 * br, 0:WIDTH], r.bqkv_low[2 * WIDTH :]
    )
    t_proj = nn(rows_two[br : 2 * br, WIDTH : 2 * WIDTH], r.bmodel_low[3])
    t_down = [
        nn(rows_two[br : 2 * br, (2 + j) * WIDTH : (3 + j) * WIDTH], r.bmodel_low[5])
        for j in range(4)
    ]
    t_head = nn(rows_head.astype(bf16), r.bmodel_low[0])
    for d in range(n_d):
        own = slice(d * bc, (d + 1) * bc)
        sizes.pack_blocks(
            r.stage_one,
            (
                t_head[0:bh, own],
                t_qkv[:, 3 * d * bc : 3 * (d + 1) * bc],
                t_proj[:, own],
                t_up[:, 4 * d * bc : 4 * (d + 1) * bc],
                jnp.concatenate([t[:, own] for t in t_down], 0),
            ),
        )
        r.t_send[d] = r.stage_one[...].astype(bf16)
    second = begin(
        links("dp", n_d, me_d, lambda p: r.t_send.at[p], r.t_got.at[me_d], r.t_ss, r.t_rs)
    )
    r.t_got[me_d] = r.t_send[me_d]
    arrived(vec_one)
    vsum = r.v_wide[0]
    for w in range(1, n_w):
        vsum += r.v_wide[w]
    r.v_dp[me_d] = vsum
    vec_two = begin(links("dp", n_d, me_d, lambda p: r.v_dp.at[me_d], r.v_dp.at[me_d], r.v2_s, r.v2_r))

    def act_part(chunk):
        at = pl.ds(chunk * 256, 256)
        table = r.table[...].reshape(9 * LANES, r.table.shape[2])
        mixed = jnp.concatenate([r.wins_big[tap, at, :] for tap in range(9)], 1)
        r.dact[at, :] = nn(mixed, table)
        copy = pltpu.make_async_copy(
            r.dact.at[at], r.dact_hbm.at[at], r.out_sem.at[sizes.pairs + 2 + chunk]
        )
        copy.start()
        return copy

    chunks = list(range(sizes.rows // 256))
    act_out = [act_part(chunk) for chunk in chunks[:1]]
    arrived(second)
    turned = r.t_got[0].astype(f32)
    for d in range(1, n_d):
        turned += r.t_got[d].astype(f32)
    r.full_got[me_d] = turned.astype(bf16)
    third = begin(
        links("dp", n_d, me_d, lambda p: r.full_got.at[me_d], r.full_got.at[me_d], r.d_s, r.d_r)
    )
    def total(value):
        return jnp.sum(jnp.sum(value * value, 0, keepdims=True), -1, keepdims=True)

    square = total(turned)
    arrived(vec_two)
    vsum = r.v_dp[0]
    for d in range(1, n_d):
        vsum += r.v_dp[d]
    last_row = lax.broadcasted_iota(jnp.int32, (8, WIDTH), 0) == 7
    r.s_wide[me_w] = jnp.where(last_row, square, vsum)
    fourth = begin(
        links("wide", n_w, me_w, lambda p: r.s_wide.at[me_w], r.s_wide.at[me_w], r.s_s, r.s_r)
    )
    act_out += [act_part(chunk) for chunk in chunks[1:2]]
    count = jnp.full((8, 128), r.step[0], jnp.int32).astype(f32)[0:1, 0:1]
    fix_one = 1.0 - jnp.exp(count * float(np.log(beta_one)))
    fix_two = 1.0 - jnp.exp(count * float(np.log(beta_two)))
    arrived(fourth)
    square = r.s_wide[0][7:8, 0:1]
    for w in range(1, n_w):
        square += r.s_wide[w][7:8, 0:1]
    r.s_dp[me_d] = jnp.broadcast_to(square, (8, 128))
    fifth = begin(links("dp", n_d, me_d, lambda p: r.s_dp.at[me_d], r.s_dp.at[me_d], r.s2_s, r.s2_r))
    vec_squares = jnp.zeros((8, WIDTH), f32)
    for w in range(n_w):
        part = jnp.where(last_row, 0.0, r.s_wide[w])
        vec_squares += part * part
        r.vtotal[w * share : (w + 1) * share] = part[0:share]
    vec_square = jnp.sum(jnp.sum(vec_squares, 0, keepdims=True), -1, keepdims=True)
    act_out += [act_part(chunk) for chunk in chunks[2:]]
    mixed = jnp.concatenate([r.wins_small[tap] for tap in range(9)], 1)
    r.dsmall[...] = nn(mixed, r.table_small[...].reshape(9 * 128, r.table_small.shape[2]))
    act_out.append(pltpu.make_async_copy(r.dsmall, r.dsmall_hbm, r.out_sem.at[sizes.pairs + 1]))
    act_out[-1].start()
    arrived(moments)
    arrived(third)
    arrived(fifth)
    square = vec_square
    for d in range(n_d):
        square += r.s_dp[d][0:1, 0:1]
    norm = jnp.sqrt(square)
    factor = jnp.minimum(1.0, clip_limit / (norm + 1e-06))
    which = lax.broadcasted_iota(jnp.int32, (8, 128), 1)
    r.scalars[...] = jnp.where(
        which == 0,
        norm,
        jnp.where(which == 1, factor, jnp.where(which == 2, fix_one, fix_two)),
    )

    def adam(gradient, old):
        scaled = gradient * factor
        moment = beta_one * old[0] + (1.0 - beta_one) * scaled
        second_moment = beta_two * old[1] * old[1] + (1.0 - beta_two) * scaled * scaled
        return moment, second_moment

    for d in range(n_d):
        moment, second_moment = adam(r.full_got[d].astype(f32), r.mpack[d])
        direction = moment / fix_one / (jnp.sqrt(second_moment / fix_two) + adam_eps)
        head, qkv, proj, up, down = sizes.unpack_blocks(direction)
        r.row_head[0:bh, d * bc : (d + 1) * bc] = head
        r.row_qkv[:, 3 * d * bc : 3 * (d + 1) * bc] = qkv
        r.row_proj[:, d * bc : (d + 1) * bc] = proj
        r.row_up[:, 4 * d * bc : 4 * (d + 1) * bc] = up
        r.row_down[:, d * bc : (d + 1) * bc] = down

    def right_rows(ref, size, unit=8):
        return ref[pl.ds(pl.multiple_of(me_d * size, unit), size), :].astype(bf16)

    sizes.pack_blocks(
        r.stage_one,
        (
            nt(r.row_head[...].astype(bf16), right_rows(r.bmodel.at[0], bc))[0:bh],
            nt(r.row_qkv[...].astype(bf16), right_rows(r.bqkv, 3 * bc)),
            nt(r.row_proj[...].astype(bf16), right_rows(r.bmodel.at[3], bc)),
            nt(r.row_up[...].astype(bf16), right_rows(r.bhidden_low.at[0], 4 * bc, 16)),
            nt(r.row_down[...].astype(bf16), right_rows(r.bmodel.at[5], bc)),
        ),
    )
    r.y_got[me_w] = r.stage_one[...].astype(bf16)
    y_across = begin(
        [
            pltpu.make_async_remote_copy(
                src_ref=r.y_got.at[me_w],
                dst_ref=r.y_got.at[me_w],
                send_sem=r.ya_send.at[j - 1],
                recv_sem=r.ya_recv.at[j - 1],
                device_id={"wide": targets[j]},
                device_id_type=MESH,
            )
            for j in range(1, half_w)
        ]
    )
    y_inside = [
        pair_copy(
            r.y_got.at[same_core[j]], r.y_got.at[same_core[j]], r.yi_send.at[j], r.yi_recv.at[j]
        )
        for j in range(half_w)
    ]
    y_inside[0].start()
    moment, second_moment = adam(turned, r.mpack[me_d])
    r.states[0] = moment
    r.states[1] = jnp.sqrt(second_moment)

    def left_rows(ref, size, unit=8):
        if size % unit == 0:
            return ref[pl.ds(pl.multiple_of(me_w * size, unit), size), :].astype(bf16)
        own = lax.broadcasted_iota(jnp.int32, (size, ref.shape[0]), 0) + me_w * size
        pick = own == lax.broadcasted_iota(jnp.int32, (size, ref.shape[0]), 1)
        return nn(pick.astype(f32).astype(bf16), ref[...].astype(bf16)).astype(bf16)

    lefts = (
        left_rows(r.binput, bh),
        left_rows(r.bmodel.at[1], br),
        left_rows(r.bmodel.at[2], br),
        left_rows(r.bmodel.at[4], br),
        left_rows(r.bhidden_low.at[1], 4 * br, 16),
    )
    r.update[...] = jnp.zeros_like(r.update)
    for j in range(1, half_w):
        y_across[j - 1].wait_recv()
        y_inside[j].start()
    arrived(y_inside)
    parts = [sizes.unpack_blocks(r.y_got[w].astype(f32)) for w in range(n_w)]
    sizes.pack_blocks(
        r.update,
        [
            nn(lefts[m], jnp.concatenate([part[m] for part in parts], 0).astype(bf16))
            for m in range(5)
        ],
    )
    for p in range(sizes.pairs):
        sent(backward_links(p))
        out_copy(p).wait()
    small_out.wait()
    for copy in act_out:
        copy.wait()
    for copies in (
        one,
        moments,
        pairs,
        first,
        vec_one,
        second,
        vec_two,
        third,
        fourth,
        fifth,
        y_across,
        y_inside,
    ):
        sent(copies)


def finish_kernel(
    sizes,
    mh,
    mqkv,
    mp,
    mu,
    md,
    vec,
    vmom,
    heads_big,
    heads_small,
    update,
    states,
    vtotal,
    scalars,
    big_from,
    small_from,
    act_from,
    act_small_from,
    big_to,
    small_to,
    act_to,
    act_small_to,
    dcls_big,
    dcls_small,
    norm,
    nvec,
    nvmom,
    *outs,
):
    outs, (hold_big, hold_small, hold_act, hold_act_small, sem) = outs[:-5], outs[-5:]
    moves = []
    for source, hold, target, parts in (
        (act_from, hold_act, act_to, 4),
        (big_from, hold_big, big_to, 4),
        (act_small_from, hold_act_small, act_small_to, 1),
        (small_from, hold_small, small_to, 1),
    ):
        size = source.shape[0] // parts
        for part in range(parts):
            at = pl.ds(part * size, size)
            pair = [(source.at[at], hold.at[at]), (hold.at[at], target.at[at])]
            moves.append(
                [
                    pltpu.make_async_copy(src, dst, sem.at[which, len(moves)])
                    for which, (src, dst) in enumerate(pair)
                ]
            )
    for move in moves:
        move[0].start()
    norm[0] = scalars[0, 0]
    factor, fix_one, fix_two = (scalars[0, j] for j in (1, 2, 3))
    for move in moves:
        move[0].wait()
        move[1].start()
    dcls_big[...] = jnp.transpose(heads_big[...])[0 : sizes.channels]
    dcls_small[...] = jnp.transpose(heads_small[...])[0 : sizes.channels]
    updates = sizes.unpack_blocks(update[...])
    firsts = sizes.unpack_blocks(states[0])
    seconds = sizes.unpack_blocks(states[1])
    for member, master in enumerate((mh, mqkv, mp, mu, md)):
        change, first, second = updates[member], firsts[member], seconds[member]
        if member == 4:
            change, first, second = (jnp.transpose(v) for v in (change, first, second))
        fresh = master[...] - rate_matrix * change
        outs[member][...] = fresh
        if member == 0:
            outs[5][:, 0, :] = first
            outs[5][:, 1, :] = second
        else:
            outs[5 + member][0] = first
            outs[5 + member][1] = second
        outs[10 + member][...] = fresh.astype(jnp.bfloat16)
    scaled = vtotal[0:23] * factor
    first = beta_one * vmom[:, 0, :] + (1.0 - beta_one) * scaled
    second = beta_two * vmom[:, 1, :] * vmom[:, 1, :] + (1.0 - beta_two) * scaled * scaled
    direction = first / fix_one / (jnp.sqrt(second / fix_two) + adam_eps)
    nvec[...] = vec[...] * (1.0 - rate_vector * decay_rate) - rate_vector * direction
    nvmom[:, 0, :] = first
    nvmom[:, 1, :] = jnp.sqrt(second)

    for move in moves:
        move[1].wait()


def run_main(sizes, lens, ins, hbm):
    bf16, f32 = jnp.bfloat16, jnp.float32
    w, d = sizes.wide, sizes.dp
    images, pairs = sizes.images, sizes.pairs
    act, table, bcot, scot, binput, bmodel, bqkv, bhidden = hbm
    table_small = ins[9]
    small_cells = table_small.shape[2]
    hidden = 4 * WIDTH
    vec_rows = w * sizes.vec_share
    pack = (sizes.pair_rows, sizes.block_lanes)
    two = (sizes.pair_rows, 6 * WIDTH)
    head = (sizes.head_rows, WIDTH)
    swap = (pairs, w, PAIR * sizes.outputs, LANES)
    big, small = sizes.rows, sizes.small_rows
    outs = [
        (bcot.shape, f32),
        (scot.shape, f32),
        ((big, act.shape[2]), f32),
        ((small, small_cells), f32),
        ((sizes.slots, 128), f32),
        ((sizes.small_slots, 128), f32),
        (pack, f32),
        ((2,) + pack, f32),
        ((vec_rows, WIDTH), f32),
        ((8, 128), f32),
    ]
    scratch = dict(
        act=(act.shape, bf16),
        table=(table.shape, bf16),
        bcot=(bcot.shape, bf16),
        scot=(scot.shape, bf16),
        binput=(binput.shape, f32),
        bmodel=(bmodel.shape, f32),
        bqkv=(bqkv.shape, f32),
        bhidden=(bhidden.shape[1:], f32),
        binput_low=(binput.shape, bf16),
        bmodel_low=(bmodel.shape, bf16),
        bqkv_low=(bqkv.shape, bf16),
        bhidden_low=(bhidden.shape, bf16),
        stage_one=(pack, f32),
        stage_two=(two, f32),
        stage_head=(head, f32),
        got_all=((w, d) + pack, bf16),
        rs_send=((w,) + two, bf16),
        rsh_send=((w,) + head, bf16),
        mpack=((d, 2) + pack, f32),
        wins_big=((9, big, LANES), bf16),
        wins_small=((9, small, 128), bf16),
        sum_big=((2, big, LANES), f32),
        sum_small=((2, small, 128), f32),
        swap=((w, sizes.piece_rows, LANES), bf16),
        pooled=(swap, bf16),
        received=(swap, bf16),
        returned=(swap, bf16),
        wh=((WIDTH, WIDTH), bf16),
        wqkv=((3, WIDTH, WIDTH), bf16),
        wp=((WIDTH, WIDTH), bf16),
        wu=((WIDTH, hidden), bf16),
        wd=((hidden, WIDTH), bf16),
        gh=((WIDTH, WIDTH), f32),
        gqkv=((3, WIDTH, WIDTH), f32),
        gp=((WIDTH, WIDTH), f32),
        gu=((WIDTH, hidden), f32),
        gdt=((WIDTH, hidden), f32),
        gvec=((16, WIDTH), f32),
        gub=((1, hidden), f32),
        probs=((PAIR, HEADS, LANES, LANES), f32),
        bias=((LANES, LANES), f32),
        cot=((PAIR * LANES, WIDTH), bf16),
        ubias=((1, hidden), f32),
        bout=(bcot.shape, f32),
        sout=((images,) + scot.shape[1:], f32),
        rs_got=((w // 2,) + two, bf16),
        pair_got=((w // 2,) + two, bf16),
        pairh_got=((w // 2,) + head, bf16),
        rsh_got=((w // 2,) + head, bf16),
        taps=((10, 2, sizes.channels * 8, 128), f32),
        dact=((big, act.shape[2]), f32),
        dsmall=((small, small_cells), f32),
        vpart=((vec_rows, WIDTH), f32),
        v_send=((w, 8, WIDTH), f32),
        v_wide=((w, 8, WIDTH), f32),
        v_dp=((d, 8, WIDTH), f32),
        t_send=((d,) + pack, bf16),
        t_got=((d,) + pack, bf16),
        full_got=((d,) + pack, bf16),
        s_wide=((w, 8, WIDTH), f32),
        s_dp=((d, 8, 128), f32),
        row_head=((sizes.bh, WIDTH), f32),
        row_qkv=((sizes.br, 3 * WIDTH), f32),
        row_proj=((sizes.br, WIDTH), f32),
        row_up=((sizes.br, hidden), f32),
        row_down=((4 * sizes.br, WIDTH), f32),
        y_got=((w,) + pack, bf16),
    )
    sems = dict(
        load_sem=9,
        out_sem=pairs + 2 + big // 256,
        one_send=d - 1,
        one_recv=d - 1,
        across_send=(w // 2 - 1) * d,
        across_recv=(w // 2 - 1) * d,
        inside_send=w // 2 * d,
        inside_recv=w // 2 * d,
        act_send=pairs * (w - 1),
        act_recv=pairs * (w - 1),
        back_send=pairs * (w - 1),
        back_recv=pairs * (w - 1),
        mom_send=d - 1,
        pair_send=w,
        pair_recv=w,
        first_send=w - 2,
        first_recv=w - 2,
        ya_send=w // 2 - 1,
        ya_recv=w // 2 - 1,
        yi_send=w // 2,
        yi_recv=w // 2,
        mom_recv=d - 1,
    )
    for name in ("v1_s", "v1_r", "s_s", "s_r"):
        sems[name] = w - 1
    for name in ("t_ss", "t_rs", "v2_s", "v2_r", "d_s", "d_r", "s2_s", "s2_r"):
        sems[name] = d - 1
    return pl.pallas_call(
        partial(main_kernel, sizes, lens, list(scratch) + list(sems)),
        in_specs=[VM] * 5 + [SM, VM, SM] + [VM] * 12 + [HB] * 8,
        out_specs=[HB] * 4 + [VM] * 6,
        out_shape=[jax.ShapeDtypeStruct(s, t) for s, t in outs],
        scratch_shapes=[pltpu.VMEM(s, t) for s, t in scratch.values()] + dma_sems(*sems.values()),
        compiler_params=pltpu.CompilerParams(
            collective_id=0, has_side_effects=True, vmem_limit_bytes=LIMIT
        ),
        name="main",
    )(*ins, *hbm)


def run_finish(sizes, masters, vec, vmom, moments, heads, packs, large):
    f32, bf16 = jnp.float32, jnp.bfloat16
    shapes = [m.shape for m in masters]
    outs = [(a.shape, f32) for a in large]
    outs += [((sizes.channels, h.shape[0]), f32) for h in heads]
    outs += [((1,), f32), (vec.shape, f32), (vmom.shape, f32)]
    outs += [(s, f32) for s in shapes] + [(m.shape, f32) for m in moments]
    outs += [(s, bf16) for s in shapes]
    return pl.pallas_call(
        partial(finish_kernel, sizes),
        in_specs=[VM] * 12 + [SM] + [HB] * 4,
        out_specs=[HB] * 4 + [VM, VM, SM] + [VM] * (len(outs) - 7),
        out_shape=[jax.ShapeDtypeStruct(s, t) for s, t in outs],
        scratch_shapes=[pltpu.VMEM(large[i].shape, f32) for i in range(4)]
        + [pltpu.SemaphoreType.DMA((2, 10))],
        compiler_params=pltpu.CompilerParams(vmem_limit_bytes=LIMIT),
        name="finish",
    )(*masters, vec, vmom, *heads, *packs, *large)


def pool_table(grid, side, lane, lanes):
    table = np.zeros((9, lanes, grid * grid), np.float32)
    for tap in range(9):
        for y in range(side):
            for x in range(side):
                sy, sx = 2 * y + tap // 3 - 1, 2 * x + tap % 3 - 1
                if 0 <= sy < grid and 0 <= sx < grid:
                    table[tap, lane + y * side + x, sy * grid + sx] = 1.0
    return jnp.asarray(table, jnp.bfloat16)


def per_device(
    wide_n,
    dp_n,
    big_act,
    big_cls,
    small_act,
    small_cls,
    big_order,
    small_order,
    big_cot,
    small_cot,
    vec_params,
    vec_moments,
    *rest,
):
    masters, moments, bases, step = list(rest[0:5]), list(rest[5:10]), rest[10:14], rest[14]
    channels = big_act.shape[1]
    images, small_images = big_cot.shape[0], small_cot.shape[0]
    lens = (big_cot.shape[1], small_cot.shape[1])
    sizes = Sizes(wide_n, dp_n, channels, images, small_images)
    side = lambda cells: round(cells**0.5)
    tables = (
        pool_table(side(big_act.shape[2]), side(lens[0] - 1), 1, LANES),
        pool_table(side(small_act.shape[2]), side(lens[1] - 1), SPLIT + 1 - 128, 128),
    )
    perm = row_permutation(channels, images)
    flip = lambda a, i, j: jnp.swapaxes(a, i, j)
    acts = [flip(a, 0, 1) for a in (big_act, small_act, big_cls, small_cls)]
    orders = (big_order, small_order)
    masters[4] = flip(masters[4], 0, 1)
    moments[0], moments[4] = flip(moments[0], 0, 1), flip(moments[4], 1, 2)
    vec_moments = flip(vec_moments, 0, 1)

    ins = (*acts[1:], *orders, vec_params, vec_params, step, perm, tables[1], *masters, *moments)
    hbm = (acts[0], tables[0], flip(big_cot, 1, 2), small_cot, *bases)
    *large, heads_big, heads_small, update, states, vtotal, scalars = run_main(
        sizes, lens, ins, hbm
    )
    packs = (update, states, vtotal, scalars)
    results = list(
        run_finish(
            sizes, masters, vec_params, vec_moments, moments, (heads_big, heads_small), packs, large
        )
    )
    big_out, small_out, dact_big, dact_small = results[0:4]
    results = results[4:]
    cls_big, cls_small, norm, new_vec, new_vec_moments = results[0:5]
    masters, moments, copies = results[5:10], results[10:15], results[15:20]
    masters[4], copies[4] = flip(masters[4], 0, 1), flip(copies[4], 0, 1)
    moments[0], moments[4] = flip(moments[0], 0, 1), flip(moments[4], 1, 2)
    return (
        flip(big_out, 1, 2),
        small_out,
        flip(dact_big.reshape(channels, sizes.slots, -1), 0, 1),
        flip(cls_big, 0, 1),
        flip(dact_small.reshape(channels, sizes.small_slots, -1), 0, 1),
        flip(cls_small, 0, 1),
        norm,
        new_vec,
        flip(new_vec_moments, 0, 1),
        *masters,
        *moments,
        *copies,
    )


def solution(mesh):
    split, wide_first, free = P("dp", "wide", None), P("wide", "dp"), P()
    moment = P(None, "wide", "dp")
    both = P(("dp", "wide"), None, None)
    acts = (split, P("dp", "wide"), split, P("dp", "wide"))
    in_specs = (
        acts
        + (P("dp", None), P("dp", None), both, both, free, free)
        + (wide_first,) * 5
        + (moment,) * 5
        + (free,) * 5
    )
    out_specs = (
        (both, both) + acts + (free,) * 3 + (wide_first,) * 5 + (moment,) * 5 + (wide_first,) * 5
    )
    return jax.shard_map(
        partial(per_device, mesh.shape["wide"], mesh.shape["dp"]),
        mesh=mesh,
        in_specs=in_specs,
        out_specs=out_specs,
        check_vma=False,
    )
```

```python
from functools import partial

import jax
import jax.numpy as jnp
import numpy as np
from jax import lax
from jax.experimental import pallas as pl
from jax.experimental.pallas import tpu as pltpu
from jax.sharding import PartitionSpec as P

HEADS = 4
HD = 48
beta_one = 0.9
beta_two = 0.999
adam_eps = 1e-08
norm_eps = 1e-06
rate_matrix = 0.08
rate_vector = 0.25
decay_rate = 0.05
clip_limit = 1.0
LANES = 256
SPLIT = 208
SCORE_SCALE = float(HD ** (-0.5) * np.log2(np.e))


def nt(a, b):
    return lax.dot_general(a, b, (((1,), (1,)), ((), ())), preferred_element_type=jnp.float32)


def tn(a, b):
    return lax.dot_general(a, b, (((0,), (0,)), ((), ())), preferred_element_type=jnp.float32)


def nn(a, b):
    return jnp.dot(a, b, preferred_element_type=jnp.float32)


def colsum(v):
    return jnp.sum(v, 0, keepdims=True)


def norm_forward(rows, gain, shift):
    centered = rows - jnp.mean(rows, -1, keepdims=True)
    scale = lax.rsqrt(jnp.mean(centered * centered, -1, keepdims=True) + norm_eps)
    hat = centered * scale
    return hat, scale, (hat * gain + shift).astype(jnp.bfloat16)


def norm_backward(grad, hat, scale, gain):
    inner = grad * gain
    mean_a = jnp.mean(inner, -1, keepdims=True)
    mean_b = jnp.mean(inner * hat, -1, keepdims=True)
    return scale * (inner - mean_a - hat * mean_b)


def block_start(big_len, small_len, vec, sums, bias, cot, ubias):
    for ref in sums:
        ref[...] = jnp.zeros_like(ref)
    cot[...] = jnp.zeros_like(cot)
    width = vec.shape[1]
    for j in range(4):
        ubias[:, j * width : (j + 1) * width] = vec[19 + j : 20 + j]
    key_id = lax.broadcasted_iota(jnp.int32, (LANES, LANES), 1)
    query_id = lax.broadcasted_iota(jnp.int32, (LANES, LANES), 0)
    keep_big = (query_id < SPLIT) & (key_id < big_len)
    keep_small = (query_id >= SPLIT) & (key_id >= SPLIT) & (key_id < SPLIT + small_len)
    bias[...] = jnp.where(keep_big | keep_small, 0.0, -1e30)


def block_step(image, raw, counts, bcot, scot, vec, weights, bout, sout, sums, scratch):
    pair, small_n, big_len, small_len = counts
    wh, wqkv, wp, wu, wd = weights
    gh, gqkv, gp, gu, gdt, gvec, gub = sums
    probs, bias, cot, ubias = scratch
    width = vec.shape[1]
    row_id = lax.broadcasted_iota(jnp.int32, (pair * LANES, 1), 0) % LANES
    lane_id = lax.broadcasted_iota(jnp.int32, (1, width), 1)
    for j in range(pair):
        base = j * LANES
        turned = jnp.transpose(bcot[image + j].astype(jnp.float32))
        cot[base : base + big_len] = turned.astype(jnp.bfloat16)
        small = scot[jnp.minimum(image + j, small_n - 1)].astype(jnp.float32)
        small = jnp.where(image + j < small_n, small, 0.0).astype(jnp.bfloat16)
        cot[base + SPLIT : base + SPLIT + small_len] = small
    raw_low = raw.astype(jnp.bfloat16)
    is_head = (row_id == 0) | (row_id == SPLIT)
    rows = jnp.where(is_head, nn(raw_low, wh[...]) + vec[10:11], raw)
    hat_one, scale_one, normed_one = norm_forward(rows, vec[11:12], vec[12:13])
    queries = (nn(normed_one, wqkv[0]) + vec[13:14]).astype(jnp.bfloat16)
    keys_in = nn(normed_one, wqkv[1]).astype(jnp.bfloat16)
    values = (nn(normed_one, wqkv[2]) + vec[14:15]).astype(jnp.bfloat16)
    zero = jnp.zeros((), jnp.bfloat16)
    in_head = [(lane_id >= h * HD) & (lane_id < (h + 1) * HD) for h in range(HEADS)]
    tiles = [slice(j * LANES, (j + 1) * LANES) for j in range(pair)]
    chains = [(j, h) for h in range(HEADS) for j in range(pair)]
    scores = {
        (j, h): nt(jnp.where(in_head[h], queries[tiles[j]], zero), keys_in[tiles[j]])
        for j, h in chains
    }
    low = {}
    for j, h in chains:
        value = scores[j, h] + bias[...]
        weights = jnp.exp2((value - jnp.max(value, -1, keepdims=True)) * SCORE_SCALE)
        probas = weights * (1.0 / jnp.sum(weights, -1, keepdims=True))
        probs[j, h] = probas
        low[j, h] = probas.astype(jnp.bfloat16)
    mixture = [
        nn(
            jnp.concatenate([low[j, h] for h in range(HEADS)], 1),
            jnp.concatenate([jnp.where(in_head[h], values[tiles[j]], zero) for h in range(HEADS)], 0),
        )
        for j in range(pair)
    ]
    mixture = jnp.concatenate(mixture, 0)
    mixture = mixture.astype(jnp.bfloat16)
    middle = rows + nn(mixture, wp[...]) + vec[15:16]
    hat_two, scale_two, normed_two = norm_forward(middle, vec[16:17], vec[17:18])
    pre = nn(normed_two, wu[...]) + ubias[...]
    cdf = 0.5 + 0.5 * lax.erf(pre * 0.7071067811865476)
    slope = cdf + pre * jnp.exp(pre * pre * -0.5) * 0.3989422804014327
    active = (pre * cdf).astype(jnp.bfloat16)
    result = middle + nn(active, wd[...]) + vec[18:19]
    for j in range(pair):
        bout[image + j] = jnp.transpose(result[tiles[j]])[:, :big_len]
        base = j * LANES + SPLIT
        sout[image + j] = result[base : base + small_len]
    cot_low = cot[...]
    cot_rows = cot_low.astype(jnp.float32)
    gdt[...] += tn(cot_low, active)
    gvec[8:9] += colsum(cot_rows)
    grad_pre = (nt(cot_low, wd[...]) * slope).astype(jnp.bfloat16)
    gu[...] += tn(normed_two, grad_pre)
    gub[...] += colsum(grad_pre.astype(jnp.float32))
    grad_two = nt(grad_pre, wu[...])
    gvec[6:7] += colsum(grad_two * hat_two)
    gvec[7:8] += colsum(grad_two)
    grad_mid = norm_backward(grad_two, hat_two, scale_two, vec[16:17]) + cot_rows
    branch = grad_mid.astype(jnp.bfloat16)
    gp[...] += tn(mixture, branch)
    gvec[5:6] += colsum(branch.astype(jnp.float32))
    grad_mix = nt(branch, wp[...]).astype(jnp.bfloat16)
    own = {(j, h): jnp.where(in_head[h], grad_mix[tiles[j]], zero) for j, h in chains}
    grad_probs = {(j, h): nt(own[j, h], values[tiles[j]]) for j, h in chains}
    grad_scores = {}
    for j, h in chains:
        probas = probs[j, h]
        inner = jnp.sum(probas * grad_probs[j, h], -1, keepdims=True)
        grad_scores[j, h] = (probas * (grad_probs[j, h] - inner)).astype(jnp.bfloat16)
    stack = lambda source: [
        jnp.concatenate([jnp.where(in_head[h], source[tile], zero) for h in range(HEADS)], 0)
        for tile in tiles
    ]
    wide_keys, wide_queries = stack(keys_in), stack(queries)
    all_scores = [jnp.concatenate([grad_scores[j, h] for h in range(HEADS)], 1) for j in range(pair)]
    tall_scores = [jnp.concatenate([grad_scores[j, h] for h in range(HEADS)], 0) for j in range(pair)]
    tall_probs = [
        jnp.concatenate([probs[j, h].astype(jnp.bfloat16) for h in range(HEADS)], 0)
        for j in range(pair)
    ]
    tall_own = [jnp.concatenate([own[j, h] for h in range(HEADS)], 0) for j in range(pair)]
    grad_q = jnp.concatenate([nn(all_scores[j], wide_keys[j]) for j in range(pair)], 0)
    grad_k = jnp.concatenate([tn(tall_scores[j], wide_queries[j]) for j in range(pair)], 0)
    grad_v = jnp.concatenate([tn(tall_probs[j], tall_own[j]) for j in range(pair)], 0)
    grad_q = (grad_q * HD ** (-0.5)).astype(jnp.bfloat16)
    grad_k = (grad_k * HD ** (-0.5)).astype(jnp.bfloat16)
    grad_v = grad_v.astype(jnp.bfloat16)
    gqkv[0] += tn(normed_one, grad_q)
    gqkv[1] += tn(normed_one, grad_k)
    gqkv[2] += tn(normed_one, grad_v)
    gvec[3:4] += colsum(grad_q.astype(jnp.float32))
    gvec[4:5] += colsum(grad_v.astype(jnp.float32))
    grad_one = nt(grad_q, wqkv[0]) + nt(grad_k, wqkv[1]) + nt(grad_v, wqkv[2])
    gvec[1:2] += colsum(grad_one * hat_one)
    gvec[2:3] += colsum(grad_one)
    grad_tok = norm_backward(grad_one, hat_one, scale_one, vec[11:12]) + grad_mid
    grad_head = jnp.where(is_head, grad_tok, 0.0).astype(jnp.bfloat16)
    gh[...] += tn(raw_low, grad_head)
    gvec[0:1] += colsum(grad_head.astype(jnp.float32))
    return jnp.where(is_head, nt(grad_head, wh[...]), grad_tok)


def row_permutation(channels, images):
    width = 192
    group = width // (2 * channels * images)
    table = np.zeros((width, width), np.float32)
    for s in range(group):
        for e in range(2):
            for c in range(channels):
                for i in range(images):
                    row = ((s * 2 + e) * channels + c) * images + i
                    table[row, i * (width // images) + s * 2 * channels + 2 * c + e] = 1.0
    return jnp.asarray(table, jnp.bfloat16)
MESH = pl.DeviceIdType.MESH
WIDTH = 192
PAIR = 2


def up_to(value, unit):
    return -(-value // unit) * unit


def links(axis, count, me, src_of, dst, send, recv, base=0):
    copies = []
    for k in range(1, count):
        peer = lax.rem(me + k, count)
        copies.append(
            pltpu.make_async_remote_copy(
                src_ref=src_of(peer),
                dst_ref=dst,
                send_sem=send.at[base + k - 1],
                recv_sem=recv.at[base + k - 1],
                device_id={axis: peer},
                device_id_type=MESH,
            )
        )
    return copies


def begin(copies):
    for copy in copies:
        copy.start()
    return copies


def arrived(copies):
    for copy in copies:
        copy.wait_recv()


def sent(copies):
    for copy in copies:
        copy.wait_send()


def greet(axes):
    barrier = pltpu.get_barrier_semaphore()
    total = 0
    for axis, count, me in axes:
        for k in range(1, count):
            pl.semaphore_signal(
                barrier,
                inc=1,
                device_id={axis: lax.rem(me + k, count)},
                device_id_type=MESH,
            )
        total += count - 1
    return lambda: pl.semaphore_wait(barrier, total)


class Sizes:
    def __init__(self, wide, dp, channels, images, small_images):
        self.wide, self.dp = wide, dp
        self.channels, self.images, self.small_images = channels, images, small_images
        self.slots = wide * images
        self.rows = channels * self.slots
        self.small_slots = wide * small_images
        self.small_rows = channels * self.small_slots
        self.piece_rows = 2 * channels * images
        self.pairs = images // PAIR
        self.outputs = 2 * channels
        self.vec_share = up_to(24, wide) // wide
        self.br = WIDTH // wide
        self.bh = self.br // 2
        self.bc = WIDTH // dp
        self.pair_rows = up_to(2 * self.br, 16)
        self.block_lanes = up_to(7 * self.bc, 128)
        self.head_rows = up_to(self.bh, 16)

    def block_places(self):
        br, bh, bc = self.br, self.bh, self.bc
        return (
            [(0, 6 * bc, bh, bc)],
            [(br, 0, br, 3 * bc)],
            [(br, 3 * bc, br, bc)],
            [(0, 0, br, 4 * bc)],
            [(0, 4 * bc, br, bc), (0, 5 * bc, br, bc), (br, 4 * bc, br, bc), (br, 5 * bc, br, bc)],
        )

    def pack_blocks(self, ref, blocks):
        for block, places in zip(blocks, self.block_places()):
            at = 0
            for row, lane, rows, lanes in places:
                ref[row : row + rows, lane : lane + lanes] = block[at : at + rows]
                at += rows

    def unpack_blocks(self, packed):
        result = []
        for places in self.block_places():
            parts = [packed[r : r + n, q : q + m] for r, q, n, m in places]
            result.append(parts[0] if len(parts) == 1 else jnp.concatenate(parts, 0))
        return result


def placements(order_big, order_small, sizes):
    n, m = sizes.slots, sizes.small_slots
    big = order_big[...] == lax.broadcasted_iota(jnp.int32, (n, n), 0)
    small = order_small[...] == lax.broadcasted_iota(jnp.int32, (m, m), 0)
    slot = lax.broadcasted_iota(jnp.int32, (m, n), 0)
    padded = lax.broadcasted_iota(jnp.int32, (m, n), 1)
    inside = padded % sizes.images
    spread_out = (slot == padded // sizes.images * sizes.small_images + inside) & (
        inside < sizes.small_images
    )
    one = lambda v: v.astype(jnp.float32).astype(jnp.bfloat16)
    return one(big), nn(one(small), one(spread_out)).astype(jnp.bfloat16)


def token_lanes(lens):
    low = lax.broadcasted_iota(jnp.int32, (1, LANES), 1)
    high = lax.broadcasted_iota(jnp.int32, (1, 128), 1) + 128
    return (low >= 1) & (low < lens[0]), (high > SPLIT) & (high < SPLIT + lens[1])


VM = pl.BlockSpec(memory_space=pltpu.VMEM)
SM = pl.BlockSpec(memory_space=pltpu.SMEM)
HB = pl.BlockSpec(memory_space=pl.ANY)
LIMIT = 62 * 1024 * 1024 + 512 * 1024


def dma_sems(*counts):
    return [pltpu.SemaphoreType.DMA((n,)) for n in counts]


class Names:
    def __init__(self, names, refs):
        self.__dict__.update(zip(names, refs))
        assert len(names) == len(refs), (len(names), len(refs))


IN_NAMES = [
    "act_small",
    "cls_big",
    "cls_small",
    "order_big",
    "order_small",
    "vec_s",
    "vec",
    "step",
    "perm",
    "table_small",
    "mh",
    "mqkv",
    "mp",
    "mu",
    "md",
    "sh",
    "sqkv",
    "sp",
    "su",
    "sd",
    "act_hbm",
    "table_hbm",
    "bcot_hbm",
    "scot_hbm",
    "binput_hbm",
    "bmodel_hbm",
    "bqkv_hbm",
    "bhidden_hbm",
]
OUT_NAMES = [
    "bout_hbm",
    "sout_hbm",
    "dact_hbm",
    "dsmall_hbm",
    "heads_big",
    "heads_small",
    "update",
    "states",
    "vtotal",
    "scalars",
]


def main_kernel(sizes, lens, scratch_names, *refs):
    bf16, f32 = jnp.bfloat16, jnp.float32
    r = Names(IN_NAMES + OUT_NAMES + scratch_names, refs)
    me_w, me_d = lax.axis_index("wide"), lax.axis_index("dp")
    n_w, n_d = sizes.wide, sizes.dp
    br, bh, bc = sizes.br, sizes.bh, sizes.bc
    half_w = n_w // 2
    partner = me_w + 1 - 2 * lax.rem(me_w, 2)
    n_big, n_small = sizes.slots, sizes.small_slots
    big_len, small_len = lens
    channels, images, outputs = sizes.channels, sizes.images, sizes.outputs

    everybody_here = greet((("wide", n_w, me_w), ("dp", n_d, me_d)))
    loads = {}
    for at, name in enumerate(("act", "table", "bcot", "scot", "bmodel", "bhidden", "bqkv", "binput")):
        source = r.bhidden_hbm.at[1] if name == "bhidden" else getattr(r, name + "_hbm")
        loads[name] = pltpu.make_async_copy(source, getattr(r, name), r.load_sem.at[at])
        loads[name].start()

    r.stage_one[...] = jnp.zeros_like(r.stage_one)
    sizes.pack_blocks(
        r.stage_one, (r.mh[...], r.mqkv[...], r.mp[...], r.mu[...], jnp.transpose(r.md[...]))
    )
    r.got_all[me_w, me_d] = r.stage_one[...].astype(bf16)
    r.mpack[me_d] = jnp.zeros(r.mpack.shape[1:], f32)
    def block_copy(row, column, target, send, recv):
        slot = r.got_all.at[row, column]
        return pltpu.make_async_remote_copy(
            src_ref=slot,
            dst_ref=slot,
            send_sem=send,
            recv_sem=recv,
            device_id=target,
            device_id_type=MESH,
        )

    columns = [lax.rem(me_d + n_d - k, n_d) for k in range(n_d)]
    same_core = [lax.rem(me_w + n_w - 2 * j, n_w) for j in range(half_w)]
    one = [
        block_copy(
            me_w, me_d, {"dp": lax.rem(me_d + k, n_d)}, r.one_send.at[k - 1], r.one_recv.at[k - 1]
        )
        for k in range(1, n_d)
    ]
    across = [
        [
            block_copy(
                me_w,
                columns[k],
                {"wide": lax.rem(me_w + 2 * j, n_w)},
                r.across_send.at[(j - 1) * n_d + k],
                r.across_recv.at[(j - 1) * n_d + k],
            )
            for j in range(1, half_w)
        ]
        for k in range(n_d)
    ]
    inside = [
        [
            block_copy(
                same_core[j],
                columns[k],
                {"wide": partner},
                r.inside_send.at[j * n_d + k],
                r.inside_recv.at[j * n_d + k],
            )
            for k in range(n_d)
        ]
        for j in range(half_w)
    ]
    everybody_here()
    begin(one)
    begin(across[0])
    inside[0][0].start()

    rows_small = r.act_small[...].reshape(sizes.small_rows, r.act_small.shape[2])

    def tap_value(row, c, e):
        return r.vec_s[row, 2 * (me_w * channels + c) + e]

    def pool(tap):
        rows_big = r.act[...].reshape(sizes.rows, r.act.shape[2])
        for rows, table, wins, sums, count in (
            (rows_big, r.table, r.wins_big, r.sum_big, n_big),
            (rows_small, r.table_small, r.wins_small, r.sum_small, n_small),
        ):
            win = nt(rows, table[tap])
            wins[tap] = win.astype(bf16)
            for c in range(channels):
                own = slice(c * count, (c + 1) * count)
                for e in range(2):
                    part = tap_value(tap, c, e) * win[own]
                    if tap == 0:
                        sums[e, own] = part
                    else:
                        sums[e, own] += part

    loads["act"].wait()
    loads["table"].wait()
    for tap in range(4):
        pool(tap)
    for k in range(1, n_d):
        one[k - 1].wait_recv()
        begin(across[k])
        inside[0][k].start()
    for tap in range(4, 9):
        pool(tap)

    put_big, put_small = placements(r.order_big, r.order_small, sizes)
    slot_big = jnp.transpose(put_big.astype(f32)).astype(bf16)
    slot_small = jnp.transpose(put_small.astype(f32)).astype(bf16)
    head_big, head_small = nt(slot_big, r.cls_big[...]), nt(slot_small, r.cls_small[...])
    token_big, token_small = token_lanes(lens)
    lane = lax.broadcasted_iota(jnp.int32, (1, 128), 1)
    for e in range(2):
        for c in range(channels):
            shift = tap_value(9, c, e)
            big = jnp.where(token_big, r.sum_big[e, c * n_big : (c + 1) * n_big] + shift, 0.0)
            small = jnp.where(
                token_small, r.sum_small[e, c * n_small : (c + 1) * n_small] + shift, 0.0
            )
            big = nn(slot_big, big.astype(bf16))
            low, high = big[:, 0:128], big[:, 128:256] + nn(slot_small, small.astype(bf16))
            if e == 0:
                low = jnp.where(lane == 0, head_big[:, c : c + 1], low)
                high = jnp.where(lane == SPLIT - 128, head_small[:, c : c + 1], high)
            at = (e * channels + c) * images
            for half, value in enumerate((low, high)):
                value = value.reshape(n_w, images, 128).astype(bf16)
                r.swap[:, at : at + images, half * 128 : half * 128 + 128] = value
    per_group = WIDTH // sizes.piece_rows
    piece = WIDTH // images
    for group in range(n_w // per_group):
        block = r.swap[group * per_group : (group + 1) * per_group].reshape(WIDTH, LANES)
        moved = tn(r.perm[...], block).astype(bf16).astype(f32)
        for i in range(images):
            for s in range(per_group):
                at, to = i * piece + s * outputs, i % PAIR * outputs
                r.pooled[i // PAIR, group * per_group + s, to : to + outputs] = moved[
                    at : at + outputs
                ].astype(bf16)

    def forward_links(p):
        return links(
            "wide",
            n_w,
            me_w,
            lambda peer: r.pooled.at[p, peer],
            r.received.at[p, me_w],
            r.act_send,
            r.act_recv,
            p * (n_w - 1),
        )

    def backward_links(p):
        return links(
            "wide",
            n_w,
            me_w,
            lambda peer: r.pooled.at[p, peer],
            r.returned.at[p, me_w],
            r.back_send,
            r.back_recv,
            p * (n_w - 1),
        )

    for p in range(sizes.pairs):
        begin(forward_links(p))
        r.received[p, me_w] = r.pooled[p, me_w]

    for half in range(2):
        sizes.pack_blocks(
            r.mpack.at[me_d, half],
            (r.sh[:, half, :], r.sqkv[half], r.sp[half], r.su[half], jnp.transpose(r.sd[half])),
        )
    moments = begin(
        links("dp", n_d, me_d, lambda p: r.mpack.at[me_d], r.mpack.at[me_d], r.mom_send, r.mom_recv)
    )

    def assemble(w, row):
        for d in range(n_d):
            head, qkv, proj, up, down = sizes.unpack_blocks(r.got_all[w, d].astype(f32))
            r.gu[row(br), d * 4 * bc : (d + 1) * 4 * bc] = up
            for part in range(3):
                low, high = d * 3 * bc, (d + 1) * 3 * bc
                a, b = max(low, part * WIDTH), min(high, (part + 1) * WIDTH)
                if a < b:
                    base = part * WIDTH
                    r.gqkv[part, row(br), a - base : b - base] = qkv[:, a - low : b - low]
            r.gp[row(br), d * bc : (d + 1) * bc] = proj
            r.dact[row(4 * br), d * bc : (d + 1) * bc] = down

    def at_row(w):
        return lambda size: pl.ds(pl.multiple_of(w * size, 8), size)

    aligned = br % 8 == 0
    if aligned:
        assemble(me_w, at_row(me_w))
    for j in range(1, half_w):
        for k in range(n_d):
            across[k][j - 1].wait_recv()
            inside[j][k].start()
        if aligned:
            assemble(same_core[j], at_row(same_core[j]))
    for name in ("bmodel", "bhidden", "bqkv", "binput"):
        loads[name].wait()
    for i in range(6):
        r.bmodel_low[i] = r.bmodel[i].astype(bf16)
    r.bhidden_low[1] = r.bhidden[...].astype(bf16)
    second_hidden = pltpu.make_async_copy(r.bhidden_hbm.at[0], r.bhidden, r.load_sem.at[8])
    second_hidden.start()
    r.bqkv_low[...] = r.bqkv[...].astype(bf16)
    r.binput_low[...] = r.binput[...].astype(bf16)
    for j in range(half_w):
        arrived(inside[j])
        if aligned:
            other = lax.rem(partner + n_w - 2 * j, n_w)
            assemble(other, at_row(other))
    for w in range(n_w):
        if not aligned:
            assemble(w, lambda size: slice(w * size, (w + 1) * size))
        row, lane_at, rows, lanes = sizes.block_places()[0][0]
        for d in range(n_d):
            piece = r.got_all[w, d].astype(f32)
            r.gh[w * bh : (w + 1) * bh, d * bc : (d + 1) * bc] = piece[
                row : row + rows, lane_at : lane_at + lanes
            ]
    even = (
        lax.broadcasted_iota(jnp.int32, (WIDTH // 2, WIDTH), 1)
        == 2 * lax.broadcasted_iota(jnp.int32, (WIDTH // 2, WIDTH), 0)
    ).astype(f32).astype(bf16)
    second_hidden.wait()
    r.bhidden_low[0] = r.bhidden[...].astype(bf16)
    r.wh[...] = tn(even, r.gh[0 : WIDTH // 2].astype(bf16)).astype(bf16)
    r.wqkv[...] = r.gqkv[...].astype(bf16)
    r.wp[...] = r.gp[...].astype(bf16)
    r.wu[...] = r.gu[...].astype(bf16)
    r.wd[...] = r.dact[:, 0:WIDTH].astype(bf16)
    sums = (r.gh, r.gqkv, r.gp, r.gu, r.gdt, r.gvec, r.gub)
    block_start(big_len, small_len, r.vec, sums, r.bias, r.cot, r.ubias)
    loads["bcot"].wait()
    loads["scot"].wait()

    def out_copy(p):
        at = pl.ds(p * PAIR, PAIR)
        return pltpu.make_async_copy(r.bout.at[at], r.bout_hbm.at[at], r.out_sem.at[p])

    @pl.loop(0, sizes.pairs)
    def _(p):
        arrived(forward_links(p))
        block = r.received[p].astype(f32)
        raw = [
            jnp.concatenate([block[w, j * outputs : (j + 1) * outputs] for w in range(n_w)], 0)
            for j in range(PAIR)
        ]
        raw = jnp.concatenate([jnp.transpose(v) for v in raw], 0)
        grad = block_step(
            p * PAIR,
            raw,
            (PAIR, sizes.small_images, big_len, small_len),
            r.bcot,
            r.scot,
            r.vec,
            (r.wh, r.wqkv, r.wp, r.wu, r.wd),
            r.bout,
            r.sout,
            sums,
            (r.probs, r.bias, r.cot, r.ubias),
        )
        sent(forward_links(p))
        for j in range(PAIR):
            turned = jnp.transpose(grad[j * LANES : (j + 1) * LANES])
            for w in range(n_w):
                r.pooled[p, w, j * outputs : (j + 1) * outputs] = turned[
                    w * outputs : (w + 1) * outputs
                ].astype(bf16)
        begin(backward_links(p))
        r.returned[p, me_w] = r.pooled[p, me_w]
        out_copy(p).start()

    small_out = pltpu.make_async_copy(
        r.sout.at[pl.ds(0, sizes.small_images)], r.sout_hbm, r.out_sem.at[sizes.pairs]
    )
    small_out.start()

    u_head = tn(r.binput_low[...], nn(even, r.gh[...].astype(bf16)).astype(bf16))
    u_qkv = [tn(r.bmodel_low[1], r.gqkv[part].astype(bf16)) for part in range(3)]
    u_proj = tn(r.bmodel_low[2], r.gp[...].astype(bf16))
    u_up = tn(r.bmodel_low[4], r.gu[...].astype(bf16))
    u_down = jnp.transpose(nn(r.gdt[...].astype(bf16), r.bhidden_low[1]))
    for copies in (*across, *inside):
        sent(copies)
    r.stage_two[...] = jnp.zeros_like(r.stage_two)
    r.stage_head[...] = jnp.zeros_like(r.stage_head)
    for w in range(n_w):
        at = w * br
        r.stage_two[0:br, 0 : 4 * WIDTH] = u_up[at : at + br]
        for part in range(2):
            r.stage_two[0:br, (4 + part) * WIDTH : (5 + part) * WIDTH] = u_qkv[part][at : at + br]
        r.stage_two[br : 2 * br, 0:WIDTH] = u_qkv[2][at : at + br]
        r.stage_two[br : 2 * br, WIDTH : 2 * WIDTH] = u_proj[at : at + br]
        for j in range(4):
            r.stage_two[br : 2 * br, (2 + j) * WIDTH : (3 + j) * WIDTH] = u_down[
                4 * at + j * br : 4 * at + (j + 1) * br
            ]
        r.stage_head[0:bh] = u_head[w * bh : (w + 1) * bh]
        r.rs_send[w] = r.stage_two[...].astype(bf16)
        r.rsh_send[w] = r.stage_head[...].astype(bf16)
    def pair_copy(source, target, send, recv):
        return pltpu.make_async_remote_copy(
            src_ref=source,
            dst_ref=target,
            send_sem=send,
            recv_sem=recv,
            device_id={"wide": partner},
            device_id_type=MESH,
        )

    buffers = ((r.rs_send, r.pair_got, r.rs_got), (r.rsh_send, r.pairh_got, r.rsh_got))
    targets = [lax.rem(me_w + 2 * j, n_w) for j in range(half_w)]
    pairs = begin(
        [
            pair_copy(
                source.at[lax.rem(partner + 2 * j, n_w)],
                got.at[j],
                r.pair_send.at[which * half_w + j],
                r.pair_recv.at[which * half_w + j],
            )
            for which, (source, got, _) in enumerate(buffers)
            for j in range(half_w)
        ]
    )

    arrived(pairs)
    first = []
    for j in range(1, half_w):
        for which, (source, got, final) in enumerate(buffers):
            source[targets[j]] = (source[targets[j]].astype(f32) + got[j].astype(f32)).astype(bf16)
            at = which * (half_w - 1) + j - 1
            first.append(
                pltpu.make_async_remote_copy(
                    src_ref=source.at[targets[j]],
                    dst_ref=final.at[j],
                    send_sem=r.first_send.at[at],
                    recv_sem=r.first_recv.at[at],
                    device_id={"wide": targets[j]},
                    device_id_type=MESH,
                )
            )
            first[-1].start()

    for p in range(sizes.pairs):
        arrived(backward_links(p))
    for group in range(n_w // per_group):
        parts = [
            r.returned[i // PAIR, group * per_group + s].astype(f32)[
                i % PAIR * outputs : (i % PAIR + 1) * outputs
            ]
            for i in range(images)
            for s in range(per_group)
        ]
        moved = nn(r.perm[...], jnp.concatenate(parts, 0).astype(bf16))
        for s in range(per_group):
            for e in range(2):
                for c in range(channels):
                    at = s * sizes.piece_rows + (e * channels + c) * images
                    to = (c * n_w + group * per_group + s) * images
                    r.sum_big[e, to : to + images] = moved[at : at + images]

    def fold(big, small):
        value = jnp.sum(big.reshape(n_big // 8, 8, LANES), 0)
        return value[:, 0:128] + value[:, 128:256] + jnp.sum(small.reshape(n_small // 8, 8, 128), 0)

    columns_big = jnp.zeros((n_big, 128), f32)
    columns_small = jnp.zeros((n_small, 128), f32)
    put_big, put_small = placements(r.order_big, r.order_small, sizes)
    for c in range(channels):
        own_big, own_small = slice(c * n_big, (c + 1) * n_big), slice(c * n_small, (c + 1) * n_small)
        group = slice(c * 8, (c + 1) * 8)
        pair = []
        for e in range(2):
            block = r.sum_big[e, own_big].astype(bf16)
            pair.append((nn(put_big, block), nn(put_small, block[:, 128:256])))
            r.taps[9, e, group] = fold(
                jnp.where(token_big, pair[e][0], 0.0), jnp.where(token_small, pair[e][1], 0.0)
            )
        columns_big = jnp.where(lane == c, pair[0][0][:, 0:1], columns_big)
        columns_small = jnp.where(lane == c, pair[0][1][:, SPLIT - 128 : SPLIT - 127], columns_small)
        for tap in range(9):
            big, small = r.wins_big[tap, own_big].astype(f32), r.wins_small[tap, own_small].astype(f32)
            for e in range(2):
                r.taps[tap, e, group] = fold(pair[e][0] * big, pair[e][1] * small)
            up, down = (tap_value(tap, c, e) for e in range(2))
            r.wins_big[tap, own_big] = (up * pair[0][0] + down * pair[1][0]).astype(bf16)
            r.wins_small[tap, own_small] = (up * pair[0][1] + down * pair[1][1]).astype(bf16)
    r.heads_big[...] = columns_big
    r.heads_small[...] = columns_small

    r.vpart[...] = jnp.zeros_like(r.vpart)
    half_rows = channels * 8
    own_channel = lax.broadcasted_iota(jnp.int32, (half_rows, WIDTH), 0) // 8
    own_lane = lax.broadcasted_iota(jnp.int32, (half_rows, WIDTH), 1)
    conv = jnp.zeros((128, WIDTH), f32)
    for e in range(2):
        place = (own_lane == 2 * (me_w * channels + own_channel) + e).astype(f32)
        part = jnp.zeros((half_rows, 128), f32)
        for tap in range(10):
            part = jnp.where(lane == tap, jnp.sum(r.taps[tap, e], -1, keepdims=True), part)
        conv += lax.dot_general(
            part,
            place,
            (((0,), (0,)), ((), ())),
            precision=lax.Precision.HIGHEST,
            preferred_element_type=f32,
        )
    r.vpart[0:10] = conv[0:10]
    r.vpart[10:19] = r.gvec[0:9]
    for j in range(4):
        r.vpart[19 + j : 20 + j] = r.gub[:, j * WIDTH : (j + 1) * WIDTH]
    r.v_send[...] = jnp.zeros_like(r.v_send)
    share = sizes.vec_share
    for w in range(n_w):
        r.v_send[w, 0:share] = r.vpart[w * share : (w + 1) * share]
    vec_one = begin(
        links("wide", n_w, me_w, lambda p: r.v_send.at[p], r.v_wide.at[me_w], r.v1_s, r.v1_r)
    )
    r.v_wide[me_w] = r.v_send[me_w]

    arrived(first)
    sums_two = []
    for source, got, final in buffers:
        rows = source[me_w].astype(f32) + got[0].astype(f32)
        for j in range(1, half_w):
            rows += final[j].astype(f32)
        sums_two.append(rows)
    rows_two, rows_head = sums_two
    rows_two = rows_two.astype(bf16)
    t_up = nn(rows_two[0:br, 0 : 4 * WIDTH], r.bhidden_low[0])
    t_qkv = nn(rows_two[0:br, 4 * WIDTH : 6 * WIDTH], r.bqkv_low[0 : 2 * WIDTH]) + nn(
        rows_two[br : 2 * br, 0:WIDTH], r.bqkv_low[2 * WIDTH :]
    )
    t_proj = nn(rows_two[br : 2 * br, WIDTH : 2 * WIDTH], r.bmodel_low[3])
    t_down = [
        nn(rows_two[br : 2 * br, (2 + j) * WIDTH : (3 + j) * WIDTH], r.bmodel_low[5])
        for j in range(4)
    ]
    t_head = nn(rows_head.astype(bf16), r.bmodel_low[0])
    for d in range(n_d):
        own = slice(d * bc, (d + 1) * bc)
        sizes.pack_blocks(
            r.stage_one,
            (
                t_head[0:bh, own],
                t_qkv[:, 3 * d * bc : 3 * (d + 1) * bc],
                t_proj[:, own],
                t_up[:, 4 * d * bc : 4 * (d + 1) * bc],
                jnp.concatenate([t[:, own] for t in t_down], 0),
            ),
        )
        r.t_send[d] = r.stage_one[...].astype(bf16)
    second = begin(
        links("dp", n_d, me_d, lambda p: r.t_send.at[p], r.t_got.at[me_d], r.t_ss, r.t_rs)
    )
    r.t_got[me_d] = r.t_send[me_d]
    arrived(vec_one)
    vsum = r.v_wide[0]
    for w in range(1, n_w):
        vsum += r.v_wide[w]
    r.v_dp[me_d] = vsum
    vec_two = begin(links("dp", n_d, me_d, lambda p: r.v_dp.at[me_d], r.v_dp.at[me_d], r.v2_s, r.v2_r))

    def act_part(chunk):
        at = pl.ds(chunk * 256, 256)
        table = r.table[...].reshape(9 * LANES, r.table.shape[2])
        mixed = jnp.concatenate([r.wins_big[tap, at, :] for tap in range(9)], 1)
        r.dact[at, :] = nn(mixed, table)
        copy = pltpu.make_async_copy(
            r.dact.at[at], r.dact_hbm.at[at], r.out_sem.at[sizes.pairs + 2 + chunk]
        )
        copy.start()
        return copy

    chunks = list(range(sizes.rows // 256))
    act_out = [act_part(chunk) for chunk in chunks[:1]]
    arrived(second)
    turned = r.t_got[0].astype(f32)
    for d in range(1, n_d):
        turned += r.t_got[d].astype(f32)
    r.full_got[me_d] = turned.astype(bf16)
    third = begin(
        links("dp", n_d, me_d, lambda p: r.full_got.at[me_d], r.full_got.at[me_d], r.d_s, r.d_r)
    )
    def total(value):
        return jnp.sum(jnp.sum(value * value, 0, keepdims=True), -1, keepdims=True)

    square = total(turned)
    arrived(vec_two)
    vsum = r.v_dp[0]
    for d in range(1, n_d):
        vsum += r.v_dp[d]
    last_row = lax.broadcasted_iota(jnp.int32, (8, WIDTH), 0) == 7
    r.s_wide[me_w] = jnp.where(last_row, square, vsum)
    fourth = begin(
        links("wide", n_w, me_w, lambda p: r.s_wide.at[me_w], r.s_wide.at[me_w], r.s_s, r.s_r)
    )
    act_out += [act_part(chunk) for chunk in chunks[1:2]]
    count = jnp.full((8, 128), r.step[0], jnp.int32).astype(f32)[0:1, 0:1]
    fix_one = 1.0 - jnp.exp(count * float(np.log(beta_one)))
    fix_two = 1.0 - jnp.exp(count * float(np.log(beta_two)))
    inverse_one, inverse_two = 1.0 / fix_one, 1.0 / fix_two
    arrived(fourth)
    square = r.s_wide[0][7:8, 0:1]
    for w in range(1, n_w):
        square += r.s_wide[w][7:8, 0:1]
    r.s_dp[me_d] = jnp.broadcast_to(square, (8, 128))
    fifth = begin(links("dp", n_d, me_d, lambda p: r.s_dp.at[me_d], r.s_dp.at[me_d], r.s2_s, r.s2_r))
    vec_squares = jnp.zeros((8, WIDTH), f32)
    for w in range(n_w):
        part = jnp.where(last_row, 0.0, r.s_wide[w])
        vec_squares += part * part
        r.vtotal[w * share : (w + 1) * share] = part[0:share]
    vec_square = jnp.sum(jnp.sum(vec_squares, 0, keepdims=True), -1, keepdims=True)
    act_out += [act_part(chunk) for chunk in chunks[2:]]
    mixed = jnp.concatenate([r.wins_small[tap] for tap in range(9)], 1)
    r.dsmall[...] = nn(mixed, r.table_small[...].reshape(9 * 128, r.table_small.shape[2]))
    act_out.append(pltpu.make_async_copy(r.dsmall, r.dsmall_hbm, r.out_sem.at[sizes.pairs + 1]))
    act_out[-1].start()
    arrived(moments)
    arrived(third)
    arrived(fifth)
    square = vec_square
    for d in range(n_d):
        square += r.s_dp[d][0:1, 0:1]
    norm = jnp.sqrt(square)
    factor = jnp.minimum(1.0, clip_limit / (norm + 1e-06))
    which = lax.broadcasted_iota(jnp.int32, (8, 128), 1)
    r.scalars[...] = jnp.where(
        which == 0,
        norm,
        jnp.where(which == 1, factor, jnp.where(which == 2, fix_one, fix_two)),
    )

    def adam(gradient, old):
        scaled = gradient * factor
        moment = beta_one * old[0] + (1.0 - beta_one) * scaled
        second_moment = beta_two * old[1] * old[1] + (1.0 - beta_two) * scaled * scaled
        return moment, second_moment

    for d in range(n_d):
        moment, second_moment = adam(r.full_got[d].astype(f32), r.mpack[d])
        direction = moment * inverse_one / (jnp.sqrt(second_moment * inverse_two) + adam_eps)
        head, qkv, proj, up, down = sizes.unpack_blocks(direction)
        r.row_head[0:bh, d * bc : (d + 1) * bc] = head
        r.row_qkv[:, 3 * d * bc : 3 * (d + 1) * bc] = qkv
        r.row_proj[:, d * bc : (d + 1) * bc] = proj
        r.row_up[:, 4 * d * bc : 4 * (d + 1) * bc] = up
        r.row_down[:, d * bc : (d + 1) * bc] = down

    def right_rows(ref, size, unit=8):
        return ref[pl.ds(pl.multiple_of(me_d * size, unit), size), :].astype(bf16)

    sizes.pack_blocks(
        r.stage_one,
        (
            nt(r.row_head[...].astype(bf16), right_rows(r.bmodel.at[0], bc))[0:bh],
            nt(r.row_qkv[...].astype(bf16), right_rows(r.bqkv, 3 * bc)),
            nt(r.row_proj[...].astype(bf16), right_rows(r.bmodel.at[3], bc)),
            nt(r.row_up[...].astype(bf16), right_rows(r.bhidden_low.at[0], 4 * bc, 16)),
            nt(r.row_down[...].astype(bf16), right_rows(r.bmodel.at[5], bc)),
        ),
    )
    r.y_got[me_w] = r.stage_one[...].astype(bf16)
    y_across = begin(
        [
            pltpu.make_async_remote_copy(
                src_ref=r.y_got.at[me_w],
                dst_ref=r.y_got.at[me_w],
                send_sem=r.ya_send.at[j - 1],
                recv_sem=r.ya_recv.at[j - 1],
                device_id={"wide": targets[j]},
                device_id_type=MESH,
            )
            for j in range(1, half_w)
        ]
    )
    y_inside = [
        pair_copy(
            r.y_got.at[same_core[j]], r.y_got.at[same_core[j]], r.yi_send.at[j], r.yi_recv.at[j]
        )
        for j in range(half_w)
    ]
    y_inside[0].start()
    moment, second_moment = adam(turned, r.mpack[me_d])
    r.states[0] = moment
    r.states[1] = jnp.sqrt(second_moment)

    def left_rows(ref, size, unit=8):
        if size % unit == 0:
            return ref[pl.ds(pl.multiple_of(me_w * size, unit), size), :].astype(bf16)
        own = lax.broadcasted_iota(jnp.int32, (size, ref.shape[0]), 0) + me_w * size
        pick = own == lax.broadcasted_iota(jnp.int32, (size, ref.shape[0]), 1)
        return nn(pick.astype(f32).astype(bf16), ref[...].astype(bf16)).astype(bf16)

    lefts = (
        left_rows(r.binput, bh),
        left_rows(r.bmodel.at[1], br),
        left_rows(r.bmodel.at[2], br),
        left_rows(r.bmodel.at[4], br),
        left_rows(r.bhidden_low.at[1], 4 * br, 16),
    )
    r.update[...] = jnp.zeros_like(r.update)
    for j in range(1, half_w):
        y_across[j - 1].wait_recv()
        y_inside[j].start()
    arrived(y_inside)
    parts = [sizes.unpack_blocks(r.y_got[w].astype(f32)) for w in range(n_w)]
    sizes.pack_blocks(
        r.update,
        [
            nn(lefts[m], jnp.concatenate([part[m] for part in parts], 0).astype(bf16))
            for m in range(5)
        ],
    )
    for p in range(sizes.pairs):
        sent(backward_links(p))
        out_copy(p).wait()
    small_out.wait()
    for copy in act_out:
        copy.wait()
    for copies in (
        one,
        moments,
        pairs,
        first,
        vec_one,
        second,
        vec_two,
        third,
        fourth,
        fifth,
        y_across,
        y_inside,
    ):
        sent(copies)


def finish_kernel(
    sizes,
    mh,
    mqkv,
    mp,
    mu,
    md,
    vec,
    vmom,
    heads_big,
    heads_small,
    update,
    states,
    vtotal,
    scalars,
    big_from,
    small_from,
    act_from,
    act_small_from,
    big_to,
    small_to,
    act_to,
    act_small_to,
    dcls_big,
    dcls_small,
    norm,
    nvec,
    nvmom,
    *outs,
):
    outs, (hold_big, hold_small, hold_act, hold_act_small, sem) = outs[:-5], outs[-5:]
    moves = []
    for source, hold, target, parts in (
        (act_from, hold_act, act_to, 2),
        (big_from, hold_big, big_to, 2),
        (act_small_from, hold_act_small, act_small_to, 1),
        (small_from, hold_small, small_to, 1),
    ):
        size = source.shape[0] // parts
        for part in range(parts):
            at = pl.ds(part * size, size)
            pair = [(source.at[at], hold.at[at]), (hold.at[at], target.at[at])]
            moves.append(
                [
                    pltpu.make_async_copy(src, dst, sem.at[which, len(moves)])
                    for which, (src, dst) in enumerate(pair)
                ]
            )
    for move in moves:
        move[0].start()
    norm[0] = scalars[0, 0]
    factor, fix_one, fix_two = (scalars[0, j] for j in (1, 2, 3))
    for move in moves:
        move[0].wait()
        move[1].start()
    dcls_big[...] = jnp.transpose(heads_big[...])[0 : sizes.channels]
    dcls_small[...] = jnp.transpose(heads_small[...])[0 : sizes.channels]
    updates = sizes.unpack_blocks(update[...])
    firsts = sizes.unpack_blocks(states[0])
    seconds = sizes.unpack_blocks(states[1])
    for member, master in enumerate((mh, mqkv, mp, mu, md)):
        change, first, second = updates[member], firsts[member], seconds[member]
        if member == 4:
            change, first, second = (jnp.transpose(v) for v in (change, first, second))
        fresh = master[...] - rate_matrix * change
        outs[member][...] = fresh
        if member == 0:
            outs[5][:, 0, :] = first
            outs[5][:, 1, :] = second
        else:
            outs[5 + member][0] = first
            outs[5 + member][1] = second
        outs[10 + member][...] = fresh.astype(jnp.bfloat16)
    scaled = vtotal[0:23] * factor
    first = beta_one * vmom[:, 0, :] + (1.0 - beta_one) * scaled
    second = beta_two * vmom[:, 1, :] * vmom[:, 1, :] + (1.0 - beta_two) * scaled * scaled
    direction = first / fix_one / (jnp.sqrt(second / fix_two) + adam_eps)
    nvec[...] = vec[...] * (1.0 - rate_vector * decay_rate) - rate_vector * direction
    nvmom[:, 0, :] = first
    nvmom[:, 1, :] = jnp.sqrt(second)

    for move in moves:
        move[1].wait()


def run_main(sizes, lens, ins, hbm):
    bf16, f32 = jnp.bfloat16, jnp.float32
    w, d = sizes.wide, sizes.dp
    images, pairs = sizes.images, sizes.pairs
    act, table, bcot, scot, binput, bmodel, bqkv, bhidden = hbm
    table_small = ins[9]
    small_cells = table_small.shape[2]
    hidden = 4 * WIDTH
    vec_rows = w * sizes.vec_share
    pack = (sizes.pair_rows, sizes.block_lanes)
    two = (sizes.pair_rows, 6 * WIDTH)
    head = (sizes.head_rows, WIDTH)
    swap = (pairs, w, PAIR * sizes.outputs, LANES)
    big, small = sizes.rows, sizes.small_rows
    outs = [
        (bcot.shape, f32),
        (scot.shape, f32),
        ((big, act.shape[2]), f32),
        ((small, small_cells), f32),
        ((sizes.slots, 128), f32),
        ((sizes.small_slots, 128), f32),
        (pack, f32),
        ((2,) + pack, f32),
        ((vec_rows, WIDTH), f32),
        ((8, 128), f32),
    ]
    scratch = dict(
        act=(act.shape, bf16),
        table=(table.shape, bf16),
        bcot=(bcot.shape, bf16),
        scot=(scot.shape, bf16),
        binput=(binput.shape, f32),
        bmodel=(bmodel.shape, f32),
        bqkv=(bqkv.shape, f32),
        bhidden=(bhidden.shape[1:], f32),
        binput_low=(binput.shape, bf16),
        bmodel_low=(bmodel.shape, bf16),
        bqkv_low=(bqkv.shape, bf16),
        bhidden_low=(bhidden.shape, bf16),
        stage_one=(pack, f32),
        stage_two=(two, f32),
        stage_head=(head, f32),
        got_all=((w, d) + pack, bf16),
        rs_send=((w,) + two, bf16),
        rsh_send=((w,) + head, bf16),
        mpack=((d, 2) + pack, f32),
        wins_big=((9, big, LANES), bf16),
        wins_small=((9, small, 128), bf16),
        sum_big=((2, big, LANES), f32),
        sum_small=((2, small, 128), f32),
        swap=((w, sizes.piece_rows, LANES), bf16),
        pooled=(swap, bf16),
        received=(swap, bf16),
        returned=(swap, bf16),
        wh=((WIDTH, WIDTH), bf16),
        wqkv=((3, WIDTH, WIDTH), bf16),
        wp=((WIDTH, WIDTH), bf16),
        wu=((WIDTH, hidden), bf16),
        wd=((hidden, WIDTH), bf16),
        gh=((WIDTH, WIDTH), f32),
        gqkv=((3, WIDTH, WIDTH), f32),
        gp=((WIDTH, WIDTH), f32),
        gu=((WIDTH, hidden), f32),
        gdt=((WIDTH, hidden), f32),
        gvec=((16, WIDTH), f32),
        gub=((1, hidden), f32),
        probs=((PAIR, HEADS, LANES, LANES), f32),
        bias=((LANES, LANES), f32),
        cot=((PAIR * LANES, WIDTH), bf16),
        ubias=((1, hidden), f32),
        bout=(bcot.shape, f32),
        sout=((images,) + scot.shape[1:], f32),
        rs_got=((w // 2,) + two, bf16),
        pair_got=((w // 2,) + two, bf16),
        pairh_got=((w // 2,) + head, bf16),
        rsh_got=((w // 2,) + head, bf16),
        taps=((10, 2, sizes.channels * 8, 128), f32),
        dact=((big, act.shape[2]), f32),
        dsmall=((small, small_cells), f32),
        vpart=((vec_rows, WIDTH), f32),
        v_send=((w, 8, WIDTH), f32),
        v_wide=((w, 8, WIDTH), f32),
        v_dp=((d, 8, WIDTH), f32),
        t_send=((d,) + pack, bf16),
        t_got=((d,) + pack, bf16),
        full_got=((d,) + pack, bf16),
        s_wide=((w, 8, WIDTH), f32),
        s_dp=((d, 8, 128), f32),
        row_head=((sizes.bh, WIDTH), f32),
        row_qkv=((sizes.br, 3 * WIDTH), f32),
        row_proj=((sizes.br, WIDTH), f32),
        row_up=((sizes.br, hidden), f32),
        row_down=((4 * sizes.br, WIDTH), f32),
        y_got=((w,) + pack, bf16),
    )
    sems = dict(
        load_sem=9,
        out_sem=pairs + 2 + big // 256,
        one_send=d - 1,
        one_recv=d - 1,
        across_send=(w // 2 - 1) * d,
        across_recv=(w // 2 - 1) * d,
        inside_send=w // 2 * d,
        inside_recv=w // 2 * d,
        act_send=pairs * (w - 1),
        act_recv=pairs * (w - 1),
        back_send=pairs * (w - 1),
        back_recv=pairs * (w - 1),
        mom_send=d - 1,
        pair_send=w,
        pair_recv=w,
        first_send=w - 2,
        first_recv=w - 2,
        ya_send=w // 2 - 1,
        ya_recv=w // 2 - 1,
        yi_send=w // 2,
        yi_recv=w // 2,
        mom_recv=d - 1,
    )
    for name in ("v1_s", "v1_r", "s_s", "s_r"):
        sems[name] = w - 1
    for name in ("t_ss", "t_rs", "v2_s", "v2_r", "d_s", "d_r", "s2_s", "s2_r"):
        sems[name] = d - 1
    return pl.pallas_call(
        partial(main_kernel, sizes, lens, list(scratch) + list(sems)),
        in_specs=[VM] * 5 + [SM, VM, SM] + [VM] * 12 + [HB] * 8,
        out_specs=[HB] * 4 + [VM] * 6,
        out_shape=[jax.ShapeDtypeStruct(s, t) for s, t in outs],
        scratch_shapes=[pltpu.VMEM(s, t) for s, t in scratch.values()] + dma_sems(*sems.values()),
        compiler_params=pltpu.CompilerParams(
            collective_id=0, has_side_effects=True, vmem_limit_bytes=LIMIT
        ),
        name="main",
    )(*ins, *hbm)


def run_finish(sizes, masters, vec, vmom, moments, heads, packs, large):
    f32, bf16 = jnp.float32, jnp.bfloat16
    shapes = [m.shape for m in masters]
    outs = [(a.shape, f32) for a in large]
    outs += [((sizes.channels, h.shape[0]), f32) for h in heads]
    outs += [((1,), f32), (vec.shape, f32), (vmom.shape, f32)]
    outs += [(s, f32) for s in shapes] + [(m.shape, f32) for m in moments]
    outs += [(s, bf16) for s in shapes]
    return pl.pallas_call(
        partial(finish_kernel, sizes),
        in_specs=[VM] * 12 + [SM] + [HB] * 4,
        out_specs=[HB] * 4 + [VM, VM, SM] + [VM] * (len(outs) - 7),
        out_shape=[jax.ShapeDtypeStruct(s, t) for s, t in outs],
        scratch_shapes=[pltpu.VMEM(large[i].shape, f32) for i in range(4)]
        + [pltpu.SemaphoreType.DMA((2, 10))],
        compiler_params=pltpu.CompilerParams(vmem_limit_bytes=LIMIT),
        name="finish",
    )(*masters, vec, vmom, *heads, *packs, *large)


def pool_table(grid, side, lane, lanes):
    table = np.zeros((9, lanes, grid * grid), np.float32)
    for tap in range(9):
        for y in range(side):
            for x in range(side):
                sy, sx = 2 * y + tap // 3 - 1, 2 * x + tap % 3 - 1
                if 0 <= sy < grid and 0 <= sx < grid:
                    table[tap, lane + y * side + x, sy * grid + sx] = 1.0
    return jnp.asarray(table, jnp.bfloat16)


def per_device(
    wide_n,
    dp_n,
    big_act,
    big_cls,
    small_act,
    small_cls,
    big_order,
    small_order,
    big_cot,
    small_cot,
    vec_params,
    vec_moments,
    *rest,
):
    masters, moments, bases, step = list(rest[0:5]), list(rest[5:10]), rest[10:14], rest[14]
    channels = big_act.shape[1]
    images, small_images = big_cot.shape[0], small_cot.shape[0]
    lens = (big_cot.shape[1], small_cot.shape[1])
    sizes = Sizes(wide_n, dp_n, channels, images, small_images)
    side = lambda cells: round(cells**0.5)
    tables = (
        pool_table(side(big_act.shape[2]), side(lens[0] - 1), 1, LANES),
        pool_table(side(small_act.shape[2]), side(lens[1] - 1), SPLIT + 1 - 128, 128),
    )
    perm = row_permutation(channels, images)
    flip = lambda a, i, j: jnp.swapaxes(a, i, j)
    acts = [flip(a, 0, 1) for a in (big_act, small_act, big_cls, small_cls)]
    orders = (big_order, small_order)
    masters[4] = flip(masters[4], 0, 1)
    moments[0], moments[4] = flip(moments[0], 0, 1), flip(moments[4], 1, 2)
    vec_moments = flip(vec_moments, 0, 1)

    ins = (*acts[1:], *orders, vec_params, vec_params, step, perm, tables[1], *masters, *moments)
    hbm = (acts[0], tables[0], flip(big_cot, 1, 2), small_cot, *bases)
    *large, heads_big, heads_small, update, states, vtotal, scalars = run_main(
        sizes, lens, ins, hbm
    )
    packs = (update, states, vtotal, scalars)
    results = list(
        run_finish(
            sizes, masters, vec_params, vec_moments, moments, (heads_big, heads_small), packs, large
        )
    )
    big_out, small_out, dact_big, dact_small = results[0:4]
    results = results[4:]
    cls_big, cls_small, norm, new_vec, new_vec_moments = results[0:5]
    masters, moments, copies = results[5:10], results[10:15], results[15:20]
    masters[4], copies[4] = flip(masters[4], 0, 1), flip(copies[4], 0, 1)
    moments[0], moments[4] = flip(moments[0], 0, 1), flip(moments[4], 1, 2)
    return (
        flip(big_out, 1, 2),
        small_out,
        flip(dact_big.reshape(channels, sizes.slots, -1), 0, 1),
        flip(cls_big, 0, 1),
        flip(dact_small.reshape(channels, sizes.small_slots, -1), 0, 1),
        flip(cls_small, 0, 1),
        norm,
        new_vec,
        flip(new_vec_moments, 0, 1),
        *masters,
        *moments,
        *copies,
    )


def solution(mesh):
    split, wide_first, free = P("dp", "wide", None), P("wide", "dp"), P()
    moment = P(None, "wide", "dp")
    both = P(("dp", "wide"), None, None)
    acts = (split, P("dp", "wide"), split, P("dp", "wide"))
    in_specs = (
        acts
        + (P("dp", None), P("dp", None), both, both, free, free)
        + (wide_first,) * 5
        + (moment,) * 5
        + (free,) * 5
    )
    out_specs = (
        (both, both) + acts + (free,) * 3 + (wide_first,) * 5 + (moment,) * 5 + (wide_first,) * 5
    )
    return jax.shard_map(
        partial(per_device, mesh.shape["wide"], mesh.shape["dp"]),
        mesh=mesh,
        in_specs=in_specs,
        out_specs=out_specs,
        check_vma=False,
    )
```
